32 devices in a mesh: dp: 8 (over y, x, core), tensor: 4 (over z).
Axes of the slice: x: 2, y: 2, z: 4, core: 2. Of those that a mesh axis runs over, the one named last changes fastest.
Arguments:
- tokens: bfloat16 [16384, 512], P('dp'), may hold values from -50 to 50
- lengths: int32 [8, 64], P('dp'), may hold values from 0 to 1000, as said below
- cotangent: bfloat16 [16384, 512], P('dp'), may hold values from -6 to 6
- qkv_weight: bfloat16 [512, 3, 512], P(None, None, 'tensor'), may hold values from -0.25 to 0.25
- qv_bias: float32 [2, 512], P(None, 'tensor'), may hold values from -3 to 3
- out_weight: bfloat16 [512, 512], P('tensor'), may hold values from -2 to 2
- out_bias: float32 [512], replicated, may hold values from -2 to 2
- up_weight: bfloat16 [512, 2048], P(None, 'tensor'), may hold values from -0.25 to 0.25
- up_bias: float32 [2048], P('tensor'), may hold values from -3 to 3
- down_weight: bfloat16 [2048, 512], P('tensor'), may hold values from -0.125 to 0.125
- down_bias: float32 [512], replicated, may hold values from -2 to 2
- first_gain: float32 [512], replicated, may hold values from 0.1 to 1.9
- first_shift: float32 [512], replicated, may hold values from -2 to 2
- second_gain: float32 [512], replicated, may hold values from 0.1 to 1.9
- second_shift: float32 [512], replicated, may hold values from -2 to 2
Outputs:
- layer_output: bfloat16 [16384, 512], P('dp')
- grad_tokens: bfloat16 [16384, 512], P('dp')
- grad_qkv_weight: float32 [512, 3, 512], P(None, None, 'tensor')
- grad_qv_bias: float32 [2, 512], P(None, 'tensor')
- grad_out_weight: float32 [512, 512], P('tensor')
- grad_out_bias: float32 [512], replicated
- grad_up_weight: float32 [512, 2048], P(None, 'tensor')
- grad_up_bias: float32 [2048], P('tensor')
- grad_down_weight: float32 [2048, 512], P('tensor')
- grad_down_bias: float32 [512], replicated
- grad_first_gain: float32 [512], replicated
- grad_first_shift: float32 [512], replicated
- grad_second_gain: float32 [512], replicated
- grad_second_shift: float32 [512], replicated
The draws below stay inside these ranges and needn't reach their ends.
Inputs may be any that keep to these rules, and one draw needn't show every extreme that they name: Row b lists the lengths of the chains laid end to end from slot 0 in the 2048 slots of pack b, so a row sums to at most 2048; later entries may be 0; the slots after the last chain are padding. Some pack has no padding and a chain of exactly 1000.
All inputs are finite; a program needn't handle non-finite values.
Results may differ from the reference program's by a relative error of at most 0.019.
Values may be sent and summed in bfloat16 or wider, within the bound.
No kernel may reach another device: no remote copies, remote signals or barrier semaphores. Data moves between devices by JAX's collectives and lax.ppermute only.
A program may use at most 128 MiB of HBM per device.

```python
import math
import jax
import jax.numpy as jnp
from jax import lax

D = 512
HEADS = 8
HEAD_DIM = 64
FF = 2048
TOK_DEV = 2048
LONGEST = 1000
CHAINS = 64
PACKS = 8
TOKENS = 16384
N_TENSOR = 4


def draw_lengths(key, part):
    key = jax.random.fold_in(key, 11)
    subkeys = jax.random.split(key, 5)
    shorter = jax.random.randint(subkeys[0], (PACKS, CHAINS), max(LONGEST // 20, 1), LONGEST // 5 + 1)
    longer = jax.random.randint(subkeys[1], (PACKS,), LONGEST // 2, LONGEST + 1)
    where_long = jax.random.randint(subkeys[2], (PACKS,), 0, CHAINS)
    columns = jnp.arange(CHAINS)
    pack_rows = jnp.arange(PACKS)
    drawn = jnp.where(columns[None, :] == where_long[:, None], longer[:, None], shorter)
    filled = jax.random.randint(subkeys[3], (PACKS,), TOK_DEV // 2, TOK_DEV + 1)
    chosen = jax.random.randint(subkeys[4], (), 0, PACKS)
    drawn = jnp.where((pack_rows[:, None] == chosen) & (columns[None, :] == 0), LONGEST, drawn)
    filled = jnp.where(pack_rows == chosen, TOK_DEV, filled)
    endings = jnp.minimum(jnp.cumsum(drawn, axis=1), filled[:, None])
    before = jnp.concatenate([jnp.zeros((PACKS, 1), jnp.int32), endings[:, :-1].astype(jnp.int32)], axis=1)
    return (endings - before).astype(jnp.int32)


def draw_tokens(key, part):
    key = jax.random.fold_in(key, 5)
    subkeys = jax.random.split(key, 3)
    row_scale = jnp.exp(jax.random.uniform(subkeys[0], (TOKENS, 1), minval=math.log(0.3), maxval=math.log(3.0)))
    column_scale = jnp.exp(jax.random.uniform(subkeys[1], (1, D), minval=math.log(0.3), maxval=math.log(3.0)))
    entries = jnp.clip(jax.random.normal(subkeys[2], (TOKENS, D)), -5.0, 5.0)
    return (entries * row_scale * column_scale).astype(jnp.float32).astype(jnp.bfloat16)


def block_levels(key, extent, cuts, smallest, largest):
    def one(dim, blocks):
        draws = jax.random.uniform(jax.random.fold_in(jax.random.fold_in(key, 6), dim), (blocks,), jnp.float32, smallest / len(cuts), largest / len(cuts))
        return jnp.repeat(jnp.exp(draws), extent[dim] // blocks).reshape((-1,) + (1,) * (len(extent) - dim - 1))

    factor_of = one(*cuts[0])
    for cut in cuts[1:]:
        factor_of = factor_of * one(*cut)
    return factor_of


def gaussian(rng, extent, scale, most, shards=(), held_as=jnp.bfloat16):
    values = scale * jax.random.normal(rng, extent, jnp.float32)
    if shards:
        values = values * block_levels(rng, extent, shards, -0.22, 0.18)
    return jnp.clip(values, -most, most).astype(held_as)


def setup_inputs(seed: int = 0) -> dict:
    streams_of = jax.random.split(jax.random.key(seed), 16)
    tokens = draw_tokens(jax.random.fold_in(streams_of[15], 71), 0)
    lengths = draw_lengths(jax.random.fold_in(streams_of[15], 71), 0)
    cotangent = gaussian(streams_of[2], (TOKENS, D), 1.0, 6.0, ((0, 8),))
    qkv_weight = gaussian(streams_of[3], (D, 3, HEADS * HEAD_DIM), D ** -0.5, 0.25, ((2, 4),))
    qv_bias = gaussian(streams_of[4], (2, HEADS * HEAD_DIM), 0.5, 3.0, ((1, 4),), jnp.float32)
    out_weight = gaussian(streams_of[5], (HEADS * HEAD_DIM, D), (max(HEADS * HEAD_DIM // 64, 1)) ** -0.5, 2.0, ((0, 4),))
    out_bias = gaussian(streams_of[6], (D,), 0.3, 2.0, (), jnp.float32)
    up_weight = gaussian(streams_of[7], (D, FF), D ** -0.5, 0.25, ((1, 4),))
    up_bias = gaussian(streams_of[8], (FF,), 0.5, 3.0, ((0, 4),), jnp.float32)
    down_weight = gaussian(streams_of[9], (FF, D), FF ** -0.5, 0.125, ((0, 4),))
    down_bias = gaussian(streams_of[10], (D,), 0.3, 2.0, (), jnp.float32)
    first_gain = jnp.clip(1.0 + 0.18 * jax.random.normal(streams_of[11], (D,), jnp.float32), 0.1, 1.9)
    first_shift = gaussian(streams_of[12], (D,), 0.3, 2.0, (), jnp.float32)
    second_gain = jnp.clip(1.0 + 0.18 * jax.random.normal(streams_of[13], (D,), jnp.float32), 0.1, 1.9)
    second_shift = gaussian(streams_of[14], (D,), 0.3, 2.0, (), jnp.float32)
    return dict(tokens=tokens, lengths=lengths, cotangent=cotangent, qkv_weight=qkv_weight, qv_bias=qv_bias, out_weight=out_weight, out_bias=out_bias, up_weight=up_weight, up_bias=up_bias, down_weight=down_weight, down_bias=down_bias, first_gain=first_gain, first_shift=first_shift, second_gain=second_gain, second_shift=second_shift)


precise = lax.Precision.HIGHEST

@jax.custom_vjp
def low(v):
    return lax.optimization_barrier(v.astype(jnp.bfloat16)).astype(jnp.float32)

@jax.custom_vjp
def low_back(v):
    return v

def low_keep(v):
    return (low(v), None)

def low_pass(kept, grad):
    return (grad,)

def back_keep(v):
    return (v, None)

def back_low(kept, grad):
    return (low(grad),)
low.defvjp(low_keep, low_pass)
low_back.defvjp(back_keep, back_low)

def layer_norm(values, scaling, offset):
    centered = values - lax.optimization_barrier(jnp.mean(values, axis=-1, keepdims=True))
    spread = lax.optimization_barrier(jnp.mean(centered * centered, axis=-1, keepdims=True))
    return centered * lax.rsqrt(spread + 1e-05) * scaling + offset

def packing(chain_lengths):
    endings = jnp.cumsum(chain_lengths).astype(jnp.int32)
    slot_index = jnp.arange(TOK_DEV, dtype=jnp.int32)
    segment = lax.optimization_barrier(jnp.sum((endings[None, :] <= slot_index[:, None]).astype(jnp.int32), axis=1))
    return (segment, slot_index < endings[-1])

def forward(source, qkv_weight, qv_bias, out_weight, out_bias, up_weight, up_bias, down_weight, down_bias, first_gain, first_shift, second_gain, second_shift, segment, live_slot):
    row_count = source.shape[0]
    hidden = HEADS * HEAD_DIM
    group_cols = hidden // N_TENSOR
    group_ffn = FF // N_TENSOR
    normed = low(layer_norm(source, first_gain, first_shift))
    joined = jnp.dot(normed, qkv_weight.reshape(D, 3 * hidden), precision=precise).reshape(row_count, 3, hidden)
    queries = low(low_back(joined[:, 0] + qv_bias[0])).reshape(row_count, HEADS, HEAD_DIM)
    keyed = low(low_back(joined[:, 1])).reshape(row_count, HEADS, HEAD_DIM)
    values = low(low_back(joined[:, 2] + qv_bias[1])).reshape(row_count, HEADS, HEAD_DIM)
    scores = low_back(jnp.einsum('qhd,khd->hqk', queries, keyed, precision=precise) * HEAD_DIM ** (-0.5))
    same_chain = segment[:, None] == segment[None, :]
    scores = jnp.where(same_chain[None], scores, -1e+30)
    shifted = jnp.exp(scores - lax.optimization_barrier(jnp.max(scores, axis=-1, keepdims=True)))
    attention = shifted / lax.optimization_barrier(jnp.sum(shifted, axis=-1, keepdims=True))
    attended = jnp.einsum('hqk,khd->qhd', low(attention), values, precision=precise).reshape(row_count, hidden)
    attended = low(low_back(attended))
    pieces = jnp.einsum('tgc,gcd->gtd', attended.reshape(row_count, N_TENSOR, group_cols), out_weight.reshape(N_TENSOR, group_cols, D), precision=precise)
    middle = source + low_back(lax.optimization_barrier(jnp.sum(low(pieces), axis=0))) + out_bias
    normed_two = low(layer_norm(middle, second_gain, second_shift))
    upward = low_back(jnp.dot(normed_two, up_weight, precision=precise) + up_bias)
    active = low(jax.nn.gelu(upward, approximate=False))
    pieces_two = jnp.einsum('tgc,gcd->gtd', active.reshape(row_count, N_TENSOR, group_ffn), down_weight.reshape(N_TENSOR, group_ffn, D), precision=precise)
    result = middle + low_back(lax.optimization_barrier(jnp.sum(low(pieces_two), axis=0))) + down_bias
    return jnp.where(live_slot[:, None], result, source)

def reference(tokens, lengths, cotangent, qkv_weight, qv_bias, out_weight, out_bias, up_weight, up_bias, down_weight, down_bias, first_gain, first_shift, second_gain, second_shift):
    params = (qkv_weight.astype(jnp.float32), qv_bias.astype(jnp.float32), out_weight.astype(jnp.float32), out_bias.astype(jnp.float32), up_weight.astype(jnp.float32), up_bias.astype(jnp.float32), down_weight.astype(jnp.float32), down_bias.astype(jnp.float32), first_gain.astype(jnp.float32), first_shift.astype(jnp.float32), second_gain.astype(jnp.float32), second_shift.astype(jnp.float32))
    sources = tokens.astype(jnp.float32).reshape(PACKS, TOK_DEV, D)
    cotangents = cotangent.astype(jnp.float32).reshape(PACKS, TOK_DEV, D)

    def one_pack(totals, packed):
        source, upstream, chain_lengths = packed
        segment, live_slot = packing(chain_lengths)

        def pack_layer(inputs, *weights):
            return forward(inputs, *weights, segment, live_slot)
        result, pullback = jax.vjp(pack_layer, source, *params)
        gradients = pullback(upstream)
        updated = tuple((running + gradient for running, gradient in zip(totals, gradients[1:])))
        return (updated, (result.astype(jnp.bfloat16), gradients[0].astype(jnp.bfloat16)))
    initial = tuple((jnp.zeros(weight.shape, jnp.float32) for weight in params))
    totals, (outputs, input_grads) = lax.scan(one_pack, initial, (sources, cotangents, lengths))
    averaged = tuple((running / PACKS for running in totals))
    return (outputs.reshape(TOKENS, D), input_grads.reshape(TOKENS, D), averaged[0], averaged[1], averaged[2], averaged[3], averaged[4], averaged[5], averaged[6], averaged[7], averaged[8], averaged[9], averaged[10], averaged[11])
```

```python
import functools
import math

import jax
import jax.numpy as jnp
from jax import lax
from jax.experimental import pallas as pl
from jax.experimental.pallas import tpu as pltpu
from jax.sharding import PartitionSpec as P

HEAD_DIM = 64
BLOCK = 256
CODES = 128
LOG2E = math.log2(math.e)
SCALE = LOG2E * HEAD_DIM**-0.5
VMEM = 60 << 20
BF16 = jnp.bfloat16
F32 = jnp.float32


def dot(a, b, ca=1, cb=0):
    return lax.dot_general(a, b, (((ca,), (cb,)), ((), ())), preferred_element_type=F32)


def whole(*shape):
    return pl.BlockSpec(shape, lambda *_: (0,) * len(shape))


def rows(n, width):
    return pl.BlockSpec((n, width), lambda i: (i, 0))


def cols(height, n):
    return pl.BlockSpec((height, n), lambda i: (0, i))


SMEM = pl.BlockSpec(memory_space=pltpu.SMEM)


def normalise(v):
    centred = v - jnp.mean(v, axis=-1, keepdims=True)
    r = lax.rsqrt(jnp.mean(centred * centred, axis=-1, keepdims=True) + 1e-05)
    return centred * r, r


def chain_ranges(len_s, meta, blocks):
    for b in range(blocks):
        meta[0, b] = blocks
        meta[1, b] = 0

    def chain(c, start):
        size = len_s[0, c]
        end = start + size

        @pl.when(size > 0)
        def _():
            first = start // BLOCK
            last = (end - 1) // BLOCK + 1

            def touch(b, _):
                meta[0, b] = jnp.minimum(meta[0, b], first)
                meta[1, b] = jnp.maximum(meta[1, b], last)
                return 0

            lax.fori_loop(first, last, touch, 0)

        return end

    meta[2, 0] = lax.fori_loop(0, len_s.shape[1], chain, 0)


def prep_kernel(groups, hc, len_s, x, length, w, bias, vbias, gain, shift, qt, kt, vt, kr, vr, nl, codek, codet, meta):
    i = pl.program_id(0)
    blocks = pl.num_programs(0)

    @pl.when(i == 0)
    def _():
        chain_ranges(len_s, meta, blocks)

    xhat, _ = normalise(x[...].astype(F32))
    low = (xhat * gain[...] + shift[...]).astype(BF16)
    nl[...] = low
    for g in range(groups):
        joined = dot(w[g], low, 1, 1) + bias[g]
        s = slice(g * hc, (g + 1) * hc)
        qt[s, :] = joined[:hc].astype(BF16)
        kt[s, :] = joined[hc : 2 * hc].astype(BF16)
        vt[s, :] = joined[2 * hc :].astype(BF16)
        kv = dot(low, w[g, hc:, :], 1, 1)
        kr[:, s] = kv[:, :hc].astype(BF16)
        vr[:, s] = (kv[:, hc:] + vbias[g]).astype(BF16)
    a = lax.broadcasted_iota(jnp.int32, (CODES, CODES), 0)
    b = lax.broadcasted_iota(jnp.int32, (CODES, CODES), 1)
    size = length[...].astype(F32)
    size_col = jnp.sum(jnp.where(a == b, size, 0.0), axis=1, keepdims=True)
    end_col = jnp.sum(jnp.where(b <= a, size, 0.0), axis=1, keepdims=True)
    end_row = jnp.sum(jnp.where(a <= b, size_col, 0.0), axis=0, keepdims=True)
    start_col, start_row = end_col - size_col, end_row - size
    chains = len_s.shape[1]
    ids_col = lax.broadcasted_iota(jnp.int32, (CODES, 1), 0)
    ids_row = lax.broadcasted_iota(jnp.int32, (1, CODES), 1)
    end_col = jnp.where(ids_col == chains, 1e9, end_col)
    end_row = jnp.where(ids_row == chains, 1e9, end_row)
    base = i * BLOCK
    slot = (base + lax.broadcasted_iota(jnp.int32, (CODES, BLOCK), 1)).astype(F32)
    codet[...] = jnp.where((slot >= start_col) & (slot < end_col), 1.0, 0.0).astype(BF16)
    slot = (base + lax.broadcasted_iota(jnp.int32, (BLOCK, CODES), 0)).astype(F32)
    codek[...] = jnp.where((slot >= start_row) & (slot < end_row), 0.0, -1e30).astype(BF16)


def prep(tokens, lengths, w, bias, vbias, gain, shift):
    slots, width = tokens.shape
    groups, hc3, _ = w.shape
    hc = hc3 // 3
    hidden = groups * hc
    chains = lengths.shape[1]
    length = jnp.pad(lengths, ((0, 0), (0, CODES - chains)))
    blocks = slots // BLOCK
    t = jax.ShapeDtypeStruct((hidden, slots), BF16)
    r = jax.ShapeDtypeStruct((slots, hidden), BF16)
    return pl.pallas_call(
        functools.partial(prep_kernel, groups, hc),
        grid=(blocks,),
        in_specs=[
            SMEM,
            rows(BLOCK, width),
            whole(1, CODES),
            whole(*w.shape),
            whole(*bias.shape),
            whole(*vbias.shape),
            whole(1, width),
            whole(1, width),
        ],
        out_specs=[
            cols(hidden, BLOCK),
            cols(hidden, BLOCK),
            cols(hidden, BLOCK),
            rows(BLOCK, hidden),
            rows(BLOCK, hidden),
            rows(BLOCK, width),
            rows(BLOCK, CODES),
            cols(CODES, BLOCK),
            SMEM,
        ],
        out_shape=[
            t,
            t,
            t,
            r,
            r,
            jax.ShapeDtypeStruct((slots, width), BF16),
            jax.ShapeDtypeStruct((slots, CODES), BF16),
            jax.ShapeDtypeStruct((CODES, slots), BF16),
            jax.ShapeDtypeStruct((3, blocks), jnp.int32),
        ],
        compiler_params=pltpu.CompilerParams(vmem_limit_bytes=VMEM),
        name="prep",
    )(lengths, tokens, length, w, bias, vbias, gain, shift)


def padded(part, h):
    zero = jnp.zeros_like(part)
    return jnp.concatenate([part, zero] if h % 2 == 0 else [zero, part], axis=0)


def pair(h):
    return pl.ds(h // 2 * 2 * HEAD_DIM, 2 * HEAD_DIM)


def head(h):
    return pl.ds(h * HEAD_DIM, HEAD_DIM)


def attend_kernel(heads, ahead, meta, qt, codet, kr, codek, vt, ot, lse, acc, top, total):
    i = pl.program_id(0)
    acc[...] = jnp.zeros_like(acc)
    total[...] = jnp.zeros_like(total)
    top[...] = jnp.full_like(top, -1e38)

    def step(j, _):
        js = pl.ds(pl.multiple_of(j * BLOCK, BLOCK), BLOCK)
        scores, probs, decays = {}, {}, {}
        code_k, code_t = codek[js, :], codet[...]
        for t in range(heads + 2 * ahead):
            if t < heads:
                left = jnp.concatenate([kr[js, pair(t)], code_k], axis=1)
                right = jnp.concatenate([padded(qt[head(t), :], t), code_t], axis=0)
                scores[t] = dot(left, right)
            h = t - ahead
            if 0 <= h < heads:
                s = scores.pop(h)
                old = top[h : h + 1, :]
                new = jnp.maximum(old, jnp.max(s, axis=0, keepdims=True))
                top[h : h + 1, :] = new
                p = jnp.exp2(s * SCALE - new * SCALE)
                decays[h] = jnp.exp2((old - new) * SCALE)
                part = jnp.sum(p.reshape(BLOCK // 8, 8, BLOCK), axis=0)
                total[8 * h : 8 * h + 8, :] = total[8 * h : 8 * h + 8, :] * decays[h] + part
                probs[h] = p.astype(BF16)
            h = t - 2 * ahead
            if 0 <= h < heads:
                mixed = dot(vt[head(h), js], probs.pop(h))
                acc[head(h), :] = acc[head(h), :] * decays.pop(h) + mixed
        return 0

    lax.fori_loop(meta[0, i], meta[1, i], step, 0)
    for h in range(heads):
        summed = jnp.sum(total[8 * h : 8 * h + 8, :], axis=0, keepdims=True)
        seen = summed > 0.0
        summed = jnp.where(seen, summed, 1.0)
        ot[head(h), :] = (acc[head(h), :] / summed).astype(BF16)
        lse[h : h + 1, :] = jnp.where(seen, top[h : h + 1, :] * SCALE + jnp.log2(summed), 0.0)


def attend(meta, qt, codet, kr, codek, vt):
    hidden, slots = qt.shape
    heads = hidden // HEAD_DIM
    return pl.pallas_call(
        functools.partial(attend_kernel, heads, 4),
        grid=(slots // BLOCK,),
        in_specs=[
            SMEM,
            cols(hidden, BLOCK),
            cols(CODES, BLOCK),
            whole(*kr.shape),
            whole(*codek.shape),
            whole(*vt.shape),
        ],
        out_specs=[cols(hidden, BLOCK), cols(heads, BLOCK)],
        out_shape=[
            jax.ShapeDtypeStruct((hidden, slots), BF16),
            jax.ShapeDtypeStruct((heads, slots), F32),
        ],
        scratch_shapes=[
            pltpu.VMEM((hidden, BLOCK), F32),
            pltpu.VMEM((heads, BLOCK), F32),
            pltpu.VMEM((8 * heads, BLOCK), F32),
        ],
        compiler_params=pltpu.CompilerParams(vmem_limit_bytes=VMEM),
        name="attend",
    )(meta, qt, codet, kr, codek, vt)


def gelu_parts(u):
    size = jnp.abs(u)
    bell = jnp.exp2(u * u * (-0.5 * LOG2E))
    t = 1.0 / (1.0 + (0.3275911 * 0.5**0.5) * size)
    q = t * (0.5 * 1.061405429)
    q = t * (q + 0.5 * -1.453152027)
    q = t * (q + 0.5 * 1.421413741)
    q = t * (q + 0.5 * -0.284496736)
    q = t * (q + 0.5 * 0.254829592)
    tail = q * bell
    cdf = jnp.where(u >= 0.0, 1.0 - tail, tail)
    return cdf, u * bell * (2.0 * math.pi) ** -0.5


def feed_kernel(
    groups, meta, x, cot, ot, wo, wu, wd, ob, ub, db, gain, shift,
    out, gm_o, dot_o, delta, grads, sums, g_up, g_down, g_out, s_up, s_rest,
):
    i = pl.program_id(0)

    @pl.when(i == 0)
    def _():
        g_up[...] = jnp.zeros_like(g_up)
        g_down[...] = jnp.zeros_like(g_down)
        g_out[...] = jnp.zeros_like(g_out)
        s_up[...] = jnp.zeros_like(s_up)
        s_rest[...] = jnp.zeros_like(s_rest)

    hc = wo.shape[1]
    hidden, width = groups * hc, wo.shape[2]
    source = x[...].astype(F32)
    o = ot[...]
    w_out = wo[...].reshape(hidden, width)
    middle = source + dot(o, w_out, 0, 0) + ob[...]
    xhat, r = normalise(middle)
    low = (xhat * gain[...] + shift[...]).astype(BF16)
    slot = i * BLOCK + lax.broadcasted_iota(jnp.int32, (BLOCK, 1), 0)
    live = slot < meta[2, 0]
    grad = jnp.where(live, cot[...].astype(F32), 0.0)
    grad_low = grad.astype(BF16)
    ahead = 1
    ups, backs, actives, gus = {}, {}, {}, {}
    down, gnt = None, None
    for t in range(groups + 2 * ahead):
        if t < groups:
            ups[t] = dot(low, wu[t]) + ub[t]
            backs[t] = dot(grad_low, wd[t], 1, 1)
        g = t - ahead
        if 0 <= g < groups:
            u = ups.pop(g)
            cdf, bump = gelu_parts(u)
            actives[g] = (u * cdf).astype(BF16)
            gus[g] = (backs.pop(g) * (cdf + bump)).astype(BF16)
        g = t - 2 * ahead
        if 0 <= g < groups:
            a, gu = actives.pop(g), gus.pop(g)
            d1, d2 = dot(a, wd[g]), dot(gu, wu[g], 1, 1)
            down = d1 if down is None else down + d1
            gnt = d2 if gnt is None else gnt + d2
            if g == 0:
                g_up[...] += dot(low, gu, 0, 0)
                g_down[...] += dot(a, grad_low, 0, 0)
                s_up[...] += jnp.sum(gu.astype(F32).reshape(BLOCK // 8, 8, -1), axis=0)
    out[...] = jnp.where(live, middle + down + db[...], source).astype(BF16)
    e = gnt * gain[...]
    gm = grad + r * (e - jnp.mean(e, axis=-1, keepdims=True) - xhat * jnp.mean(e * xhat, axis=-1, keepdims=True))
    gm_o[...] = gm
    gml = gm.astype(BF16)
    d = dot(w_out, gml, 1, 1).astype(BF16)
    dot_o[...] = d
    heads = hidden // HEAD_DIM
    delta[...] = jnp.sum((d.astype(F32) * o.astype(F32)).reshape(heads, HEAD_DIM, BLOCK), axis=1)
    g_out[...] += dot(o[:hc], gml)
    for n, v in enumerate((grad, gnt * xhat, gnt, gm)):
        s_rest[8 * n : 8 * n + 8, :] += jnp.sum(v.reshape(BLOCK // 8, 8, width), axis=0)

    @pl.when(i == pl.num_programs(0) - 1)
    def _():
        f = g_down.shape[0]
        grads[:hc, :] = g_out[...].astype(BF16)
        grads[hc : hc + width, :] = g_up[...].astype(BF16)
        grads[hc + width :, :] = g_down[...].astype(BF16)
        for n in range(4):
            sums[n : n + 1, :] = jnp.sum(s_rest[8 * n : 8 * n + 8, :], axis=0, keepdims=True)
        sums[4:5, :] = jnp.sum(s_up[...], axis=0, keepdims=True)
        sums[5:8, :] = jnp.zeros((3, width), F32)


def feed(meta, tokens, cotangent, ot, wo, wu, wd, ob, ub, db, gain, shift):
    slots, width = tokens.shape
    groups, hc, _ = wo.shape
    ffn = wu.shape[2]
    hidden = groups * hc
    heads = hidden // HEAD_DIM
    vec = whole(1, width)
    return pl.pallas_call(
        functools.partial(feed_kernel, groups),
        grid=(slots // BLOCK,),
        in_specs=[
            SMEM,
            rows(BLOCK, width),
            rows(BLOCK, width),
            cols(hidden, BLOCK),
            whole(*wo.shape),
            whole(*wu.shape),
            whole(*wd.shape),
            vec,
            whole(*ub.shape),
            vec,
            vec,
            vec,
        ],
        out_specs=[
            rows(BLOCK, width),
            rows(BLOCK, width),
            cols(hidden, BLOCK),
            cols(heads, BLOCK),
            whole(hc + width + ffn, width),
            whole(8, width),
        ],
        out_shape=[
            jax.ShapeDtypeStruct((slots, width), BF16),
            jax.ShapeDtypeStruct((slots, width), F32),
            jax.ShapeDtypeStruct((hidden, slots), BF16),
            jax.ShapeDtypeStruct((heads, slots), F32),
            jax.ShapeDtypeStruct((hc + width + ffn, width), BF16),
            jax.ShapeDtypeStruct((8, width), F32),
        ],
        scratch_shapes=[
            pltpu.VMEM((width, ffn), F32),
            pltpu.VMEM((ffn, width), F32),
            pltpu.VMEM((hc, width), F32),
            pltpu.VMEM((8, ffn), F32),
            pltpu.VMEM((32, width), F32),
        ],
        compiler_params=pltpu.CompilerParams(vmem_limit_bytes=VMEM),
        name="feed",
    )(meta, tokens, cotangent, ot, wo, wu, wd, ob, ub, db, gain, shift)


def reverse_kernel(heads, ahead, meta, kr, vr, kt, qt, dt, codek, codet, lse, delta, dq, dk, dv, dqs, dks, dvs):
    dqs[...] = jnp.zeros_like(dqs)
    dks[...] = jnp.zeros_like(dks)
    dvs[...] = jnp.zeros_like(dvs)

    def column(j, _):
        js = pl.ds(pl.multiple_of(j * BLOCK, BLOCK), BLOCK)

        def step(i, _):
            qs = pl.ds(pl.multiple_of(i * BLOCK, BLOCK), BLOCK)
            scores, backs, grads, probs = {}, {}, {}, {}
            code_k, code_t = codek[js, :], codet[:, qs]
            for t in range(heads + 2 * ahead):
                if t < heads:
                    left = jnp.concatenate([kr[js, pair(t)], code_k], axis=1)
                    right = jnp.concatenate([padded(qt[head(t), qs], t), code_t], axis=0)
                    scores[t] = dot(left, right)
                    backs[t] = dot(vr[js, pair(t)], padded(dt[head(t), qs], t))
                h = t - ahead
                if 0 <= h < heads:
                    p = jnp.exp2(scores.pop(h) * SCALE - lse[h : h + 1, qs])
                    grads[h] = (p * (backs.pop(h) - delta[h : h + 1, qs])).astype(BF16)
                    probs[h] = p.astype(BF16)
                h = t - 2 * ahead
                if 0 <= h < heads:
                    ds, p = grads.pop(h), probs.pop(h)
                    dqs[head(h), qs] += dot(kt[head(h), js], ds)
                    dks[head(h), js] += dot(qt[head(h), qs], ds, 1, 1)
                    dvs[head(h), js] += dot(dt[head(h), qs], p, 1, 1)
            return 0

        lax.fori_loop(meta[0, j], meta[1, j], step, 0)
        return 0

    lax.fori_loop(0, kr.shape[0] // BLOCK, column, 0)
    factor = HEAD_DIM**-0.5
    dq[...] = (dqs[...] * factor).astype(BF16)
    dk[...] = (dks[...] * factor).astype(BF16)
    dv[...] = dvs[...].astype(BF16)


def reverse(meta, kr, vr, kt, qt, dt, codek, codet, lse, delta):
    hidden, slots = qt.shape
    heads = hidden // HEAD_DIM
    vm = pl.BlockSpec(memory_space=pltpu.VMEM)
    t = jax.ShapeDtypeStruct((hidden, slots), BF16)
    return pl.pallas_call(
        functools.partial(reverse_kernel, heads, 2),
        in_specs=[SMEM] + [vm] * 9,
        out_specs=[vm] * 3,
        out_shape=[t, t, t],
        scratch_shapes=[pltpu.VMEM((hidden, slots), F32)] * 3,
        compiler_params=pltpu.CompilerParams(vmem_limit_bytes=VMEM),
        name="reverse",
    )(meta, kr, vr, kt, qt, dt, codek, codet, lse, delta)


def finish_kernel(groups, meta, x, cot, gm, nl, dq, dk, dv, w, gain, out, grads, sums, bias, g_w, s_rest, s_bias):
    i = pl.program_id(0)

    @pl.when(i == 0)
    def _():
        g_w[...] = jnp.zeros_like(g_w)
        s_rest[...] = jnp.zeros_like(s_rest)
        s_bias[...] = jnp.zeros_like(s_bias)

    hc, width = w.shape[1] // 3, w.shape[2]
    hidden = groups * hc
    gn = None
    for n, d in enumerate((dq, dk, dv)):
        part = dot(d[...], w[:, n * hc : (n + 1) * hc, :].reshape(hidden, width), 0, 0)
        gn = part if gn is None else gn + part
    xhat, r = normalise(x[...].astype(F32))
    e = gn * gain[...]
    inner = r * (e - jnp.mean(e, axis=-1, keepdims=True) - xhat * jnp.mean(e * xhat, axis=-1, keepdims=True))
    slot = i * BLOCK + lax.broadcasted_iota(jnp.int32, (BLOCK, 1), 0)
    skip = jnp.where(slot < meta[2, 0], 0.0, cot[...].astype(F32))
    out[...] = (gm[...] + inner + skip).astype(BF16)
    low = nl[...]
    ones = jnp.ones((8, BLOCK), BF16)
    for n, d in enumerate((dq, dk, dv)):
        own = d[:hc, :]
        g_w[n * hc : (n + 1) * hc, :] += dot(own, low)
        if n != 1:
            s_bias[n // 2] += dot(ones, own, 1, 1)
    for n, v in enumerate((gn * xhat, gn)):
        s_rest[8 * n : 8 * n + 8, :] += jnp.sum(v.reshape(BLOCK // 8, 8, width), axis=0)

    @pl.when(i == pl.num_programs(0) - 1)
    def _():
        grads[...] = g_w[...].astype(BF16)
        for n in range(2):
            sums[n : n + 1, :] = jnp.sum(s_rest[8 * n : 8 * n + 8, :], axis=0, keepdims=True)
            bias[n : n + 1, :] = s_bias[n, :1, :]


def finish(meta, tokens, cotangent, gm, nl, dq, dk, dv, w, gain):
    slots, width = tokens.shape
    groups, hc3, _ = w.shape
    hc = hc3 // 3
    hidden = groups * hc
    return pl.pallas_call(
        functools.partial(finish_kernel, groups),
        grid=(slots // BLOCK,),
        in_specs=[
            SMEM,
            rows(BLOCK, width),
            rows(BLOCK, width),
            rows(BLOCK, width),
            rows(BLOCK, width),
            cols(hidden, BLOCK),
            cols(hidden, BLOCK),
            cols(hidden, BLOCK),
            whole(*w.shape),
            whole(1, width),
        ],
        out_specs=[rows(BLOCK, width), whole(hc3, width), whole(2, width), whole(2, hc)],
        out_shape=[
            jax.ShapeDtypeStruct((slots, width), BF16),
            jax.ShapeDtypeStruct((hc3, width), BF16),
            jax.ShapeDtypeStruct((2, width), F32),
            jax.ShapeDtypeStruct((2, hc), F32),
        ],
        scratch_shapes=[
            pltpu.VMEM((hc3, width), F32),
            pltpu.VMEM((16, width), F32),
            pltpu.VMEM((2, 8, hc), F32),
        ],
        compiler_params=pltpu.CompilerParams(vmem_limit_bytes=VMEM),
        name="finish",
    )(meta, tokens, cotangent, gm, nl, dq, dk, dv, w, gain)


def layer(tokens, lengths, cotangent, wqkv, qbias, wo, ob, wu, ub, wd, db, g1, s1, g2, s2):
    groups, hc3, width = wqkv.shape
    hc = hc3 // 3
    bias = jnp.stack([qbias[:, 0], jnp.zeros_like(qbias[:, 0]), qbias[:, 1]], axis=1).reshape(groups, hc3, 1)
    vbias = qbias[:, 1:2]
    row = lambda v: v.reshape(1, width)
    qt, kt, vt, kr, vr, nl, codek, codet, meta = prep(tokens, lengths, wqkv, bias, vbias, row(g1), row(s1))
    ot, lse = attend(meta, qt, codet, kr, codek, vt)
    out, gm, dt, delta, grads, sums = feed(meta, tokens, cotangent, ot, wo, wu, wd, row(ob), ub, row(db), row(g2), row(s2))
    dq, dk, dv = reverse(meta, kr, vr, kt, qt, dt, codek, codet, lse, delta)
    grad_tokens, gw, sums1, gb = finish(meta, tokens, cotangent, gm, nl, dq, dk, dv, wqkv, row(g1))
    return out, grad_tokens, grads, sums, gw, sums1, gb


def gather_groups(local, group_count):
    core = lax.axis_index("dp") % 2
    half = local.shape[0] // 2
    mine = lax.dynamic_slice_in_dim(local, core * half, half, 0)
    swap = [(d, d ^ 1) for d in range(lax.axis_size("dp"))]
    shards = [local]
    for k in range(1, group_count):
        got = lax.ppermute(mine, "tensor", [(t, (t - k) % group_count) for t in range(group_count)])
        other = lax.ppermute(got, "dp", swap)
        shards.append(jnp.where(core == 0, jnp.concatenate([got, other]), jnp.concatenate([other, got])))
    return jnp.stack(shards)


def body(
    tokens, lengths, cotangent, qkv_weight, qv_bias, out_weight, out_bias, up_weight, up_bias,
    down_weight, down_bias, first_gain, first_shift, second_gain, second_shift,
):
    groups, packs = lax.axis_size("tensor"), lax.axis_size("dp")
    width, _, hc = qkv_weight.shape
    ffn = up_weight.shape[1]
    local_qkv = jnp.transpose(qkv_weight, (1, 2, 0)).reshape(3 * hc, width)
    wqkv = gather_groups(local_qkv, groups)
    rest = gather_groups(jnp.concatenate([out_weight, up_weight, down_weight]), groups)
    wo, wu, wd = rest[:, :hc], rest[:, hc : hc + width], rest[:, hc + width :]
    small = jnp.concatenate([qv_bias.reshape(-1), up_bias])
    smalls = jnp.stack(
        [small]
        + [lax.ppermute(small, "tensor", [(t, (t - k) % groups) for t in range(groups)]) for k in range(1, groups)]
    )
    qbias = smalls[:, : 2 * hc].reshape(groups, 2, hc)
    ub = smalls[:, 2 * hc :].reshape(groups, 1, ffn)
    out, grad_tokens, grads, sums, gw, sums1, gb = layer(
        tokens, lengths, cotangent, wqkv, qbias, wo, out_bias, wu, ub, wd, down_bias,
        first_gain, first_shift, second_gain, second_shift,
    )
    share = 1.0 / packs
    grads = lax.psum(grads, "dp").astype(F32) * share
    gw = lax.psum(gw, "dp").astype(F32) * share
    sums, sums1, gb = (v * share for v in lax.psum((sums, sums1, gb), "dp"))
    return (
        out,
        grad_tokens,
        jnp.transpose(gw.reshape(3, hc, width), (2, 0, 1)),
        gb,
        grads[:hc],
        sums[3],
        grads[hc : hc + width],
        sums[4],
        grads[hc + width :],
        sums[0],
        sums1[0],
        sums1[1],
        sums[1],
        sums[2],
    )


def solution(mesh):
    in_specs = (
        P("dp", None),
        P("dp", None),
        P("dp", None),
        P(None, None, "tensor"),
        P(None, "tensor"),
        P("tensor", None),
        P(),
        P(None, "tensor"),
        P("tensor"),
        P("tensor", None),
        P(),
        P(),
        P(),
        P(),
        P(),
    )
    out_specs = (
        P("dp", None),
        P("dp", None),
        P(None, None, "tensor"),
        P(None, "tensor"),
        P("tensor", None),
        P(),
        P(None, "tensor"),
        P("tensor"),
        P("tensor", None),
        P(),
        P(),
        P(),
        P(),
        P(),
    )
    return jax.shard_map(body, mesh=mesh, in_specs=in_specs, out_specs=out_specs, check_vma=False)
```

```python
import functools
import math

import jax
import jax.numpy as jnp
from jax import lax
from jax.experimental import pallas as pl
from jax.experimental.pallas import tpu as pltpu
from jax.sharding import PartitionSpec as P

HEAD_DIM = 64
BLOCK = 256
CODES = 128
LOG2E = math.log2(math.e)
SCALE = LOG2E * HEAD_DIM**-0.5
VMEM = 60 << 20
BF16 = jnp.bfloat16
F32 = jnp.float32


def dot(a, b, ca=1, cb=0):
    return lax.dot_general(a, b, (((ca,), (cb,)), ((), ())), preferred_element_type=F32)


def whole(*shape):
    return pl.BlockSpec(shape, lambda *_: (0,) * len(shape))


def rows(n, width):
    return pl.BlockSpec((n, width), lambda i: (i, 0))


def cols(height, n):
    return pl.BlockSpec((height, n), lambda i: (0, i))


SMEM = pl.BlockSpec(memory_space=pltpu.SMEM)


def normalise(v):
    centred = v - jnp.mean(v, axis=-1, keepdims=True)
    r = lax.rsqrt(jnp.mean(centred * centred, axis=-1, keepdims=True) + 1e-05)
    return centred * r, r


def chain_ranges(len_s, meta, blocks):
    for b in range(blocks):
        meta[0, b] = blocks
        meta[1, b] = 0

    def chain(c, start):
        size = len_s[0, c]
        end = start + size

        @pl.when(size > 0)
        def _():
            first = start // BLOCK
            last = (end - 1) // BLOCK + 1

            def touch(b, _):
                meta[0, b] = jnp.minimum(meta[0, b], first)
                meta[1, b] = jnp.maximum(meta[1, b], last)
                return 0

            lax.fori_loop(first, last, touch, 0)

        return end

    meta[2, 0] = lax.fori_loop(0, len_s.shape[1], chain, 0)


def cost(flops, moved=0):
    return pl.CostEstimate(flops=int(flops), bytes_accessed=int(moved), transcendentals=0)


def length_row(len_s):
    ids = lax.broadcasted_iota(jnp.int32, (1, CODES), 1)
    row = jnp.zeros((1, CODES), jnp.int32)
    for c in range(len_s.shape[1]):
        row = jnp.where(ids == c, len_s[0, c], row)
    return row.astype(F32)


def codes(i, chains, size, codek, codet):
    a = lax.broadcasted_iota(jnp.int32, (CODES, CODES), 0)
    b = lax.broadcasted_iota(jnp.int32, (CODES, CODES), 1)
    size_col = jnp.sum(jnp.where(a == b, size, 0.0), axis=1, keepdims=True)
    end_col = jnp.sum(jnp.where(b <= a, size, 0.0), axis=1, keepdims=True)
    end_row = jnp.sum(jnp.where(a <= b, size_col, 0.0), axis=0, keepdims=True)
    start_col, start_row = end_col - size_col, end_row - size
    ids_col = lax.broadcasted_iota(jnp.int32, (CODES, 1), 0)
    ids_row = lax.broadcasted_iota(jnp.int32, (1, CODES), 1)
    end_col = jnp.where(ids_col == chains, 1e9, end_col)
    end_row = jnp.where(ids_row == chains, 1e9, end_row)
    base = i * BLOCK
    slot = (base + lax.broadcasted_iota(jnp.int32, (CODES, BLOCK), 1)).astype(F32)
    codet[...] = jnp.where((slot >= start_col) & (slot < end_col), 1.0, 0.0).astype(BF16)
    slot = (base + lax.broadcasted_iota(jnp.int32, (BLOCK, CODES), 0)).astype(F32)
    codek[...] = jnp.where((slot >= start_row) & (slot < end_row), 0.0, -1e30).astype(BF16)


def project(g, hc, low, w, bias, vbias, qt, kt, vt, kr, vr):
    joined = dot(w, low, 1, 1)
    s = slice(g * hc, (g + 1) * hc)
    qt[s, :] = (joined[:hc] + bias[:hc]).astype(BF16)
    kt[s, :] = joined[hc : 2 * hc].astype(BF16)
    vt[s, :] = (joined[2 * hc :] + bias[hc:]).astype(BF16)
    kv = dot(low, w[hc:], 1, 1)
    kr[:, s] = kv[:, :hc].astype(BF16)
    vr[:, s] = (kv[:, hc:] + vbias).astype(BF16)


def bias_columns(extra, which):
    parts = extra.shape[0] // 4 - 2
    row = lax.broadcasted_iota(jnp.int32, (extra.shape[0], BLOCK), 0)
    picked = (row == which) | (row == which + parts) | (row == which + 2 * parts)
    return dot(extra, jnp.where(picked, 1.0, 0.0).astype(BF16), 0, 0)


def bias_row(extra, which):
    parts = extra.shape[0] // 4 - 2
    row = lax.broadcasted_iota(jnp.int32, extra.shape, 0)
    picked = (row == which) | (row == which + parts) | (row == which + 2 * parts)
    return jnp.sum(jnp.where(picked, extra.astype(F32), 0.0), axis=0, keepdims=True)


def bias_rows(extra, count):
    return jnp.concatenate([bias_row(extra, n) for n in range(count)], axis=1)


def prep_own_kernel(hc, len_s, x, wn, extra, gain, shift, qt, kt, vt, kr, vr, nl, codek, codet, meta, w, bias, size):
    i = pl.program_id(0)

    @pl.when(i == 0)
    def _():
        chain_ranges(len_s, meta, pl.num_programs(0))
        for p in range(3):
            w[p * hc : (p + 1) * hc, :] = wn[p].T
        for n in range(2):
            bias[n * hc : (n + 1) * hc, :] = bias_columns(extra[...], wn.shape[1] // hc + n)
        size[...] = length_row(len_s)

    xhat, _ = normalise(x[...].astype(F32))
    low = (xhat * gain[...] + shift[...]).astype(BF16)
    nl[...] = low
    project(0, hc, low, w[...], bias, bias_row(extra[...], wn.shape[1] // hc + 1), qt, kt, vt, kr, vr)
    codes(i, len_s.shape[1], size[...], codek, codet)


def projected(hidden, slots):
    t = jax.ShapeDtypeStruct((hidden, slots), BF16)
    r = jax.ShapeDtypeStruct((slots, hidden), BF16)
    return [cols(hidden, BLOCK)] * 3 + [rows(BLOCK, hidden)] * 2, [t, t, t, r, r]


def prep_own(tokens, lengths, w, extra, gain, shift):
    slots, width = tokens.shape
    hc = w.shape[2]
    blocks = slots // BLOCK
    specs, shapes = projected(hc, slots)
    return pl.pallas_call(
        functools.partial(prep_own_kernel, hc),
        grid=(blocks,),
        in_specs=[
            SMEM,
            rows(BLOCK, width),
            whole(*w.shape),
            whole(*extra.shape),
            whole(1, width),
            whole(1, width),
        ],
        out_specs=specs + [rows(BLOCK, width), rows(BLOCK, CODES), cols(CODES, BLOCK), SMEM, whole(3 * hc, width)],
        out_shape=shapes
        + [
            jax.ShapeDtypeStruct((slots, width), BF16),
            jax.ShapeDtypeStruct((slots, CODES), BF16),
            jax.ShapeDtypeStruct((CODES, slots), BF16),
            jax.ShapeDtypeStruct((3, blocks), jnp.int32),
            jax.ShapeDtypeStruct((3 * hc, width), BF16),
        ],
        scratch_shapes=[pltpu.VMEM((2 * hc, BLOCK), F32), pltpu.VMEM((1, CODES), F32)],
        compiler_params=pltpu.CompilerParams(vmem_limit_bytes=VMEM),
        cost_estimate=cost(8e9),
        name="prep_own",
    )(lengths, tokens, w, extra, gain, shift)


def place(core, dst, g, mine, theirs, first, count, at=0):
    for which, part in ((core, mine), (1 - core, theirs)):
        dst[g, pl.ds(pl.multiple_of(which * count, 16), count), :] = part[g, first : first + count, :]


def prep_others_kernel(others, hc, core_s, nl, mine, theirs, qt, kt, vt, kr, vr, w, ub, bias):
    half, width = w.shape[2] // 2, w.shape[2]
    extras = [mine[g, 3 * half :, :] for g in range(others)]
    first = width // hc

    @pl.when(pl.program_id(0) == 0)
    def _():
        for g in range(others):
            for p in range(3):
                for which, part in ((core_s[0], mine), (1 - core_s[0], theirs)):
                    at = pl.ds(pl.multiple_of(which * half, 128), half)
                    w[g, p * hc : (p + 1) * hc, at] = part[g, p * half : (p + 1) * half, :].T
            for n in range(2):
                bias[g, n * hc : (n + 1) * hc, :] = bias_columns(extras[g], first + n)
            ub[g] = bias_rows(extras[g], first)

    low = nl[...]
    for g in range(others):
        project(g, hc, low, w[g], bias.at[g], bias_row(extras[g], first + 1), qt, kt, vt, kr, vr)


def prep_others(core, nl, mine, theirs):
    slots, width = nl.shape
    others, _, hc = mine.shape
    specs, shapes = projected(others * hc, slots)
    return pl.pallas_call(
        functools.partial(prep_others_kernel, others, hc),
        grid=(slots // BLOCK,),
        in_specs=[
            SMEM,
            rows(BLOCK, width),
            whole(*mine.shape),
            whole(*theirs.shape),
        ],
        out_specs=specs + [whole(others, 3 * hc, width), whole(others, 1, width)],
        out_shape=shapes
        + [
            jax.ShapeDtypeStruct((others, 3 * hc, width), BF16),
            jax.ShapeDtypeStruct((others, 1, width), F32),
        ],
        scratch_shapes=[pltpu.VMEM((others, 2 * hc, BLOCK), F32)],
        compiler_params=pltpu.CompilerParams(vmem_limit_bytes=VMEM),
        cost_estimate=cost(9e9),
        name="prep_others",
    )(core, nl, mine, theirs)


def padded(part, h):
    zero = jnp.zeros_like(part)
    return jnp.concatenate([part, zero] if h % 2 == 0 else [zero, part], axis=0)


def pair(h):
    return pl.ds(h // 2 * 2 * HEAD_DIM, 2 * HEAD_DIM)


def head(h):
    return pl.ds(h * HEAD_DIM, HEAD_DIM)


def attend_kernel(heads, keys, ahead, meta, qt, codet, kr, codek, vt, ot, lse, acc, top, total):
    i = pl.program_id(0)
    acc[...] = jnp.zeros_like(acc)
    total[...] = jnp.zeros_like(total)
    top[...] = jnp.full_like(top, -1e38)
    unit = keys // BLOCK

    def step(j, _):
        js = pl.ds(pl.multiple_of(j * keys, keys), keys)
        scores, probs, decays = {}, {}, {}
        code_k, code_t = codek[js, :], codet[...]
        for t in range(heads + 2 * ahead):
            if t < heads:
                left = jnp.concatenate([kr[js, pair(t)], code_k], axis=1)
                right = jnp.concatenate([padded(qt[head(t), :], t), code_t], axis=0)
                scores[t] = dot(left, right)
            h = t - ahead
            if 0 <= h < heads:
                s = scores.pop(h)
                old = top[h : h + 1, :]
                new = jnp.maximum(old, jnp.max(s, axis=0, keepdims=True))
                top[h : h + 1, :] = new
                p = jnp.exp2(s * SCALE - new * SCALE)
                decays[h] = jnp.exp2((old - new) * SCALE)
                part = jnp.sum(p.reshape(keys // 8, 8, BLOCK), axis=0)
                total[8 * h : 8 * h + 8, :] = total[8 * h : 8 * h + 8, :] * decays[h] + part
                probs[h] = p.astype(BF16)
            h = t - 2 * ahead
            if 0 <= h < heads:
                mixed = dot(vt[head(h), js], probs.pop(h))
                acc[head(h), :] = acc[head(h), :] * decays.pop(h) + mixed
        return 0

    lax.fori_loop(meta[0, i] // unit, (meta[1, i] + unit - 1) // unit, step, 0)
    for h in range(heads):
        summed = jnp.sum(total[8 * h : 8 * h + 8, :], axis=0, keepdims=True)
        seen = summed > 0.0
        summed = jnp.where(seen, summed, 1.0)
        ot[head(h), :] = (acc[head(h), :] / summed).astype(BF16)
        lse[h : h + 1, :] = jnp.where(seen, top[h : h + 1, :] * SCALE + jnp.log2(summed), 0.0)


def attend(keys, ahead, meta, qt, codet, kr, codek, vt):
    hidden, slots = qt.shape
    heads = hidden // HEAD_DIM
    return pl.pallas_call(
        functools.partial(attend_kernel, heads, keys, ahead),
        grid=(slots // BLOCK,),
        in_specs=[
            SMEM,
            cols(hidden, BLOCK),
            cols(CODES, BLOCK),
            whole(*kr.shape),
            whole(*codek.shape),
            whole(*vt.shape),
        ],
        out_specs=[cols(hidden, BLOCK), cols(heads, BLOCK)],
        out_shape=[
            jax.ShapeDtypeStruct((hidden, slots), BF16),
            jax.ShapeDtypeStruct((heads, slots), F32),
        ],
        scratch_shapes=[
            pltpu.VMEM((hidden, BLOCK), F32),
            pltpu.VMEM((heads, BLOCK), F32),
            pltpu.VMEM((8 * heads, BLOCK), F32),
        ],
        compiler_params=pltpu.CompilerParams(vmem_limit_bytes=VMEM),
        cost_estimate=cost(4.0 * slots * slots * heads * 256),
        name="attend",
    )(meta, qt, codet, kr, codek, vt)


def gelu_parts(u):
    size = jnp.abs(u)
    bell = jnp.exp2(u * u * (-0.5 * LOG2E))
    t = 1.0 / (1.0 + (0.3275911 * 0.5**0.5) * size)
    q = t * (0.5 * 1.061405429)
    q = t * (q + 0.5 * -1.453152027)
    q = t * (q + 0.5 * 1.421413741)
    q = t * (q + 0.5 * -0.284496736)
    q = t * (q + 0.5 * 0.254829592)
    tail = q * bell
    cdf = jnp.where(u >= 0.0, 1.0 - tail, tail)
    return cdf, u * bell * (2.0 * math.pi) ** -0.5


def feed_kernel(
    groups, core_s, meta, x, cot, ot_own, ot_rest, wo_own, wu_own, wd_own, mine, theirs, ob, ub_own, ub, db, gain, shift,
    out, gm_o, dt_own, dt_rest, delta_own, delta_rest, grads, sums, wo, wu, wd, g_up, g_down, g_out, s_up, s_rest,
):
    i = pl.program_id(0)

    @pl.when(i == 0)
    def _():
        g_up[...] = jnp.zeros_like(g_up)
        g_down[...] = jnp.zeros_like(g_down)
        g_out[...] = jnp.zeros_like(g_out)
        s_up[...] = jnp.zeros_like(s_up)
        s_rest[...] = jnp.zeros_like(s_rest)
        wo[0], wu[0], wd[0] = wo_own[...], wu_own[...], wd_own[...]
        for g in range(groups - 1):
            first = 0
            for dst in (wo, wu, wd):
                count = dst.shape[1] // 2
                place(core_s[0], dst.at[1:], g, mine, theirs, first, count)
                first += count

    hc = wo.shape[1]
    hidden, width = groups * hc, wo.shape[2]
    source = x[...].astype(F32)
    o = jnp.concatenate([ot_own[...], ot_rest[...]], axis=0)
    w_out = wo[...].reshape(hidden, width)
    middle = source + dot(o, w_out, 0, 0) + ob[...]
    xhat, r = normalise(middle)
    low = (xhat * gain[...] + shift[...]).astype(BF16)
    slot = i * BLOCK + lax.broadcasted_iota(jnp.int32, (BLOCK, 1), 0)
    live = slot < meta[2, 0]
    grad = jnp.where(live, cot[...].astype(F32), 0.0)
    grad_low = grad.astype(BF16)
    ahead = 1
    ups, backs, actives, gus = {}, {}, {}, {}
    down, gnt = None, None
    for t in range(groups + 2 * ahead):
        if t < groups:
            ups[t] = dot(low, wu[t]) + (ub_own[...] if t == 0 else ub[t - 1])
            backs[t] = dot(grad_low, wd[t], 1, 1)
        g = t - ahead
        if 0 <= g < groups:
            u = ups.pop(g)
            cdf, bump = gelu_parts(u)
            actives[g] = (u * cdf).astype(BF16)
            gus[g] = (backs.pop(g) * (cdf + bump)).astype(BF16)
        g = t - 2 * ahead
        if 0 <= g < groups:
            a, gu = actives.pop(g), gus.pop(g)
            d1, d2 = dot(a, wd[g]), dot(gu, wu[g], 1, 1)
            down = d1 if down is None else down + d1
            gnt = d2 if gnt is None else gnt + d2
            if g == 0:
                g_up[...] += dot(low, gu, 0, 0)
                g_down[...] += dot(a, grad_low, 0, 0)
                s_up[...] += jnp.sum(gu.astype(F32).reshape(BLOCK // 8, 8, -1), axis=0)
    out[...] = jnp.where(live, middle + down + db[...], source).astype(BF16)
    e = gnt * gain[...]
    gm = grad + r * (e - jnp.mean(e, axis=-1, keepdims=True) - xhat * jnp.mean(e * xhat, axis=-1, keepdims=True))
    gm_o[...] = gm
    gml = gm.astype(BF16)
    d = dot(w_out, gml, 1, 1).astype(BF16)
    dt_own[...] = d[:hc]
    dt_rest[...] = d[hc:]
    inner = jnp.sum((d.astype(F32) * o.astype(F32)).reshape(hidden // HEAD_DIM, HEAD_DIM, BLOCK), axis=1)
    delta_own[...] = inner[: hc // HEAD_DIM]
    delta_rest[...] = inner[hc // HEAD_DIM :]
    g_out[...] += dot(o[:hc], gml)
    for n, v in enumerate((grad, gnt * xhat, gnt, gm)):
        s_rest[8 * n : 8 * n + 8, :] += jnp.sum(v.reshape(BLOCK // 8, 8, width), axis=0)

    @pl.when(i == pl.num_programs(0) - 1)
    def _():
        f = g_down.shape[0]
        grads[:hc, :] = g_out[...].astype(BF16)
        grads[hc : hc + width, :] = g_up[...].astype(BF16)
        grads[hc + width :, :] = g_down[...].astype(BF16)
        for n in range(4):
            sums[n : n + 1, :] = jnp.sum(s_rest[8 * n : 8 * n + 8, :], axis=0, keepdims=True)
        sums[4:5, :] = jnp.sum(s_up[...], axis=0, keepdims=True)
        sums[5:8, :] = jnp.zeros((3, width), F32)


def feed(core, meta, tokens, cotangent, ot_own, ot_rest, wo, wu, wd, mine, theirs, ob, ub_own, ub, db, gain, shift):
    slots, width = tokens.shape
    hc = wo.shape[0]
    ffn = wu.shape[1]
    others = mine.shape[0]
    groups = others + 1
    hr = others * hc
    vec = whole(1, width)
    t = lambda n, kind=BF16: jax.ShapeDtypeStruct((n, slots), kind)
    return pl.pallas_call(
        functools.partial(feed_kernel, groups),
        grid=(slots // BLOCK,),
        in_specs=[
            SMEM,
            SMEM,
            rows(BLOCK, width),
            rows(BLOCK, width),
            cols(hc, BLOCK),
            cols(hr, BLOCK),
            whole(*wo.shape),
            whole(*wu.shape),
            whole(*wd.shape),
            whole(*mine.shape),
            whole(*theirs.shape),
            vec,
            whole(*ub_own.shape),
            whole(*ub.shape),
            vec,
            vec,
            vec,
        ],
        out_specs=[
            rows(BLOCK, width),
            rows(BLOCK, width),
            cols(hc, BLOCK),
            cols(hr, BLOCK),
            cols(hc // HEAD_DIM, BLOCK),
            cols(hr // HEAD_DIM, BLOCK),
            whole(hc + width + ffn, width),
            whole(8, width),
        ],
        out_shape=[
            jax.ShapeDtypeStruct((slots, width), BF16),
            jax.ShapeDtypeStruct((slots, width), F32),
            t(hc),
            t(hr),
            t(hc // HEAD_DIM, F32),
            t(hr // HEAD_DIM, F32),
            jax.ShapeDtypeStruct((hc + width + ffn, width), BF16),
            jax.ShapeDtypeStruct((8, width), F32),
        ],
        scratch_shapes=[
            pltpu.VMEM((groups, hc, width), BF16),
            pltpu.VMEM((groups, width, ffn), BF16),
            pltpu.VMEM((groups, ffn, width), BF16),
            pltpu.VMEM((width, ffn), F32),
            pltpu.VMEM((ffn, width), F32),
            pltpu.VMEM((hc, width), F32),
            pltpu.VMEM((8, ffn), F32),
            pltpu.VMEM((32, width), F32),
        ],
        compiler_params=pltpu.CompilerParams(vmem_limit_bytes=VMEM),
        cost_estimate=cost(4.6e10),
        name="feed",
    )(core, meta, tokens, cotangent, ot_own, ot_rest, wo, wu, wd, mine, theirs, ob, ub_own, ub, db, gain, shift)


def reverse_pass(heads, keys, ahead, meta, kr, vr, kt, qt, dt, codek, codet, lse, delta, dqs, dks, dvs):
    dqs[...] = jnp.zeros_like(dqs)
    dks[...] = jnp.zeros_like(dks)
    dvs[...] = jnp.zeros_like(dvs)
    unit = keys // BLOCK

    def column(j, _):
        js = pl.ds(pl.multiple_of(j * keys, keys), keys)

        def step(i, _):
            qs = pl.ds(pl.multiple_of(i * BLOCK, BLOCK), BLOCK)
            scores, backs, grads, probs = {}, {}, {}, {}
            code_k, code_t = codek[js, :], codet[:, qs]
            for t in range(heads + 2 * ahead):
                if t < heads:
                    left = jnp.concatenate([kr[js, pair(t)], code_k], axis=1)
                    right = jnp.concatenate([padded(qt[head(t), qs], t), code_t], axis=0)
                    scores[t] = dot(left, right)
                    backs[t] = dot(vr[js, pair(t)], padded(dt[head(t), qs], t))
                h = t - ahead
                if 0 <= h < heads:
                    p = jnp.exp2(scores.pop(h) * SCALE - lse[h : h + 1, qs])
                    grads[h] = (p * (backs.pop(h) - delta[h : h + 1, qs])).astype(BF16)
                    probs[h] = p.astype(BF16)
                h = t - 2 * ahead
                if 0 <= h < heads:
                    ds, p = grads.pop(h), probs.pop(h)
                    dqs[head(h), qs] += dot(kt[head(h), js], ds)
                    dks[head(h), js] += dot(qt[head(h), qs], ds, 1, 1)
                    dvs[head(h), js] += dot(dt[head(h), qs], p, 1, 1)
            return 0

        low, high = meta[0, unit * j], meta[1, unit * j]
        for u in range(1, unit):
            low = jnp.minimum(low, meta[0, unit * j + u])
            high = jnp.maximum(high, meta[1, unit * j + u])
        lax.fori_loop(low, high, step, 0)
        return 0

    lax.fori_loop(0, kr.shape[0] // keys, column, 0)


def reverse_kernel(heads, keys, ahead, *refs):
    dq, dk, dv, dqs, dks, dvs = refs[10:]
    reverse_pass(heads, keys, ahead, *refs[:10], dqs, dks, dvs)
    factor = HEAD_DIM**-0.5
    dq[...] = (dqs[...] * factor).astype(BF16)
    dk[...] = (dks[...] * factor).astype(BF16)
    dv[...] = dvs[...].astype(BF16)


def reverse_own_kernel(heads, keys, ahead, *refs):
    x, nl, w, early = refs[10:14]
    dq, dk, dv, late, sums, dqs, dks, dvs, s_rest = refs[14:]
    reverse_kernel(heads, keys, ahead, *refs[:10], dq, dk, dv, dqs, dks, dvs)
    hc = dq.shape[0]
    parts = (dq, dk, dv)
    ones = jnp.ones((8, dq.shape[1]), BF16)
    late[3 * hc :, :] = jnp.zeros((late.shape[0] - 3 * hc, late.shape[1]), BF16)
    late[3 * hc : 3 * hc + 8, :] = early[...].astype(BF16)
    for n, d in enumerate(parts):
        late[n * hc : (n + 1) * hc, :] = dot(d[...], nl[...]).astype(BF16)
        if n != 1:
            late[3 * hc + 8 : 3 * hc + 9, n // 2 * hc : (n // 2 + 1) * hc] = dot(ones, d[...], 1, 1)[:1].astype(BF16)
    s_rest[...] = jnp.zeros_like(s_rest)

    def block(i, _):
        qs = pl.ds(pl.multiple_of(i * BLOCK, BLOCK), BLOCK)
        gn = dot(jnp.concatenate([d[:, qs] for d in parts], axis=0), w[...], 0, 0)
        xhat, _ = normalise(x[qs, :].astype(F32))
        for n, v in enumerate((gn * xhat, gn)):
            s_rest[8 * n : 8 * n + 8, :] += jnp.sum(v.reshape(BLOCK // 8, 8, -1), axis=0)
        return 0

    lax.fori_loop(0, x.shape[0] // BLOCK, block, 0)
    for n in range(2):
        sums[n : n + 1, :] = jnp.sum(s_rest[8 * n : 8 * n + 8, :], axis=0, keepdims=True)


def reverse(keys, ahead, meta, kr, vr, kt, qt, dt, codek, codet, lse, delta, own=None, late=0):
    hidden, slots = qt.shape
    heads = hidden // HEAD_DIM
    vm = pl.BlockSpec(memory_space=pltpu.VMEM)
    t = jax.ShapeDtypeStruct((hidden, slots), BF16)
    shapes = [t, t, t]
    scratch = [pltpu.VMEM((hidden, slots), F32)] * 3
    extra = ()
    if own is not None:
        extra = own
        width = own[0].shape[1]
        shapes += [
            jax.ShapeDtypeStruct((late, width), BF16),
            jax.ShapeDtypeStruct((2, width), F32),
        ]
        scratch += [pltpu.VMEM((16, width), F32)]
    return pl.pallas_call(
        functools.partial(reverse_kernel if own is None else reverse_own_kernel, heads, keys, ahead),
        in_specs=[SMEM] + [vm] * (9 + len(extra)),
        out_specs=[vm] * len(shapes),
        out_shape=shapes,
        scratch_shapes=scratch,
        compiler_params=pltpu.CompilerParams(vmem_limit_bytes=VMEM),
        cost_estimate=cost(6.0 * slots * slots * heads * 256),
        name="reverse",
    )(meta, kr, vr, kt, qt, dt, codek, codet, lse, delta, *extra)


def finish_kernel(share, meta, x, cot, gm, q0, k0, v0, q1, k1, v1, w0, w1, gain, grads, out, *shards):
    i = pl.program_id(0)
    first = 0
    for shard in shards:
        n = shard.shape[0]
        at = pl.ds(pl.multiple_of(first + i * n, 16), n)
        shard[...] = grads[at, :].astype(F32) * share
        first += n * pl.num_programs(0)
    hc, width = w0.shape[0] // 3, w0.shape[1]
    others = w1.shape[0]
    gn = dot(jnp.concatenate([q0[...], k0[...], v0[...]], axis=0), w0[...], 0, 0)
    for n, d in enumerate((q1, k1, v1)):
        gn += dot(d[...], w1[:, n * hc : (n + 1) * hc, :].reshape(others * hc, width), 0, 0)
    xhat, r = normalise(x[...].astype(F32))
    e = gn * gain[...]
    inner = r * (e - jnp.mean(e, axis=-1, keepdims=True) - xhat * jnp.mean(e * xhat, axis=-1, keepdims=True))
    slot = i * BLOCK + lax.broadcasted_iota(jnp.int32, (BLOCK, 1), 0)
    skip = jnp.where(slot < meta[2, 0], 0.0, cot[...].astype(F32))
    out[...] = (gm[...] + inner + skip).astype(BF16)


def finish(share, meta, tokens, cotangent, gm, own, rest, w0, w1, gain, grads, sizes):
    slots, width = tokens.shape
    steps = slots // BLOCK
    hc = own[0].shape[0]
    hr = rest[0].shape[0]
    return pl.pallas_call(
        functools.partial(finish_kernel, share),
        grid=(slots // BLOCK,),
        in_specs=[SMEM, rows(BLOCK, width), rows(BLOCK, width), rows(BLOCK, width)]
        + [cols(hc, BLOCK)] * 3
        + [cols(hr, BLOCK)] * 3
        + [whole(*w0.shape), whole(*w1.shape), whole(1, width), whole(*grads.shape)],
        out_specs=[rows(BLOCK, width)] + [rows(n // steps, width) for n in sizes],
        out_shape=[jax.ShapeDtypeStruct((slots, width), BF16)]
        + [jax.ShapeDtypeStruct((n, width), F32) for n in sizes],
        compiler_params=pltpu.CompilerParams(vmem_limit_bytes=VMEM),
        cost_estimate=cost(9e9),
        name="finish",
    )(meta, tokens, cotangent, gm, *own, *rest, w0, w1, gain, grads)


def last_kernel(share, late, gw, bias, sums, norm_sums, joined):
    hc = bias.shape[1]
    packs, n = late.shape[0], joined.shape[0] // late.shape[0]
    for c in range(packs):
        joined[c * n : (c + 1) * n, :] = late[c, :n, :]
    for p in range(3):
        gw[p] = joined[p * hc : (p + 1) * hc, :].astype(F32).T * share
    tail = joined[3 * hc : 3 * hc + 16, :].astype(F32) * share
    sums[...] = tail[:8]
    bias[0:1, :] = tail[8:9, :hc]
    bias[1:2, :] = tail[8:9, hc : 2 * hc]
    norm_sums[...] = jnp.sum(late[:, n:, :].astype(F32), axis=0)[:8] * share


def last(share, late, hc):
    packs, n, width = late.shape
    vm = pl.BlockSpec(memory_space=pltpu.VMEM)
    return pl.pallas_call(
        functools.partial(last_kernel, share),
        in_specs=[vm],
        out_specs=[vm] * 4,
        out_shape=[
            jax.ShapeDtypeStruct((3, width, hc), F32),
            jax.ShapeDtypeStruct((2, hc), F32),
            jax.ShapeDtypeStruct((8, width), F32),
            jax.ShapeDtypeStruct((8, width), F32),
        ],
        scratch_shapes=[pltpu.VMEM((packs * (n - 16), width), BF16)],
        compiler_params=pltpu.CompilerParams(vmem_limit_bytes=VMEM),
        name="last",
    )(late)


def around(v, axis, k):
    n = lax.axis_size(axis)
    return lax.ppermute(v, axis, [(t, (t - k) % n) for t in range(n)])


def swapped(v):
    return lax.ppermute(v, "dp", [(d, d ^ 1) for d in range(lax.axis_size("dp"))])


def summed_chunk(v):
    packs = lax.axis_size("dp")
    parts = lax.all_to_all(v, "dp", 0, 0, tiled=True)
    return jnp.sum(parts.reshape(packs, -1, v.shape[1]).astype(F32), axis=0).astype(v.dtype)


def spread(v):
    return jnp.broadcast_to(v[None], (lax.axis_size("dp"), *v.shape))


def three_parts(v):
    high = lax.reduce_precision(v, 8, 7)
    mid = lax.reduce_precision(v - high, 8, 7)
    return jnp.stack([high, mid, v - high - mid]).astype(BF16)


def body(
    tokens, lengths, cotangent, qkv_weight, qv_bias, out_weight, out_bias, up_weight, up_bias,
    down_weight, down_bias, first_gain, first_shift, second_gain, second_shift,
):
    groups, packs = lax.axis_size("tensor"), lax.axis_size("dp")
    width, _, hc = qkv_weight.shape
    ffn = up_weight.shape[1]
    share = 1.0 / packs
    core = lax.axis_index("dp") % 2
    core_s = core.reshape(1).astype(jnp.int32)
    row = lambda v: v.reshape(1, -1)
    halved = lambda v, dim: lax.dynamic_slice_in_dim(v, core * (v.shape[dim] // 2), v.shape[dim] // 2, dim)
    turns = range(1, groups)
    local_qkv = jnp.transpose(qkv_weight, (1, 0, 2))
    biases = jnp.concatenate([up_bias.reshape(-1, hc), qv_bias])
    count = biases.shape[0]
    extra = jnp.pad(three_parts(biases).reshape(3 * count, hc), ((0, count + 8), (0, 0)))
    qkv_half = jnp.concatenate([halved(local_qkv, 1).reshape(-1, hc), extra])
    qkv_mine = [around(qkv_half, "tensor", k) for k in turns]
    rest_half = jnp.concatenate([halved(out_weight, 0), halved(up_weight, 0), halved(down_weight, 0)])

    qt0, kt0, vt0, kr0, vr0, nl, codek, codet, meta, wqkv0 = prep_own(
        tokens, lengths, local_qkv, extra, row(first_gain), row(first_shift)
    )
    nl, rest_half, *qkv_mine = lax.optimization_barrier((nl, rest_half, *qkv_mine))
    rest_mine = [around(rest_half, "tensor", k) for k in turns]
    qkv_mine = jnp.stack(qkv_mine)
    qkv_theirs = swapped(qkv_mine)
    ot0, lse0 = attend(2 * BLOCK, 1, meta, qt0, codet, kr0, codek, vt0)
    ot0, qkv_theirs = lax.optimization_barrier((ot0, qkv_theirs))
    qt1, kt1, vt1, kr1, vr1, wqkv1, ub = prep_others(core_s, nl, qkv_mine, qkv_theirs)
    ot1, lse1 = attend(BLOCK, 3, meta, qt1, codet, kr1, codek, vt1)
    ot1, *rest_mine = lax.optimization_barrier((ot1, *rest_mine))
    rest_mine = jnp.stack(rest_mine)
    rest_theirs = swapped(rest_mine)
    out, gm, dt0, dt1, delta0, delta1, grads, sums = feed(
        core_s, meta, tokens, cotangent, ot0, ot1, out_weight, up_weight, down_weight, rest_mine, rest_theirs,
        row(out_bias), row(up_bias), ub, row(down_bias), row(second_gain), row(second_shift),
    )
    grads = summed_chunk(grads)
    late_rows = -(-(3 * hc + 16) // (16 * packs)) * 16 * packs
    *own, late, norm_sums = reverse(
        2 * BLOCK, 1, meta, kr0, vr0, kt0, qt0, dt0, codek, codet, lse0, delta0,
        own=(tokens, nl, wqkv0, sums), late=late_rows,
    )
    norm_sums = lax.psum(norm_sums, "tensor")
    late = lax.psum_scatter(late, "dp", scatter_dimension=0, tiled=True)
    grads, kr1 = lax.optimization_barrier((spread(grads), kr1))
    grads = lax.all_to_all(grads, "dp", 0, 0).reshape(-1, width)
    rest = reverse(BLOCK, 2, meta, kr1, vr1, kt1, qt1, dt1, codek, codet, lse1, delta1)
    late, norm_sums, grads, rest0 = lax.optimization_barrier((late, norm_sums, grads, rest[0]))
    norm_sums = jnp.pad(norm_sums.astype(BF16), ((0, 14), (0, 0)))
    late = lax.all_to_all(spread(jnp.concatenate([late, norm_sums])), "dp", 0, 0)
    grad_tokens, grad_out, grad_up, grad_down = finish(
        share, meta, tokens, cotangent, gm, own, [rest0, *rest[1:]], wqkv0, wqkv1, row(first_gain),
        grads, (hc, width, ffn),
    )
    gw, gb, sums, norm_sums = last(share, late, hc)
    return (
        out,
        grad_tokens,
        jnp.transpose(gw, (1, 0, 2)),
        gb,
        grad_out,
        sums[3],
        grad_up,
        sums[4],
        grad_down,
        sums[0],
        norm_sums[0],
        norm_sums[1],
        sums[1],
        sums[2],
    )


def solution(mesh):
    in_specs = (
        P("dp", None),
        P("dp", None),
        P("dp", None),
        P(None, None, "tensor"),
        P(None, "tensor"),
        P("tensor", None),
        P(),
        P(None, "tensor"),
        P("tensor"),
        P("tensor", None),
        P(),
        P(),
        P(),
        P(),
        P(),
    )
    out_specs = (
        P("dp", None),
        P("dp", None),
        P(None, None, "tensor"),
        P(None, "tensor"),
        P("tensor", None),
        P(),
        P(None, "tensor"),
        P("tensor"),
        P("tensor", None),
        P(),
        P(),
        P(),
        P(),
        P(),
    )
    return jax.shard_map(body, mesh=mesh, in_specs=in_specs, out_specs=out_specs, check_vma=False)
```

```python
import functools
import math

import jax
import jax.numpy as jnp
from jax import lax
from jax.experimental import pallas as pl
from jax.experimental.pallas import tpu as pltpu
from jax.sharding import PartitionSpec as P

HEAD_DIM = 64
BLOCK = 256
PREP = 512
OWNQ = 512
FEED = 512
LAST = 512
CODES = 128
LOG2E = math.log2(math.e)
SCALE = LOG2E * HEAD_DIM**-0.5
LEVEL = 90.0
COST = pl.CostEstimate(flops=10**6, bytes_accessed=0, transcendentals=0)
VMEM = 60 << 20
BF16 = jnp.bfloat16
F32 = jnp.float32


def dot(a, b, ca=1, cb=0):
    return lax.dot_general(a, b, (((ca,), (cb,)), ((), ())), preferred_element_type=F32)


def whole(*shape):
    return pl.BlockSpec(shape, lambda *_: (0,) * len(shape))


def rows(n, width):
    return pl.BlockSpec((n, width), lambda i: (i, 0))


def cols(height, n):
    return pl.BlockSpec((height, n), lambda i: (0, i))


SMEM = pl.BlockSpec(memory_space=pltpu.SMEM)
ANY = pl.BlockSpec(memory_space=pl.ANY)


def normalise(v):
    centred = v - jnp.mean(v, axis=-1, keepdims=True)
    r = lax.rsqrt(jnp.mean(centred * centred, axis=-1, keepdims=True) + 1e-05)
    return centred * r, r


def chain_ranges(len_s, meta, blocks):
    for b in range(blocks):
        meta[0, b] = blocks
        meta[1, b] = 0

    def chain(c, start):
        size = len_s[0, c]
        end = start + size

        @pl.when(size > 0)
        def _():
            first = start // BLOCK
            last = (end - 1) // BLOCK + 1

            def touch(b, _):
                meta[0, b] = jnp.minimum(meta[0, b], first)
                meta[1, b] = jnp.maximum(meta[1, b], last)
                return 0

            lax.fori_loop(first, last, touch, 0)

        return end

    meta[2, 0] = lax.fori_loop(0, len_s.shape[1], chain, 0)


def length_row(len_s):
    ids = lax.broadcasted_iota(jnp.int32, (1, CODES), 1)
    row = jnp.zeros((1, CODES), jnp.int32)
    for c in range(len_s.shape[1]):
        row = jnp.where(ids == c, len_s[0, c], row)
    return row.astype(F32)


def codes(i, chains, size, codek, codet):
    a = lax.broadcasted_iota(jnp.int32, (CODES, CODES), 0)
    b = lax.broadcasted_iota(jnp.int32, (CODES, CODES), 1)
    size_col = jnp.sum(jnp.where(a == b, size, 0.0), axis=1, keepdims=True)
    end_col = jnp.sum(jnp.where(b <= a, size, 0.0), axis=1, keepdims=True)
    end_row = jnp.sum(jnp.where(a <= b, size_col, 0.0), axis=0, keepdims=True)
    start_col, start_row = end_col - size_col, end_row - size
    ids_col = lax.broadcasted_iota(jnp.int32, (CODES, 1), 0)
    ids_row = lax.broadcasted_iota(jnp.int32, (1, CODES), 1)
    end_col = jnp.where(ids_col == chains, 1e9, end_col)
    end_row = jnp.where(ids_row == chains, 1e9, end_row)
    base = i * PREP
    slot = (base + lax.broadcasted_iota(jnp.int32, (CODES, PREP), 1)).astype(F32)
    codet[...] = jnp.where((slot >= start_col) & (slot < end_col), 1.0, 0.0).astype(BF16)
    slot = (base + lax.broadcasted_iota(jnp.int32, (PREP, CODES), 0)).astype(F32)
    codek[...] = jnp.where((slot >= start_row) & (slot < end_row), 0.0, -1e30).astype(BF16)


def head_norms(v):
    v = v.astype(F32)
    return jnp.sum((v * v).reshape(-1, HEAD_DIM, v.shape[1]), axis=1)


def project(g, hc, low, w, bias, vbias, qt, kt, vt, kr, vr, qn, kn):
    joined = dot(w, low, 1, 1)
    s = slice(g * hc, (g + 1) * hc)
    q = (joined[:hc] + bias[:hc]).astype(BF16)
    k = joined[hc : 2 * hc].astype(BF16)
    qt[s, :], kt[s, :] = q, k
    h = slice(g * hc // HEAD_DIM, (g + 1) * hc // HEAD_DIM)
    qn[h, :], kn[h, :] = head_norms(q), head_norms(k)
    vt[s, :] = (joined[2 * hc :] + bias[hc:]).astype(BF16)
    kv = dot(low, w[hc:], 1, 1)
    kr[:, s] = kv[:, :hc].astype(BF16)
    vr[:, s] = (kv[:, hc:] + vbias).astype(BF16)


def bias_columns(extra, which):
    parts = extra.shape[0] // 4 - 2
    row = lax.broadcasted_iota(jnp.int32, (extra.shape[0], PREP), 0)
    picked = (row == which) | (row == which + parts) | (row == which + 2 * parts)
    return dot(extra, jnp.where(picked, 1.0, 0.0).astype(BF16), 0, 0)


def bias_row(extra, which):
    parts = extra.shape[0] // 4 - 2
    row = lax.broadcasted_iota(jnp.int32, extra.shape, 0)
    picked = (row == which) | (row == which + parts) | (row == which + 2 * parts)
    return jnp.sum(jnp.where(picked, extra.astype(F32), 0.0), axis=0, keepdims=True)


def bias_rows(extra, count):
    return jnp.concatenate([bias_row(extra, n) for n in range(count)], axis=1)


def prep_own_kernel(
    hc, where, len_s, x, wn, extra, gain, shift, wo, wu, wd,
    qt, kt, vt, kr, vr, qn, kn, nl, codek, codet, meta, w, near, far, bias, size, sems,
):
    i = pl.program_id(0)
    m, n, h = wu.shape[0] // 4, wd.shape[0] // 8, wo.shape[0] // 2
    core, quarter = where[0], 2 * where[0] + where[1]
    plan = (
        (wu, quarter * m, m, near, 0),
        (wd, quarter * n, n, near, m),
        (wo, core * h, h, far, 0),
        (wd, 4 * n + core * 2 * n, 2 * n, far, h),
    )
    copies = [
        pltpu.make_async_copy(
            src.at[pl.ds(pl.multiple_of(first, 16), count), :], dst.at[pl.ds(at, count), :], sems.at[k]
        )
        for k, (src, first, count, dst, at) in enumerate(plan)
    ]

    @pl.when(i == 0)
    def _():
        for copy in copies:
            copy.start()
        chain_ranges(len_s, meta, meta.shape[1])
        for p in range(3):
            w[p * hc : (p + 1) * hc, :] = wn[p].T
        for n in range(2):
            bias[n * hc : (n + 1) * hc, :] = bias_columns(extra[...], wn.shape[1] // hc + n)
        size[...] = length_row(len_s)

    xhat, _ = normalise(x[...].astype(F32))
    low = (xhat * gain[...] + shift[...]).astype(BF16)
    nl[...] = low
    project(0, hc, low, w[...], bias, bias_row(extra[...], wn.shape[1] // hc + 1), qt, kt, vt, kr, vr, qn, kn)
    codes(i, len_s.shape[1], size[...], codek, codet)

    @pl.when(i == pl.num_programs(0) - 1)
    def _():
        for copy in copies:
            copy.wait()


def projected(hidden, slots):
    t = jax.ShapeDtypeStruct((hidden, slots), BF16)
    r = jax.ShapeDtypeStruct((slots, hidden), BF16)
    n = jax.ShapeDtypeStruct((hidden // HEAD_DIM, slots), F32)
    specs = [cols(hidden, PREP)] * 3 + [rows(PREP, hidden)] * 2 + [cols(hidden // HEAD_DIM, PREP)] * 2
    return specs, [t, t, t, r, r, n, n]


def prep_own(where, tokens, lengths, w, extra, gain, shift, wo, wu, wd):
    slots, width = tokens.shape
    hc = w.shape[2]
    blocks = slots // BLOCK
    specs, shapes = projected(hc, slots)
    return pl.pallas_call(
        functools.partial(prep_own_kernel, hc),
        grid=(slots // PREP,),
        in_specs=[
            SMEM,
            SMEM,
            rows(PREP, width),
            whole(*w.shape),
            whole(*extra.shape),
            whole(1, width),
            whole(1, width),
            ANY,
            ANY,
            ANY,
        ],
        out_specs=specs + [rows(PREP, width), rows(PREP, CODES), cols(CODES, PREP), SMEM, whole(3 * hc, width)]
        + [whole(wu.shape[0] // 4 + wd.shape[0] // 8, width), whole(wo.shape[0] // 2 + wd.shape[0] // 4, width)],
        out_shape=shapes
        + [
            jax.ShapeDtypeStruct((slots, width), BF16),
            jax.ShapeDtypeStruct((slots, CODES), BF16),
            jax.ShapeDtypeStruct((CODES, slots), BF16),
            jax.ShapeDtypeStruct((3, blocks), jnp.int32),
            jax.ShapeDtypeStruct((3 * hc, width), BF16),
            jax.ShapeDtypeStruct((wu.shape[0] // 4 + wd.shape[0] // 8, width), BF16),
            jax.ShapeDtypeStruct((wo.shape[0] // 2 + wd.shape[0] // 4, width), BF16),
        ],
        scratch_shapes=[
            pltpu.VMEM((2 * hc, PREP), F32),
            pltpu.VMEM((1, CODES), F32),
            pltpu.SemaphoreType.DMA((4,)),
        ],
        compiler_params=pltpu.CompilerParams(vmem_limit_bytes=VMEM),
        cost_estimate=COST,
        name="prep_own",
    )(where, lengths, tokens, w, extra, gain, shift, wo, wu, wd)


def copy_rows(dst, first, part):
    dst[pl.ds(pl.multiple_of(first, 16), part.shape[0]), :] = part


def prep_others_kernel(others, hc, core_s, nl, mine, theirs, qt, kt, vt, kr, vr, qn, kn, w, ub, bias):
    half, width = w.shape[2] // 2, w.shape[2]
    extras = [mine[g, 3 * half :, :] for g in range(others)]
    first = width // hc

    @pl.when(pl.program_id(0) == 0)
    def _():
        for g in range(others):
            for p in range(3):
                for which, part in ((core_s[0], mine), (1 - core_s[0], theirs)):
                    at = pl.ds(pl.multiple_of(which * half, 128), half)
                    w[g, p * hc : (p + 1) * hc, at] = part[g, p * half : (p + 1) * half, :].T
            for n in range(2):
                bias[g, n * hc : (n + 1) * hc, :] = bias_columns(extras[g], first + n)
            ub[g] = bias_rows(extras[g], first)

    low = nl[...]
    for g in range(others):
        project(g, hc, low, w[g], bias.at[g], bias_row(extras[g], first + 1), qt, kt, vt, kr, vr, qn, kn)


def prep_others(core, nl, mine, theirs):
    slots, width = nl.shape
    others, _, hc = mine.shape
    specs, shapes = projected(others * hc, slots)
    return pl.pallas_call(
        functools.partial(prep_others_kernel, others, hc),
        grid=(slots // PREP,),
        in_specs=[
            SMEM,
            rows(PREP, width),
            whole(*mine.shape),
            whole(*theirs.shape),
        ],
        out_specs=specs + [whole(others, 3 * hc, width), whole(others, 1, width)],
        out_shape=shapes
        + [
            jax.ShapeDtypeStruct((others, 3 * hc, width), BF16),
            jax.ShapeDtypeStruct((others, 1, width), F32),
        ],
        scratch_shapes=[pltpu.VMEM((others, 2 * hc, PREP), F32)],
        compiler_params=pltpu.CompilerParams(vmem_limit_bytes=VMEM),
        cost_estimate=COST,
        name="prep_others",
    )(core, nl, mine, theirs)


def padded(part, h):
    zero = jnp.zeros_like(part)
    return jnp.concatenate([part, zero] if h % 2 == 0 else [zero, part], axis=0)


def pair(h):
    return pl.ds(h // 2 * 2 * HEAD_DIM, 2 * HEAD_DIM)


def head(h):
    return pl.ds(h * HEAD_DIM, HEAD_DIM)


def block_range(meta, i, unit):
    low, high = meta[0, unit * i], meta[1, unit * i]
    for u in range(1, unit):
        low = jnp.minimum(low, meta[0, unit * i + u])
        high = jnp.maximum(high, meta[1, unit * i + u])
    return low, high


def attend_kernel(heads, keys, queries, ahead, meta, qt, codet, kr, codek, vt, qn, kn, ot, lse, acc, top, total):
    i = pl.program_id(0)
    acc[...] = jnp.zeros_like(acc)
    total[...] = jnp.zeros_like(total)
    unit = keys // BLOCK
    first, end = block_range(meta, i, queries // BLOCK)
    first, end = first // unit, (end + unit - 1) // unit
    longest = jnp.max(jnp.max(qn[...], axis=1, keepdims=True) * jnp.max(kn[...], axis=1, keepdims=True))
    small = longest * SCALE**2 <= LEVEL**2

    def step(j, level):
        js = pl.ds(pl.multiple_of(j * keys, keys), keys)
        scores, probs, decays = {}, {}, {}
        code_k, code_t = codek[js, :], codet[...]
        for t in range(heads + 2 * ahead):
            if t < heads:
                left = jnp.concatenate([kr[js, pair(t)], code_k], axis=1)
                right = jnp.concatenate([padded(qt[head(t), :], t), code_t], axis=0)
                scores[t] = dot(left, right)
            h = t - ahead
            if 0 <= h < heads:
                s = scores.pop(h)
                before = total[8 * h : 8 * h + 8, :]
                if level:
                    p = jnp.exp2(s * SCALE)
                else:
                    old = top[h : h + 1, :]
                    new = jnp.maximum(old, jnp.max(s, axis=0, keepdims=True))
                    top[h : h + 1, :] = new
                    p = jnp.exp2(s * SCALE - new * SCALE)
                    decays[h] = jnp.exp2((old - new) * SCALE)
                    before = before * decays[h]
                total[8 * h : 8 * h + 8, :] = before + jnp.sum(p.reshape(keys // 8, 8, queries), axis=0)
                probs[h] = p.astype(BF16)
            h = t - 2 * ahead
            if 0 <= h < heads:
                mixed = dot(vt[head(h), js], probs.pop(h))
                acc[head(h), :] = (acc[head(h), :] if level else acc[head(h), :] * decays.pop(h)) + mixed

    @pl.when(small)
    def _():
        top[...] = jnp.zeros_like(top)
        lax.fori_loop(first, end, lambda j, _: step(j, True) or 0, 0)

    @pl.when(jnp.logical_not(small))
    def _():
        top[...] = jnp.full_like(top, -1e38)
        lax.fori_loop(first, end, lambda j, _: step(j, False) or 0, 0)

    for h in range(heads):
        summed = jnp.sum(total[8 * h : 8 * h + 8, :], axis=0, keepdims=True)
        seen = summed > 0.0
        summed = jnp.where(seen, summed, 1.0)
        ot[head(h), :] = (acc[head(h), :] / summed).astype(BF16)
        lse[h : h + 1, :] = jnp.where(seen, top[h : h + 1, :] * SCALE + jnp.log2(summed), 0.0)


def attend(keys, queries, ahead, meta, qt, codet, kr, codek, vt, qn, kn):
    hidden, slots = qt.shape
    heads = hidden // HEAD_DIM
    return pl.pallas_call(
        functools.partial(attend_kernel, heads, keys, queries, ahead),
        grid=(slots // queries,),
        in_specs=[
            SMEM,
            cols(hidden, queries),
            cols(CODES, queries),
            whole(*kr.shape),
            whole(*codek.shape),
            whole(*vt.shape),
            cols(heads, queries),
            whole(*kn.shape),
        ],
        out_specs=[cols(hidden, queries), cols(heads, queries)],
        out_shape=[
            jax.ShapeDtypeStruct((hidden, slots), BF16),
            jax.ShapeDtypeStruct((heads, slots), F32),
        ],
        scratch_shapes=[
            pltpu.VMEM((hidden, queries), F32),
            pltpu.VMEM((heads, queries), F32),
            pltpu.VMEM((8 * heads, queries), F32),
        ],
        compiler_params=pltpu.CompilerParams(vmem_limit_bytes=VMEM),
        cost_estimate=COST,
        name="attend",
    )(meta, qt, codet, kr, codek, vt, qn, kn)


def gelu_parts(u):
    bell = jnp.exp2(u * u * (-0.5 * LOG2E))
    return 0.5 + 0.5 * lax.erf(u * 0.5**0.5), u * bell * (2.0 * math.pi) ** -0.5


def feed_kernel(
    groups, core_s, meta, x, cot, ot_own, ot_rest, wo_own, wu_own, wd_own, near0, near1, beside0, beside1, far0, far1, ob, ub_own, ub, db, gain, shift,
    out, gm_o, dt_own, dt_rest, delta_own, delta_rest, grads, sums, wo, wu, wd, g_up, g_down, g_out, s_up, s_rest,
):
    i = pl.program_id(0)

    @pl.when(i == 0)
    def _():
        g_up[...] = jnp.zeros_like(g_up)
        g_down[...] = jnp.zeros_like(g_down)
        g_out[...] = jnp.zeros_like(g_out)
        s_up[...] = jnp.zeros_like(s_up)
        s_rest[...] = jnp.zeros_like(s_rest)
        wo[0], wu[0], wd[0] = wo_own[...], wu_own[...], wd_own[...]
        core, side = core_s[0], core_s[1]
        for g in range(groups - 1):
            up, down, mixed = wu.at[g + 1], wd.at[g + 1], wo.at[g + 1]
            for which, near, beside, far in ((core, near0, beside0, far0), (1 - core, near1, beside1, far1)):
                n = down.shape[0] // 4
                copy_rows(mixed, which * (mixed.shape[0] // 2), far[g, : mixed.shape[0] // 2, :])
                copy_rows(down, 2 * n + which * n, far[g, mixed.shape[0] // 2 :, :])
                for turn, part in ((side, near), (1 - side, beside)):
                    at = 2 * which + turn
                    m = up.shape[0] // 4
                    copy_rows(up, at * m, part[g, :m, :])
                    copy_rows(down, at * (n // 2), part[g, m:, :])

    hc = wo.shape[1]
    hidden, width = groups * hc, wo.shape[2]
    source = x[...].astype(F32)
    o = jnp.concatenate([ot_own[...], ot_rest[...]], axis=0)
    w_out = wo[...].reshape(hidden, width)
    middle = source + dot(o, w_out, 0, 0) + ob[...]
    xhat, r = normalise(middle)
    low = (xhat * gain[...] + shift[...]).astype(BF16)
    slot = i * FEED + lax.broadcasted_iota(jnp.int32, (FEED, 1), 0)
    live = slot < meta[2, 0]
    grad = jnp.where(live, cot[...].astype(F32), 0.0)
    grad_low = grad.astype(BF16)
    ahead = 1
    ups, backs, actives, gus = {}, {}, {}, {}
    down, gnt = None, None
    for t in range(groups + 2 * ahead):
        if t < groups:
            ups[t] = dot(low, wu[t]) + (ub_own[...] if t == 0 else ub[t - 1])
            backs[t] = dot(grad_low, wd[t], 1, 1)
        g = t - ahead
        if 0 <= g < groups:
            u = ups.pop(g)
            cdf, bump = gelu_parts(u)
            actives[g] = (u * cdf).astype(BF16)
            gus[g] = (backs.pop(g) * (cdf + bump)).astype(BF16)
        g = t - 2 * ahead
        if 0 <= g < groups:
            a, gu = actives.pop(g), gus.pop(g)
            d1, d2 = dot(a, wd[g]), dot(gu, wu[g], 1, 1)
            down = d1 if down is None else down + d1
            gnt = d2 if gnt is None else gnt + d2
            if g == 0:
                g_up[...] += dot(low, gu, 0, 0)
                g_down[...] += dot(a, grad_low, 0, 0)
                s_up[...] += jnp.sum(gu.astype(F32).reshape(FEED // 8, 8, -1), axis=0)
    out[...] = jnp.where(live, middle + down + db[...], source).astype(BF16)
    e = gnt * gain[...]
    gm = grad + r * (e - jnp.mean(e, axis=-1, keepdims=True) - xhat * jnp.mean(e * xhat, axis=-1, keepdims=True))
    gml = gm.astype(BF16)
    gm_o[...] = jnp.where(live, gml, cot[...])
    d = dot(w_out, gml, 1, 1).astype(BF16)
    dt_own[...] = d[:hc]
    dt_rest[...] = d[hc:]
    inner = jnp.sum((d.astype(F32) * o.astype(F32)).reshape(hidden // HEAD_DIM, HEAD_DIM, FEED), axis=1)
    delta_own[...] = inner[: hc // HEAD_DIM]
    delta_rest[...] = inner[hc // HEAD_DIM :]
    g_out[...] += dot(o[:hc], gml)
    for n, v in enumerate((grad, gnt * xhat, gnt, gm)):
        s_rest[8 * n : 8 * n + 8, :] += jnp.sum(v.reshape(FEED // 8, 8, width), axis=0)

    @pl.when(i == pl.num_programs(0) - 1)
    def _():
        f = g_down.shape[0]
        grads[:hc, :] = g_out[...].astype(BF16)
        grads[hc : hc + width, :] = g_up[...].astype(BF16)
        grads[hc + width :, :] = g_down[...].astype(BF16)
        for n in range(4):
            sums[n : n + 1, :] = jnp.sum(s_rest[8 * n : 8 * n + 8, :], axis=0, keepdims=True)
        sums[4:5, :] = jnp.sum(s_up[...], axis=0, keepdims=True)
        sums[5:8, :] = jnp.zeros((3, width), F32)


def feed(core, meta, tokens, cotangent, ot_own, ot_rest, wo, wu, wd, pieces, ob, ub_own, ub, db, gain, shift):
    slots, width = tokens.shape
    hc = wo.shape[0]
    ffn = wu.shape[1]
    others = pieces[0].shape[0]
    groups = others + 1
    hr = others * hc
    vec = whole(1, width)
    t = lambda n, kind=BF16: jax.ShapeDtypeStruct((n, slots), kind)
    return pl.pallas_call(
        functools.partial(feed_kernel, groups),
        grid=(slots // FEED,),
        in_specs=[
            SMEM,
            SMEM,
            rows(FEED, width),
            rows(FEED, width),
            cols(hc, FEED),
            cols(hr, FEED),
            whole(*wo.shape),
            whole(*wu.shape),
            whole(*wd.shape),
            *(whole(*piece.shape) for piece in pieces),
            vec,
            whole(*ub_own.shape),
            whole(*ub.shape),
            vec,
            vec,
            vec,
        ],
        out_specs=[
            rows(FEED, width),
            rows(FEED, width),
            cols(hc, FEED),
            cols(hr, FEED),
            cols(hc // HEAD_DIM, FEED),
            cols(hr // HEAD_DIM, FEED),
            whole(hc + width + ffn, width),
            whole(8, width),
        ],
        out_shape=[
            jax.ShapeDtypeStruct((slots, width), BF16),
            jax.ShapeDtypeStruct((slots, width), BF16),
            t(hc),
            t(hr),
            t(hc // HEAD_DIM, F32),
            t(hr // HEAD_DIM, F32),
            jax.ShapeDtypeStruct((hc + width + ffn, width), BF16),
            jax.ShapeDtypeStruct((8, width), F32),
        ],
        scratch_shapes=[
            pltpu.VMEM((groups, hc, width), BF16),
            pltpu.VMEM((groups, width, ffn), BF16),
            pltpu.VMEM((groups, ffn, width), BF16),
            pltpu.VMEM((width, ffn), F32),
            pltpu.VMEM((ffn, width), F32),
            pltpu.VMEM((hc, width), F32),
            pltpu.VMEM((8, ffn), F32),
            pltpu.VMEM((32, width), F32),
        ],
        compiler_params=pltpu.CompilerParams(vmem_limit_bytes=VMEM),
        cost_estimate=COST,
        name="feed",
    )(core, meta, tokens, cotangent, ot_own, ot_rest, wo, wu, wd, *pieces, ob, ub_own, ub, db, gain, shift)


def reverse_pass(heads, keys, ahead, meta, kr, vr, kt, qt, dt, codek, codet, lse, delta, dqs, dks, dvs):
    dqs[...] = jnp.zeros_like(dqs)
    dks[...] = jnp.zeros_like(dks)
    dvs[...] = jnp.zeros_like(dvs)
    unit = keys // BLOCK

    def column(j, _):
        js = pl.ds(pl.multiple_of(j * keys, keys), keys)

        def step(i, _):
            qs = pl.ds(pl.multiple_of(i * BLOCK, BLOCK), BLOCK)
            scores, backs, grads, probs = {}, {}, {}, {}
            code_k, code_t = codek[js, :], codet[:, qs]
            for t in range(heads + 2 * ahead):
                if t < heads:
                    left = jnp.concatenate([kr[js, pair(t)], code_k], axis=1)
                    right = jnp.concatenate([padded(qt[head(t), qs], t), code_t], axis=0)
                    scores[t] = dot(left, right)
                    backs[t] = dot(vr[js, pair(t)], padded(dt[head(t), qs], t))
                h = t - ahead
                if 0 <= h < heads:
                    p = jnp.exp2(scores.pop(h) * SCALE - lse[h : h + 1, qs])
                    grads[h] = (p * (backs.pop(h) - delta[h : h + 1, qs])).astype(BF16)
                    probs[h] = p.astype(BF16)
                h = t - 2 * ahead
                if 0 <= h < heads:
                    ds, p = grads.pop(h), probs.pop(h)
                    dqs[head(h), qs] += dot(kt[head(h), js], ds)
                    dks[head(h), js] += dot(qt[head(h), qs], ds, 1, 1)
                    dvs[head(h), js] += dot(dt[head(h), qs], p, 1, 1)
            return 0

        lax.fori_loop(*block_range(meta, j, unit), step, 0)
        return 0

    lax.fori_loop(0, kr.shape[0] // keys, column, 0)


def reverse_kernel(heads, keys, ahead, *refs):
    dq, dk, dv, dqs, dks, dvs = refs[10:]
    reverse_pass(heads, keys, ahead, *refs[:10], dqs, dks, dvs)
    factor = HEAD_DIM**-0.5
    dq[...] = (dqs[...] * factor).astype(BF16)
    dk[...] = (dks[...] * factor).astype(BF16)
    dv[...] = dvs[...].astype(BF16)


def reverse_own_kernel(heads, keys, ahead, *refs):
    x, nl, w, early = refs[10:14]
    dq, dk, dv, late, sums, dqs, dks, dvs, s_rest = refs[14:]
    reverse_kernel(heads, keys, ahead, *refs[:10], dq, dk, dv, dqs, dks, dvs)
    hc = dq.shape[0]
    parts = (dq, dk, dv)
    ones = jnp.ones((8, dq.shape[1]), BF16)
    late[3 * hc :, :] = jnp.zeros((late.shape[0] - 3 * hc, late.shape[1]), BF16)
    late[3 * hc : 3 * hc + 8, :] = early[...].astype(BF16)
    for n, d in enumerate(parts):
        late[n * hc : (n + 1) * hc, :] = dot(d[...], nl[...]).astype(BF16)
        if n != 1:
            late[3 * hc + 8 : 3 * hc + 9, n // 2 * hc : (n // 2 + 1) * hc] = dot(ones, d[...], 1, 1)[:1].astype(BF16)
    s_rest[...] = jnp.zeros_like(s_rest)

    def block(i, _):
        qs = pl.ds(pl.multiple_of(i * LAST, LAST), LAST)
        gn = dot(jnp.concatenate([d[:, qs] for d in parts], axis=0), w[...], 0, 0)
        xhat, _ = normalise(x[qs, :].astype(F32))
        for n, v in enumerate((gn * xhat, gn)):
            s_rest[8 * n : 8 * n + 8, :] += jnp.sum(v.reshape(LAST // 8, 8, -1), axis=0)
        return 0

    lax.fori_loop(0, x.shape[0] // LAST, block, 0)
    for n in range(2):
        sums[n : n + 1, :] = jnp.sum(s_rest[8 * n : 8 * n + 8, :], axis=0, keepdims=True)


def reverse(keys, ahead, meta, kr, vr, kt, qt, dt, codek, codet, lse, delta, own=None, late=0):
    hidden, slots = qt.shape
    heads = hidden // HEAD_DIM
    vm = pl.BlockSpec(memory_space=pltpu.VMEM)
    t = jax.ShapeDtypeStruct((hidden, slots), BF16)
    shapes = [t, t, t]
    scratch = [pltpu.VMEM((hidden, slots), F32)] * 3
    extra = ()
    if own is not None:
        extra = own
        width = own[0].shape[1]
        shapes += [
            jax.ShapeDtypeStruct((late, width), BF16),
            jax.ShapeDtypeStruct((2, width), F32),
        ]
        scratch += [pltpu.VMEM((16, width), F32)]
    return pl.pallas_call(
        functools.partial(reverse_kernel if own is None else reverse_own_kernel, heads, keys, ahead),
        in_specs=[SMEM] + [vm] * (9 + len(extra)),
        out_specs=[vm] * len(shapes),
        out_shape=shapes,
        scratch_shapes=scratch,
        compiler_params=pltpu.CompilerParams(vmem_limit_bytes=VMEM),
        cost_estimate=COST,
        name="reverse",
    )(meta, kr, vr, kt, qt, dt, codek, codet, lse, delta, *extra)


def finish_kernel(share, x, gm, q0, k0, v0, q1, k1, v1, w0, w1, gain, grads, out, *shards):
    *shards, joined = shards
    i = pl.program_id(0)
    @pl.when(i == 0)
    def _():
        chunk = joined.shape[0] // grads.shape[0]
        for c in range(grads.shape[0]):
            joined[c * chunk : (c + 1) * chunk, :] = grads[c, :chunk, :]

    first = 0
    for shard in shards:
        n = shard.shape[0]
        at = pl.ds(pl.multiple_of(first + i * n, 16), n)
        shard[...] = joined[at, :].astype(F32) * share
        first += n * pl.num_programs(0)
    hc, width = w0.shape[0] // 3, w0.shape[1]
    others = w1.shape[0]
    gn = dot(jnp.concatenate([q0[...], k0[...], v0[...]], axis=0), w0[...], 0, 0)
    for n, d in enumerate((q1, k1, v1)):
        gn += dot(d[...], w1[:, n * hc : (n + 1) * hc, :].reshape(others * hc, width), 0, 0)
    xhat, r = normalise(x[...].astype(F32))
    e = gn * gain[...]
    inner = r * (e - jnp.mean(e, axis=-1, keepdims=True) - xhat * jnp.mean(e * xhat, axis=-1, keepdims=True))
    out[...] = (gm[...].astype(F32) + inner).astype(BF16)


def finish(share, tokens, gm, own, rest, w0, w1, gain, grads, sizes):
    slots, width = tokens.shape
    steps = slots // LAST
    hc = own[0].shape[0]
    hr = rest[0].shape[0]
    return pl.pallas_call(
        functools.partial(finish_kernel, share),
        grid=(slots // LAST,),
        in_specs=[rows(LAST, width), rows(LAST, width)]
        + [cols(hc, LAST)] * 3
        + [cols(hr, LAST)] * 3
        + [whole(*w0.shape), whole(*w1.shape), whole(1, width), whole(*grads.shape)],
        out_specs=[rows(LAST, width)] + [rows(n // steps, width) for n in sizes],
        out_shape=[jax.ShapeDtypeStruct((slots, width), BF16)]
        + [jax.ShapeDtypeStruct((n, width), F32) for n in sizes],
        scratch_shapes=[pltpu.VMEM((sum(sizes), width), BF16)],
        compiler_params=pltpu.CompilerParams(vmem_limit_bytes=VMEM),
        cost_estimate=COST,
        name="finish",
    )(tokens, gm, *own, *rest, w0, w1, gain, grads)


def last_kernel(share, late, *refs):
    *norms, gw, bias = refs[:-8]
    *sums, joined = refs[-8:]
    hc = bias.shape[1]
    packs, n = late.shape[0], late.shape[1]
    for c in range(packs):
        joined[c * n : (c + 1) * n, :] = late[c]
    for p in range(3):
        gw[p] = joined[p * hc : (p + 1) * hc, :].astype(F32).T * share
    tail = joined[3 * hc : 3 * hc + 16, :].astype(F32) * share
    bias[0:1, :] = tail[8:9, :hc]
    bias[1:2, :] = tail[8:9, hc : 2 * hc]
    for k in range(5):
        sums[k][...] = tail[k : k + 1]
    total = sum(norm[...] for norm in norms[1:]) + norms[0][...]
    for k in range(2):
        sums[5 + k][...] = total[k : k + 1] * share


def last(share, late, norms, hc):
    packs, n, width = late.shape
    vm = pl.BlockSpec(memory_space=pltpu.VMEM)
    return pl.pallas_call(
        functools.partial(last_kernel, share),
        in_specs=[vm] * (1 + len(norms)),
        out_specs=[vm] * 9,
        out_shape=[
            jax.ShapeDtypeStruct((3, width, hc), F32),
            jax.ShapeDtypeStruct((2, hc), F32),
        ]
        + [jax.ShapeDtypeStruct((1, width), F32)] * 7,
        scratch_shapes=[pltpu.VMEM((packs * n, width), BF16)],
        compiler_params=pltpu.CompilerParams(vmem_limit_bytes=VMEM),
        name="last",
    )(late, *norms)


def around(v, axis, k):
    n = lax.axis_size(axis)
    return lax.ppermute(v, axis, [(t, (t - k) % n) for t in range(n)])


def swapped(v, bit):
    return lax.ppermute(v, "dp", [(d, d ^ bit) for d in range(lax.axis_size("dp"))])


def summed_chunk(v):
    packs = lax.axis_size("dp")
    parts = lax.all_to_all(v, "dp", 0, 0, tiled=True)
    return jnp.sum(parts.reshape(packs, -1, v.shape[1]).astype(F32), axis=0).astype(v.dtype)


def spread(v):
    return jnp.broadcast_to(v[None], (lax.axis_size("dp"), *v.shape))


def three_parts(v):
    high = lax.reduce_precision(v, 8, 7)
    mid = lax.reduce_precision(v - high, 8, 7)
    return jnp.stack([high, mid, v - high - mid]).astype(BF16)


def body(
    tokens, lengths, cotangent, qkv_weight, qv_bias, out_weight, out_bias, up_weight, up_bias,
    down_weight, down_bias, first_gain, first_shift, second_gain, second_shift,
):
    groups, packs = lax.axis_size("tensor"), lax.axis_size("dp")
    width, _, hc = qkv_weight.shape
    ffn = up_weight.shape[1]
    share = 1.0 / packs
    core = lax.axis_index("dp") % 2
    side = lax.axis_index("dp") // 2 % 2
    where = jnp.stack([core, side]).astype(jnp.int32)
    row = lambda v: v.reshape(1, -1)
    halved = lambda v, dim: lax.dynamic_slice_in_dim(v, core * (v.shape[dim] // 2), v.shape[dim] // 2, dim)
    turns = range(1, groups)
    local_qkv = jnp.transpose(qkv_weight, (1, 0, 2))
    biases = jnp.concatenate([up_bias.reshape(-1, hc), qv_bias])
    count = biases.shape[0]
    extra = jnp.pad(three_parts(biases).reshape(3 * count, hc), ((0, count + 8), (0, 0)))
    qkv_half = jnp.concatenate([halved(local_qkv, 1).reshape(-1, hc), extra])
    qkv_mine = [around(qkv_half, "tensor", k) for k in turns]
    qt0, kt0, vt0, kr0, vr0, qn0, kn0, nl, codek, codet, meta, wqkv0, near, far = prep_own(
        where, tokens, lengths, local_qkv, extra, row(first_gain), row(first_shift), out_weight, up_weight, down_weight
    )
    nl, near, *qkv_mine = lax.optimization_barrier((nl, near, *qkv_mine))
    near = [around(near, "tensor", k) for k in turns]
    qkv_mine = jnp.stack(qkv_mine)
    qkv_theirs = swapped(qkv_mine, 1)
    ot0, lse0 = attend(2 * BLOCK, OWNQ, 1, meta, qt0, codet, kr0, codek, vt0, qn0, kn0)
    ot0, qkv_theirs, far = lax.optimization_barrier((ot0, qkv_theirs, far))
    far = [around(far, "tensor", k) for k in turns]
    qt1, kt1, vt1, kr1, vr1, qn1, kn1, wqkv1, ub = prep_others(where, nl, qkv_mine, qkv_theirs)
    kr1, *near = lax.optimization_barrier((kr1, *near))
    near = jnp.stack(near)
    beside = swapped(near, 2)
    ot1, lse1 = attend(BLOCK, BLOCK, 3, meta, qt1, codet, kr1, codek, vt1, qn1, kn1)
    ot1, near, beside, *far = lax.optimization_barrier((ot1, near, beside, *far))
    pieces = [near, beside, jnp.stack(far)]
    pieces = [v for piece in pieces for v in (piece, swapped(piece, 1))]
    out, gm, dt0, dt1, delta0, delta1, grads, sums = feed(
        where, meta, tokens, cotangent, ot0, ot1, out_weight, up_weight, down_weight, pieces,
        row(out_bias), row(up_bias), ub, row(down_bias), row(second_gain), row(second_shift),
    )
    grads = summed_chunk(grads)
    late_rows = -(-(3 * hc + 16) // (16 * packs)) * 16 * packs
    *own, late, norm_sums = reverse(
        2 * BLOCK, 1, meta, kr0, vr0, kt0, qt0, dt0, codek, codet, lse0, delta0,
        own=(tokens, nl, wqkv0, sums), late=late_rows,
    )
    norms = jnp.pad(norm_sums.astype(BF16), ((0, 14), (0, 0)))
    chunk = grads.shape[0]
    mixed = jnp.concatenate([spread(jnp.concatenate([grads, norms])), late.reshape(packs, -1, width)], axis=1)
    mixed, kr1 = lax.optimization_barrier((mixed, kr1))
    mixed = lax.all_to_all(mixed, "dp", 0, 0)
    rest = reverse(BLOCK, 2, meta, kr1, vr1, kt1, qt1, dt1, codek, codet, lse1, delta1)
    mixed, rest0 = lax.optimization_barrier((mixed, rest[0]))
    late = jnp.sum(mixed[:, chunk + 16 :].astype(F32), axis=0).astype(BF16)
    late = lax.all_to_all(spread(late), "dp", 0, 0)
    norms = jnp.sum(mixed[:, chunk : chunk + 8].astype(F32), axis=0)
    norms = [norms] + [around(norms, "tensor", k) for k in turns]
    grad_tokens, grad_out, grad_up, grad_down = finish(
        share, tokens, gm, own, [rest0, *rest[1:]], wqkv0, wqkv1, row(first_gain),
        mixed, (hc, width, ffn),
    )
    gw, gb, *vectors = last(share, late, norms, hc)
    sums = [v.reshape(-1) for v in vectors]
    norm_sums = sums[5:]
    return (
        out,
        grad_tokens,
        jnp.transpose(gw, (1, 0, 2)),
        gb,
        grad_out,
        sums[3],
        grad_up,
        sums[4],
        grad_down,
        sums[0],
        norm_sums[0],
        norm_sums[1],
        sums[1],
        sums[2],
    )


def solution(mesh):
    in_specs = (
        P("dp", None),
        P("dp", None),
        P("dp", None),
        P(None, None, "tensor"),
        P(None, "tensor"),
        P("tensor", None),
        P(),
        P(None, "tensor"),
        P("tensor"),
        P("tensor", None),
        P(),
        P(),
        P(),
        P(),
        P(),
    )
    out_specs = (
        P("dp", None),
        P("dp", None),
        P(None, None, "tensor"),
        P(None, "tensor"),
        P("tensor", None),
        P(),
        P(None, "tensor"),
        P("tensor"),
        P("tensor", None),
        P(),
        P(),
        P(),
        P(),
        P(),
    )
    return jax.shard_map(body, mesh=mesh, in_specs=in_specs, out_specs=out_specs, check_vma=False)
```

```python
import functools
import math

import jax
import jax.numpy as jnp
from jax import lax
from jax.experimental import pallas as pl
from jax.experimental.pallas import tpu as pltpu
from jax.sharding import PartitionSpec as P

HEAD_DIM = 64
BLOCK = 256
SUB = 128
PREP = 512
OWNQ = 512
FEED = 512
LAST = 512
CODES = 128
LOG2E = math.log2(math.e)
SCALE = LOG2E * HEAD_DIM**-0.5
LEVEL = 90.0
COST = pl.CostEstimate(flops=10**6, bytes_accessed=0, transcendentals=0)
VMEM = 60 << 20
BF16 = jnp.bfloat16
F32 = jnp.float32


def dot(a, b, ca=1, cb=0):
    return lax.dot_general(a, b, (((ca,), (cb,)), ((), ())), preferred_element_type=F32)


def whole(*shape):
    return pl.BlockSpec(shape, lambda *_: (0,) * len(shape))


def rows(n, width):
    return pl.BlockSpec((n, width), lambda i: (i, 0))


def cols(height, n):
    return pl.BlockSpec((height, n), lambda i: (0, i))


SMEM = pl.BlockSpec(memory_space=pltpu.SMEM)
ANY = pl.BlockSpec(memory_space=pl.ANY)


def normalise(v):
    centred = v - jnp.mean(v, axis=-1, keepdims=True)
    r = lax.rsqrt(jnp.mean(centred * centred, axis=-1, keepdims=True) + 1e-05)
    return centred * r, r


def chain_ranges(len_s, meta, blocks):
    for b in range(blocks):
        meta[0, b] = blocks * BLOCK // SUB
        meta[1, b] = 0

    def chain(c, start):
        size = len_s[0, c]
        end = start + size

        @pl.when(size > 0)
        def _():
            first = start // SUB
            last = (end - 1) // SUB + 1

            def touch(b, _):
                meta[0, b] = jnp.minimum(meta[0, b], first)
                meta[1, b] = jnp.maximum(meta[1, b], last)
                return 0

            lax.fori_loop(start // BLOCK, (end - 1) // BLOCK + 1, touch, 0)

        return end

    meta[2, 0] = lax.fori_loop(0, len_s.shape[1], chain, 0)


def length_row(len_s):
    ids = lax.broadcasted_iota(jnp.int32, (1, CODES), 1)
    row = jnp.zeros((1, CODES), jnp.int32)
    for c in range(len_s.shape[1]):
        row = jnp.where(ids == c, len_s[0, c], row)
    return row.astype(F32)


def codes(i, chains, size, codek, codet):
    a = lax.broadcasted_iota(jnp.int32, (CODES, CODES), 0)
    b = lax.broadcasted_iota(jnp.int32, (CODES, CODES), 1)
    size_col = jnp.sum(jnp.where(a == b, size, 0.0), axis=1, keepdims=True)
    end_col = jnp.sum(jnp.where(b <= a, size, 0.0), axis=1, keepdims=True)
    end_row = jnp.sum(jnp.where(a <= b, size_col, 0.0), axis=0, keepdims=True)
    start_col, start_row = end_col - size_col, end_row - size
    ids_col = lax.broadcasted_iota(jnp.int32, (CODES, 1), 0)
    ids_row = lax.broadcasted_iota(jnp.int32, (1, CODES), 1)
    end_col = jnp.where(ids_col == chains, 1e9, end_col)
    end_row = jnp.where(ids_row == chains, 1e9, end_row)
    base = i * PREP
    slot = (base + lax.broadcasted_iota(jnp.int32, (CODES, PREP), 1)).astype(F32)
    codet[...] = jnp.where((slot >= start_col) & (slot < end_col), 1.0, 0.0).astype(BF16)
    slot = (base + lax.broadcasted_iota(jnp.int32, (PREP, CODES), 0)).astype(F32)
    codek[...] = jnp.where((slot >= start_row) & (slot < end_row), 0.0, -1e30).astype(BF16)


def head_norms(v):
    v = v.astype(F32)
    return jnp.sum((v * v).reshape(-1, HEAD_DIM, v.shape[1]), axis=1)


def project(g, hc, low, w, bias, vbias, qt, kt, vt, kr, vr, qn, kn):
    joined = dot(w, low, 1, 1)
    s = slice(g * hc, (g + 1) * hc)
    q = (joined[:hc] + bias[:hc]).astype(BF16)
    k = joined[hc : 2 * hc].astype(BF16)
    qt[s, :], kt[s, :] = q, k
    h = slice(g * hc // HEAD_DIM, (g + 1) * hc // HEAD_DIM)
    qn[h, :], kn[h, :] = head_norms(q), head_norms(k)
    vt[s, :] = (joined[2 * hc :] + bias[hc:]).astype(BF16)
    kv = dot(low, w[hc:], 1, 1)
    kr[:, s] = kv[:, :hc].astype(BF16)
    vr[:, s] = (kv[:, hc:] + vbias).astype(BF16)


def bias_columns(extra, which):
    parts = extra.shape[0] // 4 - 2
    row = lax.broadcasted_iota(jnp.int32, (extra.shape[0], PREP), 0)
    picked = (row == which) | (row == which + parts) | (row == which + 2 * parts)
    return dot(extra, jnp.where(picked, 1.0, 0.0).astype(BF16), 0, 0)


def bias_row(extra, which):
    parts = extra.shape[0] // 4 - 2
    row = lax.broadcasted_iota(jnp.int32, extra.shape, 0)
    picked = (row == which) | (row == which + parts) | (row == which + 2 * parts)
    return jnp.sum(jnp.where(picked, extra.astype(F32), 0.0), axis=0, keepdims=True)


def bias_rows(extra, count):
    return jnp.concatenate([bias_row(extra, n) for n in range(count)], axis=1)


def prep_own_kernel(
    hc, where, len_s, x, wn, extra, gain, shift, wo, wu, wd,
    qt, kt, vt, kr, vr, qn, kn, nl, codek, codet, meta, w, near, far, bias, size, sems,
):
    i = pl.program_id(0)
    m, n, h = wu.shape[0] // 4, wd.shape[0] // 8, wo.shape[0] // 2
    core, quarter = where[0], 2 * where[0] + where[1]
    plan = (
        (wu, quarter * m, m, near, 0),
        (wd, quarter * n, n, near, m),
        (wo, core * h, h, far, 0),
        (wd, 4 * n + core * 2 * n, 2 * n, far, h),
    )
    copies = [
        pltpu.make_async_copy(
            src.at[pl.ds(pl.multiple_of(first, 16), count), :], dst.at[pl.ds(at, count), :], sems.at[k]
        )
        for k, (src, first, count, dst, at) in enumerate(plan)
    ]

    @pl.when(i == 0)
    def _():
        for copy in copies:
            copy.start()
        chain_ranges(len_s, meta, meta.shape[1])
        for p in range(3):
            w[p * hc : (p + 1) * hc, :] = wn[p].T
        for n in range(2):
            bias[n * hc : (n + 1) * hc, :] = bias_columns(extra[...], wn.shape[1] // hc + n)
        size[...] = length_row(len_s)

    xhat, _ = normalise(x[...].astype(F32))
    low = (xhat * gain[...] + shift[...]).astype(BF16)
    nl[...] = low
    project(0, hc, low, w[...], bias, bias_row(extra[...], wn.shape[1] // hc + 1), qt, kt, vt, kr, vr, qn, kn)
    codes(i, len_s.shape[1], size[...], codek, codet)

    @pl.when(i == pl.num_programs(0) - 1)
    def _():
        for copy in copies:
            copy.wait()


def projected(hidden, slots):
    t = jax.ShapeDtypeStruct((hidden, slots), BF16)
    r = jax.ShapeDtypeStruct((slots, hidden), BF16)
    n = jax.ShapeDtypeStruct((hidden // HEAD_DIM, slots), F32)
    specs = [cols(hidden, PREP)] * 3 + [rows(PREP, hidden)] * 2 + [cols(hidden // HEAD_DIM, PREP)] * 2
    return specs, [t, t, t, r, r, n, n]


def prep_own(where, tokens, lengths, w, extra, gain, shift, wo, wu, wd):
    slots, width = tokens.shape
    hc = w.shape[2]
    blocks = slots // BLOCK
    specs, shapes = projected(hc, slots)
    return pl.pallas_call(
        functools.partial(prep_own_kernel, hc),
        grid=(slots // PREP,),
        in_specs=[
            SMEM,
            SMEM,
            rows(PREP, width),
            whole(*w.shape),
            whole(*extra.shape),
            whole(1, width),
            whole(1, width),
            ANY,
            ANY,
            ANY,
        ],
        out_specs=specs + [rows(PREP, width), rows(PREP, CODES), cols(CODES, PREP), SMEM, whole(3 * hc, width)]
        + [whole(wu.shape[0] // 4 + wd.shape[0] // 8, width), whole(wo.shape[0] // 2 + wd.shape[0] // 4, width)],
        out_shape=shapes
        + [
            jax.ShapeDtypeStruct((slots, width), BF16),
            jax.ShapeDtypeStruct((slots, CODES), BF16),
            jax.ShapeDtypeStruct((CODES, slots), BF16),
            jax.ShapeDtypeStruct((3, blocks), jnp.int32),
            jax.ShapeDtypeStruct((3 * hc, width), BF16),
            jax.ShapeDtypeStruct((wu.shape[0] // 4 + wd.shape[0] // 8, width), BF16),
            jax.ShapeDtypeStruct((wo.shape[0] // 2 + wd.shape[0] // 4, width), BF16),
        ],
        scratch_shapes=[
            pltpu.VMEM((2 * hc, PREP), F32),
            pltpu.VMEM((1, CODES), F32),
            pltpu.SemaphoreType.DMA((4,)),
        ],
        compiler_params=pltpu.CompilerParams(vmem_limit_bytes=VMEM),
        cost_estimate=COST,
        name="prep_own",
    )(where, lengths, tokens, w, extra, gain, shift, wo, wu, wd)


def copy_rows(dst, first, part):
    dst[pl.ds(pl.multiple_of(first, 16), part.shape[0]), :] = part


def prep_others_kernel(others, hc, where, nl, near0, near1, beside0, beside1, qt, kt, vt, kr, vr, qn, kn, w, ub, bias):
    quarter, width = w.shape[2] // 4, w.shape[2]
    extras = [near0[g, 3 * quarter :, :] for g in range(others)]
    first = width // hc

    @pl.when(pl.program_id(0) == 0)
    def _():
        for g in range(others):
            for p in range(3):
                for flip_core, flip_side, part in ((0, 0, near0), (1, 0, near1), (0, 1, beside0), (1, 1, beside1)):
                    core = where[0] + flip_core - 2 * flip_core * where[0]
                    side = where[1] + flip_side - 2 * flip_side * where[1]
                    at = pl.ds(pl.multiple_of((2 * core + side) * quarter, 128), quarter)
                    w[g, p * hc : (p + 1) * hc, at] = part[g, p * quarter : (p + 1) * quarter, :].T
            for n in range(2):
                bias[g, n * hc : (n + 1) * hc, :] = bias_columns(extras[g], first + n)
            ub[g] = bias_rows(extras[g], first)

    low = nl[...]
    for g in range(others):
        project(g, hc, low, w[g], bias.at[g], bias_row(extras[g], first + 1), qt, kt, vt, kr, vr, qn, kn)


def prep_others(nl, where, parts):
    slots, width = nl.shape
    others, _, hc = parts[0].shape
    specs, shapes = projected(others * hc, slots)
    return pl.pallas_call(
        functools.partial(prep_others_kernel, others, hc),
        grid=(slots // PREP,),
        in_specs=[
            SMEM,
            rows(PREP, width),
            *(whole(*part.shape) for part in parts),
        ],
        out_specs=specs + [whole(others, 3 * hc, width), whole(others, 1, width)],
        out_shape=shapes
        + [
            jax.ShapeDtypeStruct((others, 3 * hc, width), BF16),
            jax.ShapeDtypeStruct((others, 1, width), F32),
        ],
        scratch_shapes=[pltpu.VMEM((others, 2 * hc, PREP), F32)],
        compiler_params=pltpu.CompilerParams(vmem_limit_bytes=VMEM),
        cost_estimate=COST,
        name="prep_others",
    )(where, nl, *parts)


def padded(part, h):
    zero = jnp.zeros_like(part)
    return jnp.concatenate([part, zero] if h % 2 == 0 else [zero, part], axis=0)


def pair(h):
    return pl.ds(h // 2 * 2 * HEAD_DIM, 2 * HEAD_DIM)


def head(h):
    return pl.ds(h * HEAD_DIM, HEAD_DIM)


def steps_over(meta, i, unit, size, slots):
    low, high = meta[0, unit * i], meta[1, unit * i]
    for u in range(1, unit):
        low = jnp.minimum(low, meta[0, unit * i + u])
        high = jnp.maximum(high, meta[1, unit * i + u])
    each = size // SUB
    count = jnp.maximum(high - low + each - 1, 0) // each
    return count, jnp.minimum(low, slots // SUB - count * each)


def step_slots(first, n, size):
    return pl.ds(pl.multiple_of((first + n * (size // SUB)) * SUB, SUB), size)


def attend_kernel(heads, keys, queries, ahead, meta, qt, codet, kr, codek, vt, qn, kn, ot, ot_low, lse, acc, top, total):
    i = pl.program_id(0)
    acc[...] = jnp.zeros_like(acc)
    total[...] = jnp.zeros_like(total)
    count, first = steps_over(meta, i, queries // BLOCK, keys, kr.shape[0])
    longest = jnp.max(jnp.max(qn[...], axis=1, keepdims=True) * jnp.max(kn[...], axis=1, keepdims=True))
    small = longest * SCALE**2 <= LEVEL**2

    def step(j, level):
        js = step_slots(first, j, keys)
        scores, probs, decays = {}, {}, {}
        code_k, code_t = codek[js, :], codet[...]
        for t in range(heads + 2 * ahead):
            if t < heads:
                left = jnp.concatenate([kr[js, pair(t)], code_k], axis=1)
                right = jnp.concatenate([padded(qt[head(t), :], t), code_t], axis=0)
                scores[t] = dot(left, right)
            h = t - ahead
            if 0 <= h < heads:
                s = scores.pop(h)
                before = total[8 * h : 8 * h + 8, :]
                if level:
                    p = jnp.exp2(s * SCALE)
                else:
                    old = top[h : h + 1, :]
                    new = jnp.maximum(old, jnp.max(s, axis=0, keepdims=True))
                    top[h : h + 1, :] = new
                    p = jnp.exp2(s * SCALE - new * SCALE)
                    decays[h] = jnp.exp2((old - new) * SCALE)
                    before = before * decays[h]
                total[8 * h : 8 * h + 8, :] = before + jnp.sum(p.reshape(keys // 8, 8, queries), axis=0)
                probs[h] = p.astype(BF16)
            h = t - 2 * ahead
            if 0 <= h < heads:
                mixed = dot(vt[head(h), js], probs.pop(h))
                acc[head(h), :] = (acc[head(h), :] if level else acc[head(h), :] * decays.pop(h)) + mixed

    @pl.when(small)
    def _():
        top[...] = jnp.zeros_like(top)
        lax.fori_loop(0, count, lambda j, _: step(j, True) or 0, 0)

    @pl.when(jnp.logical_not(small))
    def _():
        top[...] = jnp.full_like(top, -1e38)
        lax.fori_loop(0, count, lambda j, _: step(j, False) or 0, 0)

    slot = i * queries + lax.broadcasted_iota(jnp.int32, (1, queries), 1)
    live = slot < meta[2, 0]
    for h in range(heads):
        summed = jnp.sum(total[8 * h : 8 * h + 8, :], axis=0, keepdims=True)
        seen = summed > 0.0
        summed = jnp.where(seen, summed, 1.0)
        mixture = acc[head(h), :] / summed
        high = mixture.astype(BF16)
        ot[head(h), :] = high
        ot_low[head(h), :] = (mixture - high.astype(F32)).astype(BF16)
        lse[h : h + 1, :] = jnp.where(live, top[h : h + 1, :] * SCALE + jnp.log2(summed), 1e30)


def attend(keys, queries, ahead, meta, qt, codet, kr, codek, vt, qn, kn):
    hidden, slots = qt.shape
    heads = hidden // HEAD_DIM
    return pl.pallas_call(
        functools.partial(attend_kernel, heads, keys, queries, ahead),
        grid=(slots // queries,),
        in_specs=[
            SMEM,
            cols(hidden, queries),
            cols(CODES, queries),
            whole(*kr.shape),
            whole(*codek.shape),
            whole(*vt.shape),
            cols(heads, queries),
            whole(*kn.shape),
        ],
        out_specs=[cols(hidden, queries), cols(hidden, queries), cols(heads, queries)],
        out_shape=[
            jax.ShapeDtypeStruct((hidden, slots), BF16),
            jax.ShapeDtypeStruct((hidden, slots), BF16),
            jax.ShapeDtypeStruct((heads, slots), F32),
        ],
        scratch_shapes=[
            pltpu.VMEM((hidden, queries), F32),
            pltpu.VMEM((heads, queries), F32),
            pltpu.VMEM((8 * heads, queries), F32),
        ],
        compiler_params=pltpu.CompilerParams(vmem_limit_bytes=VMEM),
        cost_estimate=COST,
        name="attend",
    )(meta, qt, codet, kr, codek, vt, qn, kn)


def gelu_parts(u):
    bell = jnp.exp2(u * u * (-0.5 * LOG2E))
    return 0.5 + 0.5 * lax.erf(u * 0.5**0.5), u * bell * (2.0 * math.pi) ** -0.5


def feed_kernel(
    groups, core_s, meta, x, cot, ot_own, ot_rest, low_own, low_rest, wo_own, wu_own, wd_own, near0, near1, beside0, beside1, far0, far1, ob, ub_own, ub, db, gain, shift,
    out, gm_o, dt_own, dt_rest, delta_own, delta_rest, grads, sums, wo, wu, wd, g_up, g_down, g_out, s_up, s_rest,
):
    i = pl.program_id(0)

    @pl.when(i == 0)
    def _():
        g_up[...] = jnp.zeros_like(g_up)
        g_down[...] = jnp.zeros_like(g_down)
        g_out[...] = jnp.zeros_like(g_out)
        s_up[...] = jnp.zeros_like(s_up)
        s_rest[...] = jnp.zeros_like(s_rest)
        wo[0], wu[0], wd[0] = wo_own[...], wu_own[...], wd_own[...]
        core, side = core_s[0], core_s[1]
        for g in range(groups - 1):
            up, down, mixed = wu.at[g + 1], wd.at[g + 1], wo.at[g + 1]
            for which, near, beside, far in ((core, near0, beside0, far0), (1 - core, near1, beside1, far1)):
                n = down.shape[0] // 4
                copy_rows(mixed, which * (mixed.shape[0] // 2), far[g, : mixed.shape[0] // 2, :])
                copy_rows(down, 2 * n + which * n, far[g, mixed.shape[0] // 2 :, :])
                for turn, part in ((side, near), (1 - side, beside)):
                    at = 2 * which + turn
                    m = up.shape[0] // 4
                    copy_rows(up, at * m, part[g, :m, :])
                    copy_rows(down, at * (n // 2), part[g, m:, :])

    hc = wo.shape[1]
    hidden, width = groups * hc, wo.shape[2]
    source = x[...].astype(F32)
    o = jnp.concatenate([ot_own[...], ot_rest[...]], axis=0)
    w_out = wo[...].reshape(hidden, width)
    middle = source + dot(o, w_out, 0, 0) + ob[...]
    xhat, r = normalise(middle)
    low = (xhat * gain[...] + shift[...]).astype(BF16)
    slot = i * FEED + lax.broadcasted_iota(jnp.int32, (FEED, 1), 0)
    live = slot < meta[2, 0]
    grad = jnp.where(live, cot[...].astype(F32), 0.0)
    grad_low = grad.astype(BF16)
    ahead = 1
    ups, backs, actives, gus = {}, {}, {}, {}
    down, gnt = None, None
    for t in range(groups + 2 * ahead):
        if t < groups:
            ups[t] = dot(low, wu[t]) + (ub_own[...] if t == 0 else ub[t - 1])
            backs[t] = dot(grad_low, wd[t], 1, 1)
        g = t - ahead
        if 0 <= g < groups:
            u = ups.pop(g)
            cdf, bump = gelu_parts(u)
            actives[g] = (u * cdf).astype(BF16)
            gus[g] = (backs.pop(g) * (cdf + bump)).astype(BF16)
        g = t - 2 * ahead
        if 0 <= g < groups:
            a, gu = actives.pop(g), gus.pop(g)
            d1, d2 = dot(a, wd[g]), dot(gu, wu[g], 1, 1)
            down = d1 if down is None else down + d1
            gnt = d2 if gnt is None else gnt + d2
            if g == 0:
                g_up[...] += dot(low, gu, 0, 0)
                g_down[...] += dot(a, grad_low, 0, 0)
                s_up[...] += jnp.sum(gu.astype(F32).reshape(FEED // 8, 8, -1), axis=0)
    out[...] = jnp.where(live, middle + down + db[...], source).astype(BF16)
    e = gnt * gain[...]
    gm = grad + r * (e - jnp.mean(e, axis=-1, keepdims=True) - xhat * jnp.mean(e * xhat, axis=-1, keepdims=True))
    gml = gm.astype(BF16)
    gm_o[...] = jnp.where(live, gml, cot[...])
    d = dot(w_out, gml, 1, 1).astype(BF16)
    dt_own[...] = d[:hc]
    dt_rest[...] = d[hc:]
    exact = o.astype(F32) + jnp.concatenate([low_own[...], low_rest[...]], axis=0).astype(F32)
    inner = jnp.sum((d.astype(F32) * exact).reshape(hidden // HEAD_DIM, HEAD_DIM, FEED), axis=1)
    delta_own[...] = inner[: hc // HEAD_DIM]
    delta_rest[...] = inner[hc // HEAD_DIM :]
    g_out[...] += dot(o[:hc], gml)
    for n, v in enumerate((grad, gnt * xhat, gnt, gm)):
        s_rest[8 * n : 8 * n + 8, :] += jnp.sum(v.reshape(FEED // 8, 8, width), axis=0)

    @pl.when(i == pl.num_programs(0) - 1)
    def _():
        f = g_down.shape[0]
        grads[:hc, :] = g_out[...].astype(BF16)
        grads[hc : hc + width, :] = g_up[...].astype(BF16)
        grads[hc + width :, :] = g_down[...].astype(BF16)
        for n in range(4):
            sums[n : n + 1, :] = jnp.sum(s_rest[8 * n : 8 * n + 8, :], axis=0, keepdims=True)
        sums[4:5, :] = jnp.sum(s_up[...], axis=0, keepdims=True)
        sums[5:8, :] = jnp.zeros((3, width), F32)


def feed(core, meta, tokens, cotangent, ot_own, ot_rest, low_own, low_rest, wo, wu, wd, pieces, ob, ub_own, ub, db, gain, shift):
    slots, width = tokens.shape
    hc = wo.shape[0]
    ffn = wu.shape[1]
    others = pieces[0].shape[0]
    groups = others + 1
    hr = others * hc
    vec = whole(1, width)
    t = lambda n, kind=BF16: jax.ShapeDtypeStruct((n, slots), kind)
    return pl.pallas_call(
        functools.partial(feed_kernel, groups),
        grid=(slots // FEED,),
        in_specs=[
            SMEM,
            SMEM,
            rows(FEED, width),
            rows(FEED, width),
            cols(hc, FEED),
            cols(hr, FEED),
            cols(hc, FEED),
            cols(hr, FEED),
            whole(*wo.shape),
            whole(*wu.shape),
            whole(*wd.shape),
            *(whole(*piece.shape) for piece in pieces),
            vec,
            whole(*ub_own.shape),
            whole(*ub.shape),
            vec,
            vec,
            vec,
        ],
        out_specs=[
            rows(FEED, width),
            rows(FEED, width),
            cols(hc, FEED),
            cols(hr, FEED),
            cols(hc // HEAD_DIM, FEED),
            cols(hr // HEAD_DIM, FEED),
            whole(hc + width + ffn, width),
            whole(8, width),
        ],
        out_shape=[
            jax.ShapeDtypeStruct((slots, width), BF16),
            jax.ShapeDtypeStruct((slots, width), BF16),
            t(hc),
            t(hr),
            t(hc // HEAD_DIM, F32),
            t(hr // HEAD_DIM, F32),
            jax.ShapeDtypeStruct((hc + width + ffn, width), BF16),
            jax.ShapeDtypeStruct((8, width), F32),
        ],
        scratch_shapes=[
            pltpu.VMEM((groups, hc, width), BF16),
            pltpu.VMEM((groups, width, ffn), BF16),
            pltpu.VMEM((groups, ffn, width), BF16),
            pltpu.VMEM((width, ffn), F32),
            pltpu.VMEM((ffn, width), F32),
            pltpu.VMEM((hc, width), F32),
            pltpu.VMEM((8, ffn), F32),
            pltpu.VMEM((32, width), F32),
        ],
        compiler_params=pltpu.CompilerParams(vmem_limit_bytes=VMEM),
        cost_estimate=COST,
        name="feed",
    )(core, meta, tokens, cotangent, ot_own, ot_rest, low_own, low_rest, wo, wu, wd, *pieces, ob, ub_own, ub, db, gain, shift)


def at_block(b, size=BLOCK):
    return pl.ds(pl.multiple_of(b * size, size), size)


def reverse_pass(
    heads, keys, ahead, meta, lse, delta, sources, held, outs, staged, sums, in_sems, out_sems, more=()
):
    kr, vr, codek, kt, qt, dt, codet = held
    dq, dk, dv = staged
    dqs, dks, dvs = sums
    blocks = kr.shape[0] // BLOCK
    unit = keys // BLOCK
    factor = HEAD_DIM**-0.5

    def fetches(b):
        where = [(at_block(b), slice(None))] * 3 + [(slice(None), at_block(b))] * 4
        return [
            pltpu.make_async_copy(src.at[w], dst.at[w], in_sems.at[n, b])
            for n, (src, dst, w) in enumerate(zip(sources, held, where))
        ]

    def send(n, b, size):
        w = (slice(None), at_block(b, size))
        return pltpu.make_async_copy(staged[n].at[w], outs[n].at[w], out_sems.at[n, b])

    def start(b, _):
        for copy in fetches(b):
            copy.start()
        return 0

    def arrive(b, _):
        for copy in fetches(b):
            copy.wait()
        return 0

    lax.fori_loop(0, blocks, start, 0)
    for copy in more:
        copy.start()
    dqs[...] = jnp.zeros_like(dqs)

    def column(j, state):
        ready, flushed = state
        js = at_block(j, keys)
        dks[...] = jnp.zeros_like(dks)
        dvs[...] = jnp.zeros_like(dvs)

        count, first = steps_over(meta, j, unit, BLOCK, kr.shape[0])

        def step(i, _):
            qs = step_slots(first, i, BLOCK)
            scores, backs, grads, probs = {}, {}, {}, {}
            code_k, code_t = codek[js, :], codet[:, qs]
            for t in range(heads + 2 * ahead):
                if t < heads:
                    left = jnp.concatenate([kr[js, pair(t)], code_k], axis=1)
                    right = jnp.concatenate([padded(qt[head(t), qs], t), code_t], axis=0)
                    scores[t] = dot(left, right)
                    backs[t] = dot(vr[js, pair(t)], padded(dt[head(t), qs], t))
                h = t - ahead
                if 0 <= h < heads:
                    p = jnp.exp2(scores.pop(h) * SCALE - lse[h : h + 1, qs])
                    grads[h] = (p * (backs.pop(h) - delta[h : h + 1, qs])).astype(BF16)
                    probs[h] = p.astype(BF16)
                h = t - 2 * ahead
                if 0 <= h < heads:
                    ds, p = grads.pop(h), probs.pop(h)
                    dqs[head(h), qs] += dot(kt[head(h), js], ds)
                    dks[head(h), :] += dot(qt[head(h), qs], ds, 1, 1)
                    dvs[head(h), :] += dot(dt[head(h), qs], p, 1, 1)
            return 0

        end = (first * SUB + count * BLOCK + BLOCK - 1) // BLOCK
        need = jnp.where(count > 0, jnp.maximum(end, (j + 1) * unit), 0)
        lax.fori_loop(ready, need, arrive, 0)
        lax.fori_loop(0, count, step, 0)
        dk[:, js] = (dks[...] * factor).astype(BF16)
        dv[:, js] = dvs[...].astype(BF16)
        send(1, j, keys).start()
        send(2, j, keys).start()

        def whole_row(b):
            return (b < blocks) & (meta[1, jnp.minimum(b, blocks - 1)] <= (j + 1) * (keys // SUB))

        def flush(b):
            dq[:, at_block(b)] = (dqs[:, at_block(b)] * factor).astype(BF16)
            send(0, b, BLOCK).start()
            return b + 1

        return jnp.maximum(ready, need), lax.while_loop(whole_row, flush, flushed)

    ready, _ = lax.fori_loop(0, blocks // unit, column, (jnp.int32(0), jnp.int32(0)))
    lax.fori_loop(ready, blocks, arrive, 0)

    def finish_sends():
        def sent(b, _):
            send(0, b, BLOCK).wait()
            return 0

        def sent_column(j, _):
            send(1, j, keys).wait()
            send(2, j, keys).wait()
            return 0

        lax.fori_loop(0, blocks, sent, 0)
        lax.fori_loop(0, blocks // unit, sent_column, 0)

    return finish_sends


def reverse_kernel(heads, keys, ahead, meta, lse, delta, *refs):
    sources, outs, held, staged, sums = refs[:7], refs[7:10], refs[10:17], refs[17:20], refs[20:23]
    reverse_pass(heads, keys, ahead, meta, lse, delta, sources, held, outs, staged, sums, *refs[23:])()


def reverse_own_kernel(heads, keys, ahead, meta, lse, delta, early, *refs):
    sources, others, outs, (late, norms) = refs[:7], refs[7:10], refs[10:13], refs[13:15]
    held, staged, sums = refs[15:22], refs[22:25], refs[25:28]
    in_sems, out_sems, x, nl, w, s_rest, sems = refs[28:]
    copies = [pltpu.make_async_copy(src, dst, sems.at[n]) for n, (src, dst) in enumerate(zip(others, (x, nl, w)))]
    finish_sends = reverse_pass(
        heads, keys, ahead, meta, lse, delta, sources, held, outs, staged, sums, in_sems, out_sems, copies
    )
    hc = staged[0].shape[0]
    ones = jnp.ones((8, x.shape[0]), BF16)
    late[3 * hc :, :] = jnp.zeros((late.shape[0] - 3 * hc, late.shape[1]), BF16)
    late[3 * hc : 3 * hc + 8, :] = early[...].astype(BF16)
    for copy in copies:
        copy.wait()
    for n, d in enumerate(staged):
        late[n * hc : (n + 1) * hc, :] = dot(d[...], nl[...]).astype(BF16)
        if n != 1:
            late[3 * hc + 8 : 3 * hc + 9, n // 2 * hc : (n // 2 + 1) * hc] = dot(ones, d[...], 1, 1)[:1].astype(BF16)
    s_rest[...] = jnp.zeros_like(s_rest)

    def block(i, _):
        qs = at_block(i, LAST)
        gn = dot(jnp.concatenate([d[:, qs] for d in staged], axis=0), w[...], 0, 0)
        xhat, _ = normalise(x[qs, :].astype(F32))
        for n, v in enumerate((gn * xhat, gn)):
            s_rest[8 * n : 8 * n + 8, :] += jnp.sum(v.reshape(LAST // 8, 8, -1), axis=0)
        return 0

    lax.fori_loop(0, x.shape[0] // LAST, block, 0)
    for n in range(2):
        norms[n : n + 1, :] = jnp.sum(s_rest[8 * n : 8 * n + 8, :], axis=0, keepdims=True)
    finish_sends()


def reverse(keys, ahead, meta, kr, vr, kt, qt, dt, codek, codet, lse, delta, own=None, late=0):
    hidden, slots = qt.shape
    heads = hidden // HEAD_DIM
    blocks = slots // BLOCK
    vm = pl.BlockSpec(memory_space=pltpu.VMEM)
    sources = (kr, vr, codek, kt, qt, dt, codet)
    shapes = [jax.ShapeDtypeStruct((hidden, slots), BF16)] * 3
    scratch = [pltpu.VMEM(v.shape, BF16) for v in sources] + [pltpu.VMEM((hidden, slots), BF16)] * 3
    scratch += [pltpu.VMEM((hidden, slots), F32)] + [pltpu.VMEM((hidden, keys), F32)] * 2
    scratch += [pltpu.SemaphoreType.DMA((7, blocks)), pltpu.SemaphoreType.DMA((3, blocks))]
    small, late_shapes = (lse, delta), []
    if own is not None:
        *others, early = own
        sources += tuple(others)
        small += (early,)
        width = early.shape[1]
        late_shapes = [jax.ShapeDtypeStruct((late, width), BF16), jax.ShapeDtypeStruct((2, width), F32)]
        scratch += [pltpu.VMEM(v.shape, BF16) for v in others]
        scratch += [pltpu.VMEM((16, width), F32), pltpu.SemaphoreType.DMA((3,))]
    return pl.pallas_call(
        functools.partial(reverse_kernel if own is None else reverse_own_kernel, heads, keys, ahead),
        in_specs=[SMEM] + [vm] * len(small) + [ANY] * len(sources),
        out_specs=[ANY] * 3 + [vm] * len(late_shapes),
        out_shape=shapes + late_shapes,
        scratch_shapes=scratch,
        compiler_params=pltpu.CompilerParams(vmem_limit_bytes=VMEM),
        cost_estimate=COST,
        name="reverse",
    )(meta, *small, *sources)


def finish_kernel(share, x, gm, q0, k0, v0, q1, k1, v1, w0, w1, gain, grads, out, *shards):
    *shards, joined = shards
    i = pl.program_id(0)
    @pl.when(i == 0)
    def _():
        chunk = joined.shape[0] // grads.shape[0]
        for c in range(grads.shape[0]):
            joined[c * chunk : (c + 1) * chunk, :] = grads[c, :chunk, :]

    first = 0
    for shard in shards:
        n = shard.shape[0]
        at = pl.ds(pl.multiple_of(first + i * n, 16), n)
        shard[...] = joined[at, :].astype(F32) * share
        first += n * pl.num_programs(0)
    hc, width = w0.shape[0] // 3, w0.shape[1]
    others = w1.shape[0]
    gn = dot(jnp.concatenate([q0[...], k0[...], v0[...]], axis=0), w0[...], 0, 0)
    for n, d in enumerate((q1, k1, v1)):
        gn += dot(d[...], w1[:, n * hc : (n + 1) * hc, :].reshape(others * hc, width), 0, 0)
    xhat, r = normalise(x[...].astype(F32))
    e = gn * gain[...]
    inner = r * (e - jnp.mean(e, axis=-1, keepdims=True) - xhat * jnp.mean(e * xhat, axis=-1, keepdims=True))
    out[...] = (gm[...].astype(F32) + inner).astype(BF16)


def finish(share, tokens, gm, own, rest, w0, w1, gain, grads, sizes):
    slots, width = tokens.shape
    steps = slots // LAST
    hc = own[0].shape[0]
    hr = rest[0].shape[0]
    return pl.pallas_call(
        functools.partial(finish_kernel, share),
        grid=(slots // LAST,),
        in_specs=[rows(LAST, width), rows(LAST, width)]
        + [cols(hc, LAST)] * 3
        + [cols(hr, LAST)] * 3
        + [whole(*w0.shape), whole(*w1.shape), whole(1, width), whole(*grads.shape)],
        out_specs=[rows(LAST, width)] + [rows(n // steps, width) for n in sizes],
        out_shape=[jax.ShapeDtypeStruct((slots, width), BF16)]
        + [jax.ShapeDtypeStruct((n, width), F32) for n in sizes],
        scratch_shapes=[pltpu.VMEM((sum(sizes), width), BF16)],
        compiler_params=pltpu.CompilerParams(vmem_limit_bytes=VMEM),
        cost_estimate=COST,
        name="finish",
    )(tokens, gm, *own, *rest, w0, w1, gain, grads)


def last_kernel(share, late, *refs):
    *norms, gw, bias = refs[:-8]
    *sums, joined = refs[-8:]
    hc = bias.shape[1]
    packs, n = late.shape[0], late.shape[1]
    for c in range(packs):
        joined[c * n : (c + 1) * n, :] = late[c]
    for p in range(3):
        gw[p] = joined[p * hc : (p + 1) * hc, :].astype(F32).T * share
    tail = joined[3 * hc : 3 * hc + 16, :].astype(F32) * share
    bias[0:1, :] = tail[8:9, :hc]
    bias[1:2, :] = tail[8:9, hc : 2 * hc]
    for k in range(5):
        sums[k][...] = tail[k : k + 1]
    total = sum(norm[...] for norm in norms[1:]) + norms[0][...]
    for k in range(2):
        sums[5 + k][...] = total[k : k + 1] * share


def last(share, late, norms, hc):
    packs, n, width = late.shape
    vm = pl.BlockSpec(memory_space=pltpu.VMEM)
    return pl.pallas_call(
        functools.partial(last_kernel, share),
        in_specs=[vm] * (1 + len(norms)),
        out_specs=[vm] * 9,
        out_shape=[
            jax.ShapeDtypeStruct((3, width, hc), F32),
            jax.ShapeDtypeStruct((2, hc), F32),
        ]
        + [jax.ShapeDtypeStruct((1, width), F32)] * 7,
        scratch_shapes=[pltpu.VMEM((packs * n, width), BF16)],
        compiler_params=pltpu.CompilerParams(vmem_limit_bytes=VMEM),
        name="last",
    )(late, *norms)


def around(v, axis, k):
    n = lax.axis_size(axis)
    return lax.ppermute(v, axis, [(t, (t - k) % n) for t in range(n)])


def swapped(v, bit):
    return lax.ppermute(v, "dp", [(d, d ^ bit) for d in range(lax.axis_size("dp"))])


def summed_chunk(v):
    packs = lax.axis_size("dp")
    parts = lax.all_to_all(v, "dp", 0, 0, tiled=True)
    return jnp.sum(parts.reshape(packs, -1, v.shape[1]).astype(F32), axis=0).astype(v.dtype)


def spread(v):
    return jnp.broadcast_to(v[None], (lax.axis_size("dp"), *v.shape))


def three_parts(v):
    high = lax.reduce_precision(v, 8, 7)
    mid = lax.reduce_precision(v - high, 8, 7)
    return jnp.stack([high, mid, v - high - mid]).astype(BF16)


def body(
    tokens, lengths, cotangent, qkv_weight, qv_bias, out_weight, out_bias, up_weight, up_bias,
    down_weight, down_bias, first_gain, first_shift, second_gain, second_shift,
):
    groups, packs = lax.axis_size("tensor"), lax.axis_size("dp")
    width, _, hc = qkv_weight.shape
    ffn = up_weight.shape[1]
    share = 1.0 / packs
    core = lax.axis_index("dp") % 2
    side = lax.axis_index("dp") // 2 % 2
    where = jnp.stack([core, side]).astype(jnp.int32)
    row = lambda v: v.reshape(1, -1)
    turns = range(1, groups)
    local_qkv = jnp.transpose(qkv_weight, (1, 0, 2))
    biases = jnp.concatenate([up_bias.reshape(-1, hc), qv_bias])
    count = biases.shape[0]
    extra = jnp.pad(three_parts(biases).reshape(3 * count, hc), ((0, count + 8), (0, 0)))
    quarter = lax.dynamic_slice_in_dim(local_qkv, (2 * core + side) * (width // 4), width // 4, 1)
    quarter = jnp.concatenate([quarter.reshape(-1, hc), extra])
    qkv_mine = [around(quarter, "tensor", k) for k in turns]
    qt0, kt0, vt0, kr0, vr0, qn0, kn0, nl, codek, codet, meta, wqkv0, near, far = prep_own(
        where, tokens, lengths, local_qkv, extra, row(first_gain), row(first_shift), out_weight, up_weight, down_weight
    )
    nl, near, *qkv_mine = lax.optimization_barrier((nl, near, *qkv_mine))
    qkv_mine = jnp.stack(qkv_mine)
    qkv_beside = swapped(qkv_mine, 2)
    near = [around(near, "tensor", k) for k in turns]
    ot0, low0, lse0 = attend(2 * BLOCK, OWNQ, 1, meta, qt0, codet, kr0, codek, vt0, qn0, kn0)
    ot0, qkv_beside, qkv_mine, far, near[0], near[-1] = lax.optimization_barrier(
        (ot0, qkv_beside, qkv_mine, far, near[0], near[-1])
    )
    qkv_parts = [v for part in (qkv_mine, qkv_beside) for v in (part, swapped(part, 1))]
    far = [around(far, "tensor", k) for k in turns]
    qt1, kt1, vt1, kr1, vr1, qn1, kn1, wqkv1, ub = prep_others(nl, where, qkv_parts)
    kr1, *near = lax.optimization_barrier((kr1, *near))
    near = jnp.stack(near)
    beside = swapped(near, 2)
    ot1, low1, lse1 = attend(BLOCK, BLOCK, 3, meta, qt1, codet, kr1, codek, vt1, qn1, kn1)
    ot1, near, beside, *far = lax.optimization_barrier((ot1, near, beside, *far))
    pieces = [near, beside, jnp.stack(far)]
    pieces = [v for piece in pieces for v in (piece, swapped(piece, 1))]
    out, gm, dt0, dt1, delta0, delta1, grads, sums = feed(
        where, meta, tokens, cotangent, ot0, ot1, low0, low1, out_weight, up_weight, down_weight, pieces,
        row(out_bias), row(up_bias), ub, row(down_bias), row(second_gain), row(second_shift),
    )
    grads = summed_chunk(grads)
    late_rows = -(-(3 * hc + 16) // (16 * packs)) * 16 * packs
    *own, late, norm_sums = reverse(
        2 * BLOCK, 1, meta, kr0, vr0, kt0, qt0, dt0, codek, codet, lse0, delta0,
        own=(tokens, nl, wqkv0, sums), late=late_rows,
    )
    norms = jnp.pad(norm_sums.astype(BF16), ((0, 14), (0, 0)))
    chunk = grads.shape[0]
    mixed = jnp.concatenate([spread(jnp.concatenate([grads, norms])), late.reshape(packs, -1, width)], axis=1)
    mixed, kr1 = lax.optimization_barrier((mixed, kr1))
    mixed = lax.all_to_all(mixed, "dp", 0, 0)
    rest = reverse(BLOCK, 2, meta, kr1, vr1, kt1, qt1, dt1, codek, codet, lse1, delta1)
    mixed, rest0 = lax.optimization_barrier((mixed, rest[0]))
    late = jnp.sum(mixed[:, chunk + 16 :].astype(F32), axis=0).astype(BF16)
    late = lax.all_to_all(spread(late), "dp", 0, 0)
    norms = jnp.sum(mixed[:, chunk : chunk + 8].astype(F32), axis=0)
    norms = [norms] + [around(norms, "tensor", k) for k in turns]
    grad_tokens, grad_out, grad_up, grad_down = finish(
        share, tokens, gm, own, [rest0, *rest[1:]], wqkv0, wqkv1, row(first_gain),
        mixed, (hc, width, ffn),
    )
    gw, gb, *vectors = last(share, late, norms, hc)
    sums = [v.reshape(-1) for v in vectors]
    norm_sums = sums[5:]
    return (
        out,
        grad_tokens,
        jnp.transpose(gw, (1, 0, 2)),
        gb,
        grad_out,
        sums[3],
        grad_up,
        sums[4],
        grad_down,
        sums[0],
        norm_sums[0],
        norm_sums[1],
        sums[1],
        sums[2],
    )


def solution(mesh):
    in_specs = (
        P("dp", None),
        P("dp", None),
        P("dp", None),
        P(None, None, "tensor"),
        P(None, "tensor"),
        P("tensor", None),
        P(),
        P(None, "tensor"),
        P("tensor"),
        P("tensor", None),
        P(),
        P(),
        P(),
        P(),
        P(),
    )
    out_specs = (
        P("dp", None),
        P("dp", None),
        P(None, None, "tensor"),
        P(None, "tensor"),
        P("tensor", None),
        P(),
        P(None, "tensor"),
        P("tensor"),
        P("tensor", None),
        P(),
        P(),
        P(),
        P(),
        P(),
    )
    return jax.shard_map(body, mesh=mesh, in_specs=in_specs, out_specs=out_specs, check_vma=False)
```

```python
import functools
import math

import jax
import jax.numpy as jnp
from jax import lax
from jax.experimental import pallas as pl
from jax.experimental.pallas import tpu as pltpu
from jax.sharding import PartitionSpec as P

HEAD_DIM = 64
BLOCK = 256
SUB = 128
PREP = 512
OWNQ = 512
FEED = 512
LAST = 512
CODES = 128
LOG2E = math.log2(math.e)
SCALE = LOG2E * HEAD_DIM**-0.5
LEVEL = 90.0
COST = pl.CostEstimate(flops=10**6, bytes_accessed=0, transcendentals=0)
VMEM = 60 << 20
BF16 = jnp.bfloat16
F32 = jnp.float32


def dot(a, b, ca=1, cb=0):
    return lax.dot_general(a, b, (((ca,), (cb,)), ((), ())), preferred_element_type=F32)


def whole(*shape):
    return pl.BlockSpec(shape, lambda *_: (0,) * len(shape))


def rows(n, width):
    return pl.BlockSpec((n, width), lambda i: (i, 0))


def cols(height, n):
    return pl.BlockSpec((height, n), lambda i: (0, i))


SMEM = pl.BlockSpec(memory_space=pltpu.SMEM)
ANY = pl.BlockSpec(memory_space=pl.ANY)


def normalise(v):
    centred = v - jnp.mean(v, axis=-1, keepdims=True)
    r = lax.rsqrt(jnp.mean(centred * centred, axis=-1, keepdims=True) + 1e-05)
    return centred * r, r


def chain_ranges(len_s, meta, blocks):
    for b in range(blocks):
        meta[0, b] = blocks * BLOCK // SUB
        meta[1, b] = 0

    def chain(c, start):
        size = len_s[0, c]
        end = start + size

        @pl.when(size > 0)
        def _():
            first = start // SUB
            last = (end - 1) // SUB + 1

            def touch(b, _):
                meta[0, b] = jnp.minimum(meta[0, b], first)
                meta[1, b] = jnp.maximum(meta[1, b], last)
                return 0

            lax.fori_loop(start // BLOCK, (end - 1) // BLOCK + 1, touch, 0)

        return end

    meta[2, 0] = lax.fori_loop(0, len_s.shape[1], chain, 0)


def length_row(len_s):
    ids = lax.broadcasted_iota(jnp.int32, (1, CODES), 1)
    row = jnp.zeros((1, CODES), jnp.int32)
    for c in range(len_s.shape[1]):
        row = jnp.where(ids == c, len_s[0, c], row)
    return row.astype(F32)


def codes(i, chains, size, codek, codet):
    a = lax.broadcasted_iota(jnp.int32, (CODES, CODES), 0)
    b = lax.broadcasted_iota(jnp.int32, (CODES, CODES), 1)
    size_col = jnp.sum(jnp.where(a == b, size, 0.0), axis=1, keepdims=True)
    end_col = jnp.sum(jnp.where(b <= a, size, 0.0), axis=1, keepdims=True)
    end_row = jnp.sum(jnp.where(a <= b, size_col, 0.0), axis=0, keepdims=True)
    start_col, start_row = end_col - size_col, end_row - size
    ids_col = lax.broadcasted_iota(jnp.int32, (CODES, 1), 0)
    ids_row = lax.broadcasted_iota(jnp.int32, (1, CODES), 1)
    end_col = jnp.where(ids_col == chains, 1e9, end_col)
    end_row = jnp.where(ids_row == chains, 1e9, end_row)
    base = i * PREP
    slot = (base + lax.broadcasted_iota(jnp.int32, (CODES, PREP), 1)).astype(F32)
    codet[...] = jnp.where((slot >= start_col) & (slot < end_col), 1.0, 0.0).astype(BF16)
    slot = (base + lax.broadcasted_iota(jnp.int32, (PREP, CODES), 0)).astype(F32)
    codek[...] = jnp.where((slot >= start_row) & (slot < end_row), 0.0, -1e30).astype(BF16)


def head_norms(v):
    v = v.astype(F32)
    return jnp.sum((v * v).reshape(-1, HEAD_DIM, v.shape[1]), axis=1)


def project(g, hc, low, w, bias, vbias, qt, kt, vt, kr, vr, qn, kn):
    joined = dot(w, low, 1, 1)
    s = slice(g * hc, (g + 1) * hc)
    q = (joined[:hc] + bias[:hc]).astype(BF16)
    k = joined[hc : 2 * hc].astype(BF16)
    qt[s, :], kt[s, :] = q, k
    h = slice(g * hc // HEAD_DIM, (g + 1) * hc // HEAD_DIM)
    qn[h, :], kn[h, :] = head_norms(q), head_norms(k)
    vt[s, :] = (joined[2 * hc :] + bias[hc:]).astype(BF16)
    kv = dot(low, w[hc:], 1, 1)
    kr[:, s] = kv[:, :hc].astype(BF16)
    vr[:, s] = (kv[:, hc:] + vbias).astype(BF16)


def bias_columns(extra, which):
    parts = extra.shape[0] // 4 - 2
    row = lax.broadcasted_iota(jnp.int32, (extra.shape[0], PREP), 0)
    picked = (row == which) | (row == which + parts) | (row == which + 2 * parts)
    return dot(extra, jnp.where(picked, 1.0, 0.0).astype(BF16), 0, 0)


def bias_row(extra, which):
    parts = extra.shape[0] // 4 - 2
    row = lax.broadcasted_iota(jnp.int32, extra.shape, 0)
    picked = (row == which) | (row == which + parts) | (row == which + 2 * parts)
    return jnp.sum(jnp.where(picked, extra.astype(F32), 0.0), axis=0, keepdims=True)


def bias_rows(extra, count):
    return jnp.concatenate([bias_row(extra, n) for n in range(count)], axis=1)


def prep_own_kernel(
    hc, len_s, x, wn, extra, gain, shift, wo, wu, wd,
    qt, kt, vt, kr, vr, qn, kn, nl, xh, codek, codet, meta, w, near, far, bias, size, sems,
):
    i = pl.program_id(0)
    m, n, h = wu.shape[0] // 4, wd.shape[0] // 8, wo.shape[0] // 2
    core, side = place_of()
    quarter = 2 * core + side
    plan = (
        (wu, quarter * m, m, near, 0),
        (wd, quarter * n, n, near, m),
        (wo, core * h, h, far, 0),
        (wd, 4 * n + core * 2 * n, 2 * n, far, h),
    )
    copies = [
        pltpu.make_async_copy(
            src.at[pl.ds(pl.multiple_of(first, 16), count), :], dst.at[pl.ds(at, count), :], sems.at[k]
        )
        for k, (src, first, count, dst, at) in enumerate(plan)
    ]

    @pl.when(i == 0)
    def _():
        for copy in copies:
            copy.start()
        chain_ranges(len_s, meta, meta.shape[1])
        for p in range(3):
            w[p * hc : (p + 1) * hc, :] = wn[p].T
        for n in range(2):
            bias[n * hc : (n + 1) * hc, :] = bias_columns(extra[...], wn.shape[1] // hc + n)
        size[...] = length_row(len_s)

    xhat, _ = normalise(x[...].astype(F32))
    low = (xhat * gain[...] + shift[...]).astype(BF16)
    nl[...] = low
    xh[...] = xhat.astype(BF16)
    project(0, hc, low, w[...], bias, bias_row(extra[...], wn.shape[1] // hc + 1), qt, kt, vt, kr, vr, qn, kn)
    codes(i, len_s.shape[1], size[...], codek, codet)

    @pl.when(i == pl.num_programs(0) - 1)
    def _():
        for copy in copies:
            copy.wait()


def projected(hidden, slots):
    t = jax.ShapeDtypeStruct((hidden, slots), BF16)
    r = jax.ShapeDtypeStruct((slots, hidden), BF16)
    n = jax.ShapeDtypeStruct((hidden // HEAD_DIM, slots), F32)
    specs = [cols(hidden, PREP)] * 3 + [rows(PREP, hidden)] * 2 + [cols(hidden // HEAD_DIM, PREP)] * 2
    return specs, [t, t, t, r, r, n, n]


def prep_own(tokens, lengths, w, extra, gain, shift, wo, wu, wd):
    slots, width = tokens.shape
    hc = w.shape[2]
    blocks = slots // BLOCK
    specs, shapes = projected(hc, slots)
    return pl.pallas_call(
        functools.partial(prep_own_kernel, hc),
        grid=(slots // PREP,),
        in_specs=[
            SMEM,
            rows(PREP, width),
            whole(*w.shape),
            whole(*extra.shape),
            whole(1, width),
            whole(1, width),
            ANY,
            ANY,
            ANY,
        ],
        out_specs=specs + [rows(PREP, width), rows(PREP, width), rows(PREP, CODES), cols(CODES, PREP), SMEM, whole(3 * hc, width)]
        + [whole(wu.shape[0] // 4 + wd.shape[0] // 8, width), whole(wo.shape[0] // 2 + wd.shape[0] // 4, width)],
        out_shape=shapes
        + [
            jax.ShapeDtypeStruct((slots, width), BF16),
            jax.ShapeDtypeStruct((slots, width), BF16),
            jax.ShapeDtypeStruct((slots, CODES), BF16),
            jax.ShapeDtypeStruct((CODES, slots), BF16),
            jax.ShapeDtypeStruct((3, blocks), jnp.int32),
            jax.ShapeDtypeStruct((3 * hc, width), BF16),
            jax.ShapeDtypeStruct((wu.shape[0] // 4 + wd.shape[0] // 8, width), BF16),
            jax.ShapeDtypeStruct((wo.shape[0] // 2 + wd.shape[0] // 4, width), BF16),
        ],
        scratch_shapes=[
            pltpu.VMEM((2 * hc, PREP), F32),
            pltpu.VMEM((1, CODES), F32),
            pltpu.SemaphoreType.DMA((4,)),
        ],
        compiler_params=pltpu.CompilerParams(vmem_limit_bytes=VMEM),
        cost_estimate=COST,
        name="prep_own",
    )(lengths, tokens, w, extra, gain, shift, wo, wu, wd)


def copy_rows(dst, first, part):
    dst[pl.ds(pl.multiple_of(first, 16), part.shape[0]), :] = part


def prep_others_kernel(others, hc, nl, near0, near1, beside0, beside1, qt, kt, vt, kr, vr, qn, kn, w, ub, bias):
    quarter, width = w.shape[2] // 4, w.shape[2]
    where = place_of()
    extras = [near0[g, 3 * quarter :, :] for g in range(others)]
    first = width // hc

    @pl.when(pl.program_id(0) == 0)
    def _():
        for g in range(others):
            for p in range(3):
                for flip_core, flip_side, part in ((0, 0, near0), (1, 0, near1), (0, 1, beside0), (1, 1, beside1)):
                    core = where[0] + flip_core * (1 - 2 * where[0])
                    side = where[1] + flip_side * (1 - 2 * where[1])
                    at = pl.ds(pl.multiple_of((2 * core + side) * quarter, 128), quarter)
                    w[g, p * hc : (p + 1) * hc, at] = part[g, p * quarter : (p + 1) * quarter, :].T
            for n in range(2):
                bias[g, n * hc : (n + 1) * hc, :] = bias_columns(extras[g], first + n)
            ub[g] = bias_rows(extras[g], first)

    low = nl[...]
    for g in range(others):
        project(g, hc, low, w[g], bias.at[g], bias_row(extras[g], first + 1), qt, kt, vt, kr, vr, qn, kn)


def prep_others(nl, parts):
    slots, width = nl.shape
    others, _, hc = parts[0].shape
    specs, shapes = projected(others * hc, slots)
    return pl.pallas_call(
        functools.partial(prep_others_kernel, others, hc),
        grid=(slots // PREP,),
        in_specs=[
            rows(PREP, width),
            *(whole(*part.shape) for part in parts),
        ],
        out_specs=specs + [whole(others, 3 * hc, width), whole(others, 1, width)],
        out_shape=shapes
        + [
            jax.ShapeDtypeStruct((others, 3 * hc, width), BF16),
            jax.ShapeDtypeStruct((others, 1, width), F32),
        ],
        scratch_shapes=[pltpu.VMEM((others, 2 * hc, PREP), F32)],
        compiler_params=pltpu.CompilerParams(vmem_limit_bytes=VMEM),
        cost_estimate=COST,
        name="prep_others",
    )(nl, *parts)


def padded(part, h):
    zero = jnp.zeros_like(part)
    return jnp.concatenate([part, zero] if h % 2 == 0 else [zero, part], axis=0)


def pair(h):
    return pl.ds(h // 2 * 2 * HEAD_DIM, 2 * HEAD_DIM)


def head(h):
    return pl.ds(h * HEAD_DIM, HEAD_DIM)


def steps_over(meta, i, unit, size, slots):
    low, high = meta[0, unit * i], meta[1, unit * i]
    for u in range(1, unit):
        low = jnp.minimum(low, meta[0, unit * i + u])
        high = jnp.maximum(high, meta[1, unit * i + u])
    each = size // SUB
    count = jnp.maximum(high - low + each - 1, 0) // each
    return count, jnp.minimum(low, slots // SUB - count * each)


def step_slots(first, n, size):
    return pl.ds(pl.multiple_of((first + n * (size // SUB)) * SUB, SUB), size)


def attend_kernel(heads, keys, queries, ahead, meta, qt, codet, kr, codek, vt, qn, kn, ot, ot_low, lse, acc, top, total):
    i = pl.program_id(0)
    acc[...] = jnp.zeros_like(acc)
    total[...] = jnp.zeros_like(total)
    count, first = steps_over(meta, i, queries // BLOCK, keys, kr.shape[0])
    longest = jnp.max(jnp.max(qn[...], axis=1, keepdims=True) * jnp.max(kn[...], axis=1, keepdims=True))
    small = longest * SCALE**2 <= LEVEL**2

    def step(j, level):
        js = step_slots(first, j, keys)
        scores, probs, decays = {}, {}, {}
        code_k, code_t = codek[js, :], codet[...]
        for t in range(heads + 2 * ahead):
            if t < heads:
                left = jnp.concatenate([kr[js, pair(t)], code_k], axis=1)
                right = jnp.concatenate([padded(qt[head(t), :], t), code_t], axis=0)
                scores[t] = dot(left, right)
            h = t - ahead
            if 0 <= h < heads:
                s = scores.pop(h)
                before = total[8 * h : 8 * h + 8, :]
                if level:
                    p = jnp.exp2(s * SCALE)
                else:
                    old = top[h : h + 1, :]
                    new = jnp.maximum(old, jnp.max(s, axis=0, keepdims=True))
                    top[h : h + 1, :] = new
                    p = jnp.exp2(s * SCALE - new * SCALE)
                    decays[h] = jnp.exp2((old - new) * SCALE)
                    before = before * decays[h]
                total[8 * h : 8 * h + 8, :] = before + jnp.sum(p.reshape(keys // 8, 8, queries), axis=0)
                probs[h] = p.astype(BF16)
            h = t - 2 * ahead
            if 0 <= h < heads:
                mixed = dot(vt[head(h), js], probs.pop(h))
                acc[head(h), :] = (acc[head(h), :] if level else acc[head(h), :] * decays.pop(h)) + mixed

    @pl.when(small)
    def _():
        top[...] = jnp.zeros_like(top)
        lax.fori_loop(0, count, lambda j, _: step(j, True) or 0, 0)

    @pl.when(jnp.logical_not(small))
    def _():
        top[...] = jnp.full_like(top, -1e38)
        lax.fori_loop(0, count, lambda j, _: step(j, False) or 0, 0)

    slot = i * queries + lax.broadcasted_iota(jnp.int32, (1, queries), 1)
    live = slot < meta[2, 0]
    for h in range(heads):
        summed = jnp.sum(total[8 * h : 8 * h + 8, :], axis=0, keepdims=True)
        seen = summed > 0.0
        summed = jnp.where(seen, summed, 1.0)
        mixture = acc[head(h), :] / summed
        high = mixture.astype(BF16)
        ot[head(h), :] = high
        ot_low[head(h), :] = (mixture - high.astype(F32)).astype(BF16)
        lse[h : h + 1, :] = jnp.where(live, top[h : h + 1, :] * SCALE + jnp.log2(summed), 1e30)


def attend(keys, queries, ahead, meta, qt, codet, kr, codek, vt, qn, kn):
    hidden, slots = qt.shape
    heads = hidden // HEAD_DIM
    return pl.pallas_call(
        functools.partial(attend_kernel, heads, keys, queries, ahead),
        grid=(slots // queries,),
        in_specs=[
            SMEM,
            cols(hidden, queries),
            cols(CODES, queries),
            whole(*kr.shape),
            whole(*codek.shape),
            whole(*vt.shape),
            cols(heads, queries),
            whole(*kn.shape),
        ],
        out_specs=[cols(hidden, queries), cols(hidden, queries), cols(heads, queries)],
        out_shape=[
            jax.ShapeDtypeStruct((hidden, slots), BF16),
            jax.ShapeDtypeStruct((hidden, slots), BF16),
            jax.ShapeDtypeStruct((heads, slots), F32),
        ],
        scratch_shapes=[
            pltpu.VMEM((hidden, queries), F32),
            pltpu.VMEM((heads, queries), F32),
            pltpu.VMEM((8 * heads, queries), F32),
        ],
        compiler_params=pltpu.CompilerParams(vmem_limit_bytes=VMEM),
        cost_estimate=COST,
        name="attend",
    )(meta, qt, codet, kr, codek, vt, qn, kn)


def gelu_parts(u):
    bell = jnp.exp2(u * u * (-0.5 * LOG2E))
    return 0.5 + 0.5 * lax.erf(u * 0.5**0.5), u * bell * (2.0 * math.pi) ** -0.5


def feed_kernel(
    groups, meta, x, cot, ot_own, ot_rest, low_own, low_rest, wo_own, wu_own, wd_own, near0, near1, beside0, beside1, far0, far1, ob, ub_own, ub, db, gain, shift,
    out, gm_o, dt_own, dt_rest, delta_own, delta_rest, grads, sums, wo, wu, wd, g_up, g_down, g_out, s_up, s_rest,
):
    i = pl.program_id(0)

    @pl.when(i == 0)
    def _():
        g_up[...] = jnp.zeros_like(g_up)
        g_down[...] = jnp.zeros_like(g_down)
        g_out[...] = jnp.zeros_like(g_out)
        s_up[...] = jnp.zeros_like(s_up)
        s_rest[...] = jnp.zeros_like(s_rest)
        wo[0], wu[0], wd[0] = wo_own[...], wu_own[...], wd_own[...]
        core, side = place_of()
        for g in range(groups - 1):
            up, down, mixed = wu.at[g + 1], wd.at[g + 1], wo.at[g + 1]
            for which, near, beside, far in ((core, near0, beside0, far0), (1 - core, near1, beside1, far1)):
                n = down.shape[0] // 4
                copy_rows(mixed, which * (mixed.shape[0] // 2), far[g, : mixed.shape[0] // 2, :])
                copy_rows(down, 2 * n + which * n, far[g, mixed.shape[0] // 2 :, :])
                for turn, part in ((side, near), (1 - side, beside)):
                    at = 2 * which + turn
                    m = up.shape[0] // 4
                    copy_rows(up, at * m, part[g, :m, :])
                    copy_rows(down, at * (n // 2), part[g, m:, :])

    hc = wo.shape[1]
    hidden, width = groups * hc, wo.shape[2]
    source = x[...].astype(F32)
    o = jnp.concatenate([ot_own[...], ot_rest[...]], axis=0)
    w_out = wo[...].reshape(hidden, width)
    middle = source + dot(o, w_out, 0, 0) + ob[...]
    xhat, r = normalise(middle)
    low = (xhat * gain[...] + shift[...]).astype(BF16)
    slot = i * FEED + lax.broadcasted_iota(jnp.int32, (FEED, 1), 0)
    live = slot < meta[2, 0]
    grad = jnp.where(live, cot[...].astype(F32), 0.0)
    grad_low = grad.astype(BF16)
    ahead = 1
    ups, backs, actives, gus = {}, {}, {}, {}
    down, gnt = None, None
    for t in range(groups + 2 * ahead):
        if t < groups:
            ups[t] = dot(low, wu[t]) + (ub_own[...] if t == 0 else ub[t - 1])
            backs[t] = dot(grad_low, wd[t], 1, 1)
        g = t - ahead
        if 0 <= g < groups:
            u = ups.pop(g)
            cdf, bump = gelu_parts(u)
            actives[g] = (u * cdf).astype(BF16)
            gus[g] = (backs.pop(g) * (cdf + bump)).astype(BF16)
        g = t - 2 * ahead
        if 0 <= g < groups:
            a, gu = actives.pop(g), gus.pop(g)
            d1, d2 = dot(a, wd[g]), dot(gu, wu[g], 1, 1)
            down = d1 if down is None else down + d1
            gnt = d2 if gnt is None else gnt + d2
            if g == 0:
                g_up[...] += dot(low, gu, 0, 0)
                g_down[...] += dot(a, grad_low, 0, 0)
                s_up[...] += jnp.sum(gu.astype(F32).reshape(FEED // 8, 8, -1), axis=0)
    out[...] = jnp.where(live, middle + down + db[...], source).astype(BF16)
    e = gnt * gain[...]
    gm = grad + r * (e - jnp.mean(e, axis=-1, keepdims=True) - xhat * jnp.mean(e * xhat, axis=-1, keepdims=True))
    gml = gm.astype(BF16)
    gm_o[...] = jnp.where(live, gml, cot[...])
    d = dot(w_out, gml, 1, 1).astype(BF16)
    dt_own[...] = d[:hc]
    dt_rest[...] = d[hc:]
    exact = o.astype(F32) + jnp.concatenate([low_own[...], low_rest[...]], axis=0).astype(F32)
    inner = jnp.sum((d.astype(F32) * exact).reshape(hidden // HEAD_DIM, HEAD_DIM, FEED), axis=1)
    delta_own[...] = inner[: hc // HEAD_DIM]
    delta_rest[...] = inner[hc // HEAD_DIM :]
    g_out[...] += dot(o[:hc], gml)
    for n, v in enumerate((grad, gnt * xhat, gnt, gm)):
        s_rest[8 * n : 8 * n + 8, :] += jnp.sum(v.reshape(FEED // 8, 8, width), axis=0)

    @pl.when(i == pl.num_programs(0) - 1)
    def _():
        f = g_down.shape[0]
        grads[:hc, :] = g_out[...].astype(BF16)
        grads[hc : hc + width, :] = g_up[...].astype(BF16)
        grads[hc + width :, :] = g_down[...].astype(BF16)
        for n in range(4):
            sums[n : n + 1, :] = jnp.sum(s_rest[8 * n : 8 * n + 8, :], axis=0, keepdims=True)
        sums[4:5, :] = jnp.sum(s_up[...], axis=0, keepdims=True)
        sums[5:8, :] = jnp.zeros((3, width), F32)


def feed(meta, tokens, cotangent, ot_own, ot_rest, low_own, low_rest, wo, wu, wd, pieces, ob, ub_own, ub, db, gain, shift):
    slots, width = tokens.shape
    hc = wo.shape[0]
    ffn = wu.shape[1]
    others = pieces[0].shape[0]
    groups = others + 1
    hr = others * hc
    vec = whole(1, width)
    t = lambda n, kind=BF16: jax.ShapeDtypeStruct((n, slots), kind)
    return pl.pallas_call(
        functools.partial(feed_kernel, groups),
        grid=(slots // FEED,),
        in_specs=[
            SMEM,
            rows(FEED, width),
            rows(FEED, width),
            cols(hc, FEED),
            cols(hr, FEED),
            cols(hc, FEED),
            cols(hr, FEED),
            whole(*wo.shape),
            whole(*wu.shape),
            whole(*wd.shape),
            *(whole(*piece.shape) for piece in pieces),
            vec,
            whole(*ub_own.shape),
            whole(*ub.shape),
            vec,
            vec,
            vec,
        ],
        out_specs=[
            rows(FEED, width),
            rows(FEED, width),
            cols(hc, FEED),
            cols(hr, FEED),
            cols(hc // HEAD_DIM, FEED),
            cols(hr // HEAD_DIM, FEED),
            whole(hc + width + ffn, width),
            whole(8, width),
        ],
        out_shape=[
            jax.ShapeDtypeStruct((slots, width), BF16),
            jax.ShapeDtypeStruct((slots, width), BF16),
            t(hc),
            t(hr),
            t(hc // HEAD_DIM, F32),
            t(hr // HEAD_DIM, F32),
            jax.ShapeDtypeStruct((hc + width + ffn, width), BF16),
            jax.ShapeDtypeStruct((8, width), F32),
        ],
        scratch_shapes=[
            pltpu.VMEM((groups, hc, width), BF16),
            pltpu.VMEM((groups, width, ffn), BF16),
            pltpu.VMEM((groups, ffn, width), BF16),
            pltpu.VMEM((width, ffn), F32),
            pltpu.VMEM((ffn, width), F32),
            pltpu.VMEM((hc, width), F32),
            pltpu.VMEM((8, ffn), F32),
            pltpu.VMEM((32, width), F32),
        ],
        compiler_params=pltpu.CompilerParams(vmem_limit_bytes=VMEM),
        cost_estimate=COST,
        name="feed",
    )(meta, tokens, cotangent, ot_own, ot_rest, low_own, low_rest, wo, wu, wd, *pieces, ob, ub_own, ub, db, gain, shift)


def place_of():
    d = lax.axis_index("dp")
    return d % 2, d // 2 % 2


def at_block(b, size=BLOCK):
    return pl.ds(pl.multiple_of(b * size, size), size)


def reverse_pass(
    heads, keys, ahead, meta, lse, delta, sources, held, outs, staged, sums, in_sems, out_sems, more=()
):
    kr, vr, codek, kt, qt, dt, codet = held
    dq, dk, dv = staged
    dqs, dks, dvs = sums
    blocks = kr.shape[0] // BLOCK
    unit = keys // BLOCK
    factor = HEAD_DIM**-0.5

    def fetches(b):
        where = [(at_block(b), slice(None))] * 3 + [(slice(None), at_block(b))] * 4
        return [
            pltpu.make_async_copy(src.at[w], dst.at[w], in_sems.at[n, b])
            for n, (src, dst, w) in enumerate(zip(sources, held, where))
        ]

    def send(n, b, size):
        w = (slice(None), at_block(b, size))
        return pltpu.make_async_copy(staged[n].at[w], outs[n].at[w], out_sems.at[n, b])

    def start(b, _):
        for copy in fetches(b):
            copy.start()
        return 0

    def arrive(b, _):
        for copy in fetches(b):
            copy.wait()
        return 0

    lax.fori_loop(0, blocks, start, 0)
    for copy in more:
        copy.start()
    dqs[...] = jnp.zeros_like(dqs)

    def column(j, state):
        ready, flushed = state
        js = at_block(j, keys)
        dks[...] = jnp.zeros_like(dks)
        dvs[...] = jnp.zeros_like(dvs)

        count, first = steps_over(meta, j, unit, BLOCK, kr.shape[0])

        def step(i, _):
            qs = step_slots(first, i, BLOCK)
            scores, backs, grads, probs = {}, {}, {}, {}
            code_k, code_t = codek[js, :], codet[:, qs]
            for t in range(heads + 2 * ahead):
                if t < heads:
                    left = jnp.concatenate([kr[js, pair(t)], code_k], axis=1)
                    right = jnp.concatenate([padded(qt[head(t), qs], t), code_t], axis=0)
                    scores[t] = dot(left, right)
                    backs[t] = dot(vr[js, pair(t)], padded(dt[head(t), qs], t))
                h = t - ahead
                if 0 <= h < heads:
                    p = jnp.exp2(scores.pop(h) * SCALE - lse[h : h + 1, qs])
                    grads[h] = (p * (backs.pop(h) - delta[h : h + 1, qs])).astype(BF16)
                    probs[h] = p.astype(BF16)
                h = t - 2 * ahead
                if 0 <= h < heads:
                    ds, p = grads.pop(h), probs.pop(h)
                    dqs[head(h), qs] += dot(kt[head(h), js], ds)
                    dks[head(h), :] += dot(qt[head(h), qs], ds, 1, 1)
                    dvs[head(h), :] += dot(dt[head(h), qs], p, 1, 1)
            return 0

        end = (first * SUB + count * BLOCK + BLOCK - 1) // BLOCK
        need = jnp.where(count > 0, jnp.maximum(end, (j + 1) * unit), 0)
        lax.fori_loop(ready, need, arrive, 0)
        lax.fori_loop(0, count, step, 0)
        dk[:, js] = (dks[...] * factor).astype(BF16)
        dv[:, js] = dvs[...].astype(BF16)
        send(1, j, keys).start()
        send(2, j, keys).start()

        def whole_row(b):
            return (b < blocks) & (meta[1, jnp.minimum(b, blocks - 1)] <= (j + 1) * (keys // SUB))

        def flush(b):
            dq[:, at_block(b)] = (dqs[:, at_block(b)] * factor).astype(BF16)
            send(0, b, BLOCK).start()
            return b + 1

        return jnp.maximum(ready, need), lax.while_loop(whole_row, flush, flushed)

    ready, _ = lax.fori_loop(0, blocks // unit, column, (jnp.int32(0), jnp.int32(0)))
    lax.fori_loop(ready, blocks, arrive, 0)

    def finish_sends():
        def sent(b, _):
            send(0, b, BLOCK).wait()
            return 0

        def sent_column(j, _):
            send(1, j, keys).wait()
            send(2, j, keys).wait()
            return 0

        lax.fori_loop(0, blocks, sent, 0)
        lax.fori_loop(0, blocks // unit, sent_column, 0)

    return finish_sends


def reverse_kernel(heads, keys, ahead, meta, lse, delta, *refs):
    sources, outs, held, staged, sums = refs[:7], refs[7:10], refs[10:17], refs[17:20], refs[20:23]
    reverse_pass(heads, keys, ahead, meta, lse, delta, sources, held, outs, staged, sums, *refs[23:])()


def reverse_own_kernel(heads, keys, ahead, meta, lse, delta, early, gain, shift, *refs):
    sources, others, outs, (late, norms) = refs[:7], refs[7:9], refs[9:12], refs[12:14]
    held, staged, sums = refs[14:21], refs[21:24], refs[24:27]
    in_sems, out_sems, xh, w, sems = refs[27:]
    copies = [pltpu.make_async_copy(src, dst, sems.at[n]) for n, (src, dst) in enumerate(zip(others, (xh, w)))]
    finish_sends = reverse_pass(
        heads, keys, ahead, meta, lse, delta, sources, held, outs, staged, sums, in_sems, out_sems, copies
    )
    hc = staged[0].shape[0]
    slots = xh.shape[0]
    late[3 * hc :, :] = jnp.zeros((late.shape[0] - 3 * hc, late.shape[1]), BF16)
    late[3 * hc : 3 * hc + 8, :] = early[...].astype(BF16)
    for copy in copies:
        copy.wait()
    norm_gain, norm_shift = 0.0, 0.0
    for n, d in enumerate(staged):
        rows_of = slice(n * hc, (n + 1) * hc)
        product = dot(d[...], xh[...])
        total = dot(d[...], jnp.ones((slots, 128), BF16))[:, :1]
        late[rows_of, :] = (product * gain[...] + total * shift[...]).astype(BF16)
        if n != 1:
            row = dot(jnp.ones((8, slots), BF16), d[...], 1, 1)[:1]
            late[3 * hc + 8 : 3 * hc + 9, n // 2 * hc : (n // 2 + 1) * hc] = row.astype(BF16)
        part = w[rows_of, :].astype(F32)
        norm_gain += jnp.sum(part * product, axis=0, keepdims=True)
        norm_shift += jnp.sum(part * total, axis=0, keepdims=True)
    norms[0:1, :] = norm_gain
    norms[1:2, :] = norm_shift
    finish_sends()


def reverse(keys, ahead, meta, kr, vr, kt, qt, dt, codek, codet, lse, delta, own=None, late=0):
    hidden, slots = qt.shape
    heads = hidden // HEAD_DIM
    blocks = slots // BLOCK
    vm = pl.BlockSpec(memory_space=pltpu.VMEM)
    sources = (kr, vr, codek, kt, qt, dt, codet)
    shapes = [jax.ShapeDtypeStruct((hidden, slots), BF16)] * 3
    scratch = [pltpu.VMEM(v.shape, BF16) for v in sources] + [pltpu.VMEM((hidden, slots), BF16)] * 3
    scratch += [pltpu.VMEM((hidden, slots), F32)] + [pltpu.VMEM((hidden, keys), F32)] * 2
    scratch += [pltpu.SemaphoreType.DMA((7, blocks)), pltpu.SemaphoreType.DMA((3, blocks))]
    small, late_shapes = (lse, delta), []
    if own is not None:
        *others, early, gain, shift = own
        sources += tuple(others)
        small += (early, gain, shift)
        width = early.shape[1]
        late_shapes = [jax.ShapeDtypeStruct((late, width), BF16), jax.ShapeDtypeStruct((2, width), F32)]
        scratch += [pltpu.VMEM(v.shape, BF16) for v in others]
        scratch += [pltpu.SemaphoreType.DMA((2,))]
    return pl.pallas_call(
        functools.partial(reverse_kernel if own is None else reverse_own_kernel, heads, keys, ahead),
        in_specs=[SMEM] + [vm] * len(small) + [ANY] * len(sources),
        out_specs=[ANY] * 3 + [vm] * len(late_shapes),
        out_shape=shapes + late_shapes,
        scratch_shapes=scratch,
        compiler_params=pltpu.CompilerParams(vmem_limit_bytes=VMEM),
        cost_estimate=COST,
        name="reverse",
    )(meta, *small, *sources)


def finish_kernel(share, x, gm, q0, k0, v0, q1, k1, v1, w0, w1, gain, grads, out, *shards):
    *shards, joined = shards
    i = pl.program_id(0)
    @pl.when(i == 0)
    def _():
        chunk = joined.shape[0] // grads.shape[0]
        for c in range(grads.shape[0]):
            joined[c * chunk : (c + 1) * chunk, :] = grads[c, :chunk, :]

    first = 0
    for shard in shards:
        n = shard.shape[0]
        at = pl.ds(pl.multiple_of(first + i * n, 16), n)
        shard[...] = joined[at, :].astype(F32) * share
        first += n * pl.num_programs(0)
    hc, width = w0.shape[0] // 3, w0.shape[1]
    others = w1.shape[0]
    gn = dot(jnp.concatenate([q0[...], k0[...], v0[...]], axis=0), w0[...], 0, 0)
    for n, d in enumerate((q1, k1, v1)):
        gn += dot(d[...], w1[:, n * hc : (n + 1) * hc, :].reshape(others * hc, width), 0, 0)
    xhat, r = normalise(x[...].astype(F32))
    e = gn * gain[...]
    inner = r * (e - jnp.mean(e, axis=-1, keepdims=True) - xhat * jnp.mean(e * xhat, axis=-1, keepdims=True))
    out[...] = (gm[...].astype(F32) + inner).astype(BF16)


def finish(share, tokens, gm, own, rest, w0, w1, gain, grads, sizes):
    slots, width = tokens.shape
    steps = slots // LAST
    hc = own[0].shape[0]
    hr = rest[0].shape[0]
    return pl.pallas_call(
        functools.partial(finish_kernel, share),
        grid=(slots // LAST,),
        in_specs=[rows(LAST, width), rows(LAST, width)]
        + [cols(hc, LAST)] * 3
        + [cols(hr, LAST)] * 3
        + [whole(*w0.shape), whole(*w1.shape), whole(1, width), whole(*grads.shape)],
        out_specs=[rows(LAST, width)] + [rows(n // steps, width) for n in sizes],
        out_shape=[jax.ShapeDtypeStruct((slots, width), BF16)]
        + [jax.ShapeDtypeStruct((n, width), F32) for n in sizes],
        scratch_shapes=[pltpu.VMEM((sum(sizes), width), BF16)],
        compiler_params=pltpu.CompilerParams(vmem_limit_bytes=VMEM),
        cost_estimate=COST,
        name="finish",
    )(tokens, gm, *own, *rest, w0, w1, gain, grads)


def last_kernel(share, late, *refs):
    *norms, gw, bias = refs[:-8]
    *sums, joined = refs[-8:]
    hc = bias.shape[1]
    packs, n = late.shape[0], late.shape[1]
    for c in range(packs):
        joined[c * n : (c + 1) * n, :] = late[c]
    for p in range(3):
        gw[p] = joined[p * hc : (p + 1) * hc, :].astype(F32).T * share
    tail = joined[3 * hc : 3 * hc + 16, :].astype(F32) * share
    bias[0:1, :] = tail[8:9, :hc]
    bias[1:2, :] = tail[8:9, hc : 2 * hc]
    for k in range(5):
        sums[k][...] = tail[k : k + 1]
    total = sum(norm[...] for norm in norms[1:]) + norms[0][...]
    for k in range(2):
        sums[5 + k][...] = total[k : k + 1] * share


def last(share, late, norms, hc):
    packs, n, width = late.shape
    vm = pl.BlockSpec(memory_space=pltpu.VMEM)
    return pl.pallas_call(
        functools.partial(last_kernel, share),
        in_specs=[vm] * (1 + len(norms)),
        out_specs=[vm] * 9,
        out_shape=[
            jax.ShapeDtypeStruct((3, width, hc), F32),
            jax.ShapeDtypeStruct((2, hc), F32),
        ]
        + [jax.ShapeDtypeStruct((1, width), F32)] * 7,
        scratch_shapes=[pltpu.VMEM((packs * n, width), BF16)],
        compiler_params=pltpu.CompilerParams(vmem_limit_bytes=8 << 20),
        name="last",
    )(late, *norms)


def around(v, axis, k):
    n = lax.axis_size(axis)
    return lax.ppermute(v, axis, [(t, (t - k) % n) for t in range(n)])


def swapped(v, bit):
    return lax.ppermute(v, "dp", [(d, d ^ bit) for d in range(lax.axis_size("dp"))])


def summed_chunk(v):
    packs = lax.axis_size("dp")
    parts = lax.all_to_all(v, "dp", 0, 0, tiled=True)
    return jnp.sum(parts.reshape(packs, -1, v.shape[1]).astype(F32), axis=0).astype(v.dtype)


def spread(v):
    return jnp.broadcast_to(v[None], (lax.axis_size("dp"), *v.shape))


def three_parts(v):
    high = lax.reduce_precision(v, 8, 7)
    mid = lax.reduce_precision(v - high, 8, 7)
    return jnp.stack([high, mid, v - high - mid]).astype(BF16)


def body(
    tokens, lengths, cotangent, qkv_weight, qv_bias, out_weight, out_bias, up_weight, up_bias,
    down_weight, down_bias, first_gain, first_shift, second_gain, second_shift,
):
    groups, packs = lax.axis_size("tensor"), lax.axis_size("dp")
    width, _, hc = qkv_weight.shape
    ffn = up_weight.shape[1]
    share = 1.0 / packs
    core, side = place_of()
    row = lambda v: v.reshape(1, -1)
    turns = range(1, groups)
    local_qkv = jnp.transpose(qkv_weight, (1, 0, 2))
    biases = jnp.concatenate([up_bias.reshape(-1, hc), qv_bias])
    count = biases.shape[0]
    extra = jnp.pad(three_parts(biases).reshape(3 * count, hc), ((0, count + 8), (0, 0)))
    quarter = lax.dynamic_slice_in_dim(local_qkv, (2 * core + side) * (width // 4), width // 4, 1)
    quarter = jnp.concatenate([quarter.reshape(-1, hc), extra])
    qkv_mine = [around(quarter, "tensor", k) for k in turns]
    qt0, kt0, vt0, kr0, vr0, qn0, kn0, nl, xh, codek, codet, meta, wqkv0, near, far = prep_own(
        tokens, lengths, local_qkv, extra, row(first_gain), row(first_shift), out_weight, up_weight, down_weight
    )
    nl, near, *qkv_mine = lax.optimization_barrier((nl, near, *qkv_mine))
    qkv_mine = jnp.stack(qkv_mine)
    qkv_beside = swapped(qkv_mine, 2)
    near = [around(near, "tensor", k) for k in turns]
    ot0, low0, lse0 = attend(2 * BLOCK, OWNQ, 1, meta, qt0, codet, kr0, codek, vt0, qn0, kn0)
    ot0, qkv_beside, qkv_mine, far, near[0], near[-1] = lax.optimization_barrier(
        (ot0, qkv_beside, qkv_mine, far, near[0], near[-1])
    )
    qkv_parts = [v for part in (qkv_mine, qkv_beside) for v in (part, swapped(part, 1))]
    far = [around(far, "tensor", k) for k in turns]
    qt1, kt1, vt1, kr1, vr1, qn1, kn1, wqkv1, ub = prep_others(nl, qkv_parts)
    kr1, *near = lax.optimization_barrier((kr1, *near))
    near = jnp.stack(near)
    beside = swapped(near, 2)
    ot1, low1, lse1 = attend(BLOCK, BLOCK, 3, meta, qt1, codet, kr1, codek, vt1, qn1, kn1)
    ot1, near, beside, *far = lax.optimization_barrier((ot1, near, beside, *far))
    pieces = [near, beside, jnp.stack(far)]
    pieces = [v for piece in pieces for v in (piece, swapped(piece, 1))]
    out, gm, dt0, dt1, delta0, delta1, grads, sums = feed(
        meta, tokens, cotangent, ot0, ot1, low0, low1, out_weight, up_weight, down_weight, pieces,
        row(out_bias), row(up_bias), ub, row(down_bias), row(second_gain), row(second_shift),
    )
    grads = summed_chunk(grads)
    late_rows = -(-(3 * hc + 16) // (16 * packs)) * 16 * packs
    *own, late, norm_sums = reverse(
        2 * BLOCK, 1, meta, kr0, vr0, kt0, qt0, dt0, codek, codet, lse0, delta0,
        own=(xh, wqkv0, sums, row(first_gain), row(first_shift)), late=late_rows,
    )
    norms = jnp.pad(norm_sums.astype(BF16), ((0, 14), (0, 0)))
    chunk = grads.shape[0]
    mixed = jnp.concatenate([spread(jnp.concatenate([grads, norms])), late.reshape(packs, -1, width)], axis=1)
    mixed, kr1 = lax.optimization_barrier((mixed, kr1))
    mixed = lax.all_to_all(mixed, "dp", 0, 0)
    rest = reverse(BLOCK, 2, meta, kr1, vr1, kt1, qt1, dt1, codek, codet, lse1, delta1)
    mixed, rest0 = lax.optimization_barrier((mixed, rest[0]))
    late = jnp.sum(mixed[:, chunk + 16 :].astype(F32), axis=0).astype(BF16)
    late = lax.all_to_all(spread(late), "dp", 0, 0)
    norms = jnp.sum(mixed[:, chunk : chunk + 8].astype(F32), axis=0)
    norms = [norms] + [around(norms, "tensor", k) for k in turns]
    grad_tokens, grad_out, grad_up, grad_down = finish(
        share, tokens, gm, own, [rest0, *rest[1:]], wqkv0, wqkv1, row(first_gain),
        mixed, (hc, width, ffn),
    )
    gw, gb, *vectors = last(share, late, norms, hc)
    sums = [v.reshape(-1) for v in vectors]
    norm_sums = sums[5:]
    return (
        out,
        grad_tokens,
        jnp.transpose(gw, (1, 0, 2)),
        gb,
        grad_out,
        sums[3],
        grad_up,
        sums[4],
        grad_down,
        sums[0],
        norm_sums[0],
        norm_sums[1],
        sums[1],
        sums[2],
    )


def solution(mesh):
    in_specs = (
        P("dp", None),
        P("dp", None),
        P("dp", None),
        P(None, None, "tensor"),
        P(None, "tensor"),
        P("tensor", None),
        P(),
        P(None, "tensor"),
        P("tensor"),
        P("tensor", None),
        P(),
        P(),
        P(),
        P(),
        P(),
    )
    out_specs = (
        P("dp", None),
        P("dp", None),
        P(None, None, "tensor"),
        P(None, "tensor"),
        P("tensor", None),
        P(),
        P(None, "tensor"),
        P("tensor"),
        P("tensor", None),
        P(),
        P(),
        P(),
        P(),
        P(),
    )
    return jax.shard_map(body, mesh=mesh, in_specs=in_specs, out_specs=out_specs, check_vma=False)
```

```python
import functools
import math

import jax
import jax.numpy as jnp
from jax import lax
from jax.experimental import pallas as pl
from jax.experimental.pallas import tpu as pltpu
from jax.sharding import PartitionSpec as P

HEAD_DIM = 64
BLOCK = 256
SUB = 128
PREP = 512
OWNQ = 512
FEED = 512
LAST = 512
CODES = 128
LOG2E = math.log2(math.e)
SCALE = LOG2E * HEAD_DIM**-0.5
LEVEL = 90.0
COST = pl.CostEstimate(flops=10**6, bytes_accessed=0, transcendentals=0)
VMEM = 60 << 20
BF16 = jnp.bfloat16
F32 = jnp.float32


def dot(a, b, ca=1, cb=0):
    return lax.dot_general(a, b, (((ca,), (cb,)), ((), ())), preferred_element_type=F32)


def whole(*shape):
    return pl.BlockSpec(shape, lambda *_: (0,) * len(shape))


def rows(n, width):
    return pl.BlockSpec((n, width), lambda i: (i, 0))


def cols(height, n):
    return pl.BlockSpec((height, n), lambda i: (0, i))


SMEM = pl.BlockSpec(memory_space=pltpu.SMEM)
ANY = pl.BlockSpec(memory_space=pl.ANY)


def normalise(v):
    centred = v - jnp.mean(v, axis=-1, keepdims=True)
    r = lax.rsqrt(jnp.mean(centred * centred, axis=-1, keepdims=True) + 1e-05)
    return centred * r, r


def chain_ranges(len_s, meta, blocks):
    for b in range(blocks):
        meta[0, b] = blocks * BLOCK // SUB
        meta[1, b] = 0

    def chain(c, start):
        size = len_s[0, c]
        end = start + size

        @pl.when(size > 0)
        def _():
            first = start // SUB
            last = (end - 1) // SUB + 1

            def touch(b, _):
                meta[0, b] = jnp.minimum(meta[0, b], first)
                meta[1, b] = jnp.maximum(meta[1, b], last)
                return 0

            lax.fori_loop(start // BLOCK, (end - 1) // BLOCK + 1, touch, 0)

        return end

    meta[2, 0] = lax.fori_loop(0, len_s.shape[1], chain, 0)


def length_row(len_s):
    ids = lax.broadcasted_iota(jnp.int32, (1, CODES), 1)
    row = jnp.zeros((1, CODES), jnp.int32)
    for c in range(len_s.shape[1]):
        row = jnp.where(ids == c, len_s[0, c], row)
    return row.astype(F32)


def codes(i, chains, size, codek, codet):
    a = lax.broadcasted_iota(jnp.int32, (CODES, CODES), 0)
    b = lax.broadcasted_iota(jnp.int32, (CODES, CODES), 1)
    size_col = jnp.sum(jnp.where(a == b, size, 0.0), axis=1, keepdims=True)
    end_col = jnp.sum(jnp.where(b <= a, size, 0.0), axis=1, keepdims=True)
    end_row = jnp.sum(jnp.where(a <= b, size_col, 0.0), axis=0, keepdims=True)
    start_col, start_row = end_col - size_col, end_row - size
    ids_col = lax.broadcasted_iota(jnp.int32, (CODES, 1), 0)
    ids_row = lax.broadcasted_iota(jnp.int32, (1, CODES), 1)
    end_col = jnp.where(ids_col == chains, 1e9, end_col)
    end_row = jnp.where(ids_row == chains, 1e9, end_row)
    base = i * PREP
    slot = (base + lax.broadcasted_iota(jnp.int32, (CODES, PREP), 1)).astype(F32)
    codet[...] = jnp.where((slot >= start_col) & (slot < end_col), 1.0, 0.0).astype(BF16)
    slot = (base + lax.broadcasted_iota(jnp.int32, (PREP, CODES), 0)).astype(F32)
    codek[...] = jnp.where((slot >= start_row) & (slot < end_row), 0.0, -1e30).astype(BF16)


def head_norms(v):
    v = v.astype(F32)
    return jnp.sum((v * v).reshape(-1, HEAD_DIM, v.shape[1]), axis=1)


def project(g, hc, low, w, bias, vbias, qt, kt, vt, kr, vr, qn, kn):
    joined = dot(w, low, 1, 1)
    s = slice(g * hc, (g + 1) * hc)
    q = (joined[:hc] + bias[:hc]).astype(BF16)
    k = joined[hc : 2 * hc].astype(BF16)
    qt[s, :], kt[s, :] = q, k
    h = slice(g * hc // HEAD_DIM, (g + 1) * hc // HEAD_DIM)
    qn[h, :], kn[h, :] = head_norms(q), head_norms(k)
    vt[s, :] = (joined[2 * hc :] + bias[hc:]).astype(BF16)
    kv = dot(low, w[hc:], 1, 1)
    kr[:, s] = kv[:, :hc].astype(BF16)
    vr[:, s] = (kv[:, hc:] + vbias).astype(BF16)


def bias_columns(extra, which):
    parts = extra.shape[0] // 4 - 2
    row = lax.broadcasted_iota(jnp.int32, (extra.shape[0], PREP), 0)
    picked = (row == which) | (row == which + parts) | (row == which + 2 * parts)
    return dot(extra, jnp.where(picked, 1.0, 0.0).astype(BF16), 0, 0)


def bias_row(extra, which):
    parts = extra.shape[0] // 4 - 2
    row = lax.broadcasted_iota(jnp.int32, extra.shape, 0)
    picked = (row == which) | (row == which + parts) | (row == which + 2 * parts)
    return jnp.sum(jnp.where(picked, extra.astype(F32), 0.0), axis=0, keepdims=True)


def bias_rows(extra, count):
    return jnp.concatenate([bias_row(extra, n) for n in range(count)], axis=1)


def prep_own_kernel(
    hc, len_s, x, wn, extra, gain, shift, wo, wu, wd,
    qt, kt, vt, kr, vr, qn, kn, nl, xh, codek, codet, meta, w, near, far, bias, size, sems,
):
    i = pl.program_id(0)
    m, n, h = wu.shape[0] // 4, wd.shape[0] // 8, wo.shape[0] // 2
    core, side = place_of()
    quarter = 2 * core + side
    plan = (
        (wu, quarter * m, m, near, 0),
        (wd, quarter * n, n, near, m),
        (wo, core * h, h, far, 0),
        (wd, 4 * n + core * 2 * n, 2 * n, far, h),
    )
    copies = [
        pltpu.make_async_copy(
            src.at[pl.ds(pl.multiple_of(first, 16), count), :], dst.at[pl.ds(at, count), :], sems.at[k]
        )
        for k, (src, first, count, dst, at) in enumerate(plan)
    ]

    @pl.when(i == 0)
    def _():
        for copy in copies:
            copy.start()
        chain_ranges(len_s, meta, meta.shape[1])
        for p in range(3):
            w[p * hc : (p + 1) * hc, :] = wn[p].T
        for n in range(2):
            bias[n * hc : (n + 1) * hc, :] = bias_columns(extra[...], wn.shape[1] // hc + n)
        size[...] = length_row(len_s)

    xhat, _ = normalise(x[...].astype(F32))
    low = (xhat * gain[...] + shift[...]).astype(BF16)
    nl[...] = low
    xh[...] = xhat.astype(BF16)
    project(0, hc, low, w[...], bias, bias_row(extra[...], wn.shape[1] // hc + 1), qt, kt, vt, kr, vr, qn, kn)
    codes(i, len_s.shape[1], size[...], codek, codet)

    @pl.when(i == pl.num_programs(0) - 1)
    def _():
        for copy in copies:
            copy.wait()


def projected(hidden, slots):
    t = pltpu.HBM((hidden, slots), BF16)
    r = pltpu.HBM((slots, hidden), BF16)
    n = pltpu.HBM((hidden // HEAD_DIM, slots), F32)
    specs = [cols(hidden, PREP)] * 3 + [rows(PREP, hidden)] * 2 + [cols(hidden // HEAD_DIM, PREP)] * 2
    return specs, [t, t, t, r, r, n, n]


def prep_own(tokens, lengths, w, extra, gain, shift, wo, wu, wd):
    slots, width = tokens.shape
    hc = w.shape[2]
    blocks = slots // BLOCK
    specs, shapes = projected(hc, slots)
    return pl.pallas_call(
        functools.partial(prep_own_kernel, hc),
        grid=(slots // PREP,),
        in_specs=[
            SMEM,
            rows(PREP, width),
            whole(*w.shape),
            whole(*extra.shape),
            whole(1, width),
            whole(1, width),
            ANY,
            ANY,
            ANY,
        ],
        out_specs=specs + [rows(PREP, width), rows(PREP, width), rows(PREP, CODES), cols(CODES, PREP), SMEM, whole(3 * hc, width)]
        + [whole(wu.shape[0] // 4 + wd.shape[0] // 8, width), whole(wo.shape[0] // 2 + wd.shape[0] // 4, width)],
        out_shape=shapes
        + [
            pltpu.HBM((slots, width), BF16),
            pltpu.HBM((slots, width), BF16),
            pltpu.HBM((slots, CODES), BF16),
            pltpu.HBM((CODES, slots), BF16),
            jax.ShapeDtypeStruct((3, blocks), jnp.int32),
            pltpu.HBM((3 * hc, width), BF16),
            pltpu.HBM((wu.shape[0] // 4 + wd.shape[0] // 8, width), BF16),
            pltpu.HBM((wo.shape[0] // 2 + wd.shape[0] // 4, width), BF16),
        ],
        scratch_shapes=[
            pltpu.VMEM((2 * hc, PREP), F32),
            pltpu.VMEM((1, CODES), F32),
            pltpu.SemaphoreType.DMA((4,)),
        ],
        compiler_params=pltpu.CompilerParams(vmem_limit_bytes=VMEM),
        cost_estimate=COST,
        name="prep_own",
    )(lengths, tokens, w, extra, gain, shift, wo, wu, wd)


def copy_rows(dst, first, part):
    dst[pl.ds(pl.multiple_of(first, 16), part.shape[0]), :] = part


def prep_others_kernel(others, hc, nl, near0, near1, beside0, beside1, qt, kt, vt, kr, vr, qn, kn, w, ub, bias):
    quarter, width = w.shape[2] // 4, w.shape[2]
    where = place_of()
    extras = [near0[g, 3 * quarter :, :] for g in range(others)]
    first = width // hc

    @pl.when(pl.program_id(0) == 0)
    def _():
        for g in range(others):
            for p in range(3):
                for flip_core, flip_side, part in ((0, 0, near0), (1, 0, near1), (0, 1, beside0), (1, 1, beside1)):
                    core = where[0] + flip_core * (1 - 2 * where[0])
                    side = where[1] + flip_side * (1 - 2 * where[1])
                    at = pl.ds(pl.multiple_of((2 * core + side) * quarter, 128), quarter)
                    w[g, p * hc : (p + 1) * hc, at] = part[g, p * quarter : (p + 1) * quarter, :].T
            for n in range(2):
                bias[g, n * hc : (n + 1) * hc, :] = bias_columns(extras[g], first + n)
            ub[g] = bias_rows(extras[g], first)

    low = nl[...]
    for g in range(others):
        project(g, hc, low, w[g], bias.at[g], bias_row(extras[g], first + 1), qt, kt, vt, kr, vr, qn, kn)


def prep_others(nl, parts):
    slots, width = nl.shape
    others, _, hc = parts[0].shape
    specs, shapes = projected(others * hc, slots)
    return pl.pallas_call(
        functools.partial(prep_others_kernel, others, hc),
        grid=(slots // PREP,),
        in_specs=[
            rows(PREP, width),
            *(whole(*part.shape) for part in parts),
        ],
        out_specs=specs + [whole(others, 3 * hc, width), whole(others, 1, width)],
        out_shape=shapes
        + [
            pltpu.HBM((others, 3 * hc, width), BF16),
            pltpu.HBM((others, 1, width), F32),
        ],
        scratch_shapes=[pltpu.VMEM((others, 2 * hc, PREP), F32)],
        compiler_params=pltpu.CompilerParams(vmem_limit_bytes=40 << 20),
        cost_estimate=COST,
        name="prep_others",
    )(nl, *parts)


def padded(part, h):
    zero = jnp.zeros_like(part)
    return jnp.concatenate([part, zero] if h % 2 == 0 else [zero, part], axis=0)


def pair(h):
    return pl.ds(h // 2 * 2 * HEAD_DIM, 2 * HEAD_DIM)


def head(h):
    return pl.ds(h * HEAD_DIM, HEAD_DIM)


def steps_over(meta, i, unit, size, slots):
    low, high = meta[0, unit * i], meta[1, unit * i]
    for u in range(1, unit):
        low = jnp.minimum(low, meta[0, unit * i + u])
        high = jnp.maximum(high, meta[1, unit * i + u])
    each = size // SUB
    count = jnp.maximum(high - low + each - 1, 0) // each
    return count, jnp.minimum(low, slots // SUB - count * each)


def step_slots(first, n, size):
    return pl.ds(pl.multiple_of((first + n * (size // SUB)) * SUB, SUB), size)


def attend_kernel(heads, keys, queries, ahead, meta, qt, codet, kr, codek, vt, qn, kn, ot, ot_low, lse, acc, top, total):
    i = pl.program_id(0)
    acc[...] = jnp.zeros_like(acc)
    total[...] = jnp.zeros_like(total)
    count, first = steps_over(meta, i, queries // BLOCK, keys, kr.shape[0])
    longest = jnp.max(jnp.max(qn[...], axis=1, keepdims=True) * jnp.max(kn[...], axis=1, keepdims=True))
    small = longest * SCALE**2 <= LEVEL**2

    def step(j, level):
        js = step_slots(first, j, keys)
        scores, probs, decays = {}, {}, {}
        code_k, code_t = codek[js, :], codet[...]
        for t in range(heads + 2 * ahead):
            if t < heads:
                left = jnp.concatenate([kr[js, pair(t)], code_k], axis=1)
                right = jnp.concatenate([padded(qt[head(t), :], t), code_t], axis=0)
                scores[t] = dot(left, right)
            h = t - ahead
            if 0 <= h < heads:
                s = scores.pop(h)
                before = total[8 * h : 8 * h + 8, :]
                if level:
                    p = jnp.exp2(s * SCALE)
                else:
                    old = top[h : h + 1, :]
                    new = jnp.maximum(old, jnp.max(s, axis=0, keepdims=True))
                    top[h : h + 1, :] = new
                    p = jnp.exp2(s * SCALE - new * SCALE)
                    decays[h] = jnp.exp2((old - new) * SCALE)
                    before = before * decays[h]
                total[8 * h : 8 * h + 8, :] = before + jnp.sum(p.reshape(keys // 8, 8, queries), axis=0)
                probs[h] = p.astype(BF16)
            h = t - 2 * ahead
            if 0 <= h < heads:
                mixed = dot(vt[head(h), js], probs.pop(h))
                acc[head(h), :] = (acc[head(h), :] if level else acc[head(h), :] * decays.pop(h)) + mixed

    @pl.when(small)
    def _():
        top[...] = jnp.zeros_like(top)
        lax.fori_loop(0, count, lambda j, _: step(j, True) or 0, 0)

    @pl.when(jnp.logical_not(small))
    def _():
        top[...] = jnp.full_like(top, -1e38)
        lax.fori_loop(0, count, lambda j, _: step(j, False) or 0, 0)

    slot = i * queries + lax.broadcasted_iota(jnp.int32, (1, queries), 1)
    live = slot < meta[2, 0]
    for h in range(heads):
        summed = jnp.sum(total[8 * h : 8 * h + 8, :], axis=0, keepdims=True)
        seen = summed > 0.0
        summed = jnp.where(seen, summed, 1.0)
        mixture = acc[head(h), :] / summed
        high = mixture.astype(BF16)
        ot[head(h), :] = high
        ot_low[head(h), :] = (mixture - high.astype(F32)).astype(BF16)
        lse[h : h + 1, :] = jnp.where(live, top[h : h + 1, :] * SCALE + jnp.log2(summed), 1e30)


def attend(keys, queries, ahead, meta, qt, codet, kr, codek, vt, qn, kn):
    hidden, slots = qt.shape
    heads = hidden // HEAD_DIM
    return pl.pallas_call(
        functools.partial(attend_kernel, heads, keys, queries, ahead),
        grid=(slots // queries,),
        in_specs=[
            SMEM,
            cols(hidden, queries),
            cols(CODES, queries),
            whole(*kr.shape),
            whole(*codek.shape),
            whole(*vt.shape),
            cols(heads, queries),
            whole(*kn.shape),
        ],
        out_specs=[cols(hidden, queries), cols(hidden, queries), cols(heads, queries)],
        out_shape=[
            pltpu.HBM((hidden, slots), BF16),
            pltpu.HBM((hidden, slots), BF16),
            pltpu.HBM((heads, slots), F32),
        ],
        scratch_shapes=[
            pltpu.VMEM((hidden, queries), F32),
            pltpu.VMEM((heads, queries), F32),
            pltpu.VMEM((8 * heads, queries), F32),
        ],
        compiler_params=pltpu.CompilerParams(vmem_limit_bytes=VMEM),
        cost_estimate=COST,
        name="attend",
    )(meta, qt, codet, kr, codek, vt, qn, kn)


def gelu_parts(u):
    bell = jnp.exp2(u * u * (-0.5 * LOG2E))
    return 0.5 + 0.5 * lax.erf(u * 0.5**0.5), u * bell * (2.0 * math.pi) ** -0.5


def feed_kernel(
    groups, meta, x, cot, ot_own, ot_rest, low_own, low_rest, wo_own, wu_own, wd_own, near0, near1, beside0, beside1, far0, far1, ob, ub_own, ub, db, gain, shift,
    out, gm_o, dt_own, dt_rest, delta_own, delta_rest, grads, sums, wo, wu, wd, g_up, g_down, g_out, s_up, s_rest,
):
    i = pl.program_id(0)

    @pl.when(i == 0)
    def _():
        g_up[...] = jnp.zeros_like(g_up)
        g_down[...] = jnp.zeros_like(g_down)
        g_out[...] = jnp.zeros_like(g_out)
        s_up[...] = jnp.zeros_like(s_up)
        s_rest[...] = jnp.zeros_like(s_rest)
        wo[0], wu[0], wd[0] = wo_own[...], wu_own[...], wd_own[...]
        core, side = place_of()
        for g in range(groups - 1):
            up, down, mixed = wu.at[g + 1], wd.at[g + 1], wo.at[g + 1]
            for which, near, beside, far in ((core, near0, beside0, far0), (1 - core, near1, beside1, far1)):
                n = down.shape[0] // 4
                copy_rows(mixed, which * (mixed.shape[0] // 2), far[g, : mixed.shape[0] // 2, :])
                copy_rows(down, 2 * n + which * n, far[g, mixed.shape[0] // 2 :, :])
                for turn, part in ((side, near), (1 - side, beside)):
                    at = 2 * which + turn
                    m = up.shape[0] // 4
                    copy_rows(up, at * m, part[g, :m, :])
                    copy_rows(down, at * (n // 2), part[g, m:, :])

    hc = wo.shape[1]
    hidden, width = groups * hc, wo.shape[2]
    source = x[...].astype(F32)
    o = jnp.concatenate([ot_own[...], ot_rest[...]], axis=0)
    w_out = wo[...].reshape(hidden, width)
    middle = source + dot(o, w_out, 0, 0) + ob[...]
    xhat, r = normalise(middle)
    low = (xhat * gain[...] + shift[...]).astype(BF16)
    slot = i * FEED + lax.broadcasted_iota(jnp.int32, (FEED, 1), 0)
    live = slot < meta[2, 0]
    grad = jnp.where(live, cot[...].astype(F32), 0.0)
    grad_low = grad.astype(BF16)
    ahead = 1
    ups, backs, actives, gus = {}, {}, {}, {}
    down, gnt = None, None
    for t in range(groups + 2 * ahead):
        if t < groups:
            ups[t] = dot(low, wu[t]) + (ub_own[...] if t == 0 else ub[t - 1])
            backs[t] = dot(grad_low, wd[t], 1, 1)
        g = t - ahead
        if 0 <= g < groups:
            u = ups.pop(g)
            cdf, bump = gelu_parts(u)
            actives[g] = (u * cdf).astype(BF16)
            gus[g] = (backs.pop(g) * (cdf + bump)).astype(BF16)
        g = t - 2 * ahead
        if 0 <= g < groups:
            a, gu = actives.pop(g), gus.pop(g)
            d1, d2 = dot(a, wd[g]), dot(gu, wu[g], 1, 1)
            down = d1 if down is None else down + d1
            gnt = d2 if gnt is None else gnt + d2
            if g == 0:
                g_up[...] += dot(low, gu, 0, 0)
                g_down[...] += dot(a, grad_low, 0, 0)
                s_up[...] += jnp.sum(gu.astype(F32).reshape(FEED // 8, 8, -1), axis=0)
    out[...] = jnp.where(live, middle + down + db[...], source).astype(BF16)
    e = gnt * gain[...]
    gm = grad + r * (e - jnp.mean(e, axis=-1, keepdims=True) - xhat * jnp.mean(e * xhat, axis=-1, keepdims=True))
    gml = gm.astype(BF16)
    gm_o[...] = jnp.where(live, gml, cot[...])
    d = dot(w_out, gml, 1, 1).astype(BF16)
    dt_own[...] = d[:hc]
    dt_rest[...] = d[hc:]
    exact = o.astype(F32) + jnp.concatenate([low_own[...], low_rest[...]], axis=0).astype(F32)
    inner = jnp.sum((d.astype(F32) * exact).reshape(hidden // HEAD_DIM, HEAD_DIM, FEED), axis=1)
    delta_own[...] = inner[: hc // HEAD_DIM]
    delta_rest[...] = inner[hc // HEAD_DIM :]
    g_out[...] += dot(o[:hc], gml)
    for n, v in enumerate((grad, gnt * xhat, gnt, gm)):
        s_rest[8 * n : 8 * n + 8, :] += jnp.sum(v.reshape(FEED // 8, 8, width), axis=0)

    @pl.when(i == pl.num_programs(0) - 1)
    def _():
        f = g_down.shape[0]
        grads[:hc, :] = g_out[...].astype(BF16)
        grads[hc : hc + width, :] = g_up[...].astype(BF16)
        grads[hc + width :, :] = g_down[...].astype(BF16)
        for n in range(4):
            sums[n : n + 1, :] = jnp.sum(s_rest[8 * n : 8 * n + 8, :], axis=0, keepdims=True)
        sums[4:5, :] = jnp.sum(s_up[...], axis=0, keepdims=True)
        sums[5:8, :] = jnp.zeros((3, width), F32)


def feed(meta, tokens, cotangent, ot_own, ot_rest, low_own, low_rest, wo, wu, wd, pieces, ob, ub_own, ub, db, gain, shift):
    slots, width = tokens.shape
    hc = wo.shape[0]
    ffn = wu.shape[1]
    others = pieces[0].shape[0]
    groups = others + 1
    hr = others * hc
    vec = whole(1, width)
    t = lambda n, kind=BF16: pltpu.HBM((n, slots), kind)
    return pl.pallas_call(
        functools.partial(feed_kernel, groups),
        grid=(slots // FEED,),
        in_specs=[
            SMEM,
            rows(FEED, width),
            rows(FEED, width),
            cols(hc, FEED),
            cols(hr, FEED),
            cols(hc, FEED),
            cols(hr, FEED),
            whole(*wo.shape),
            whole(*wu.shape),
            whole(*wd.shape),
            *(whole(*piece.shape) for piece in pieces),
            vec,
            whole(*ub_own.shape),
            whole(*ub.shape),
            vec,
            vec,
            vec,
        ],
        out_specs=[
            rows(FEED, width),
            rows(FEED, width),
            cols(hc, FEED),
            cols(hr, FEED),
            cols(hc // HEAD_DIM, FEED),
            cols(hr // HEAD_DIM, FEED),
            whole(hc + width + ffn, width),
            whole(8, width),
        ],
        out_shape=[
            pltpu.HBM((slots, width), BF16),
            pltpu.HBM((slots, width), BF16),
            t(hc),
            t(hr),
            t(hc // HEAD_DIM, F32),
            t(hr // HEAD_DIM, F32),
            pltpu.HBM((hc + width + ffn, width), BF16),
            pltpu.HBM((8, width), F32),
        ],
        scratch_shapes=[
            pltpu.VMEM((groups, hc, width), BF16),
            pltpu.VMEM((groups, width, ffn), BF16),
            pltpu.VMEM((groups, ffn, width), BF16),
            pltpu.VMEM((width, ffn), F32),
            pltpu.VMEM((ffn, width), F32),
            pltpu.VMEM((hc, width), F32),
            pltpu.VMEM((8, ffn), F32),
            pltpu.VMEM((32, width), F32),
        ],
        compiler_params=pltpu.CompilerParams(vmem_limit_bytes=50 << 20),
        cost_estimate=COST,
        name="feed",
    )(meta, tokens, cotangent, ot_own, ot_rest, low_own, low_rest, wo, wu, wd, *pieces, ob, ub_own, ub, db, gain, shift)


def place_of():
    d = lax.axis_index("dp")
    return d % 2, d // 2 % 2


def at_block(b, size=BLOCK):
    return pl.ds(pl.multiple_of(b * size, size), size)


def reverse_pass(
    heads, keys, ahead, meta, lse, delta, sources, held, outs, staged, sums, in_sems, out_sems, more=()
):
    kr, vr, codek, kt, qt, dt, codet = held
    dq, dk, dv = staged
    dqs, dks, dvs = sums
    blocks = kr.shape[0] // BLOCK
    unit = keys // BLOCK
    factor = HEAD_DIM**-0.5

    def fetches(b):
        where = [(at_block(b), slice(None))] * 3 + [(slice(None), at_block(b))] * 4
        return [
            pltpu.make_async_copy(src.at[w], dst.at[w], in_sems.at[n, b])
            for n, (src, dst, w) in enumerate(zip(sources, held, where))
        ]

    def send(n, b, size):
        w = (slice(None), at_block(b, size))
        return pltpu.make_async_copy(staged[n].at[w], outs[n].at[w], out_sems.at[n, b])

    def start(b, _):
        for copy in fetches(b):
            copy.start()
        return 0

    def arrive(b, _):
        for copy in fetches(b):
            copy.wait()
        return 0

    lax.fori_loop(0, blocks, start, 0)
    for copy in more:
        copy.start()
    dqs[...] = jnp.zeros_like(dqs)

    def column(j, state):
        ready, flushed = state
        js = at_block(j, keys)
        dks[...] = jnp.zeros_like(dks)
        dvs[...] = jnp.zeros_like(dvs)

        count, first = steps_over(meta, j, unit, BLOCK, kr.shape[0])

        def step(i, _):
            qs = step_slots(first, i, BLOCK)
            scores, backs, grads, probs = {}, {}, {}, {}
            code_k, code_t = codek[js, :], codet[:, qs]
            for t in range(heads + 2 * ahead):
                if t < heads:
                    left = jnp.concatenate([kr[js, pair(t)], code_k], axis=1)
                    right = jnp.concatenate([padded(qt[head(t), qs], t), code_t], axis=0)
                    scores[t] = dot(left, right)
                    backs[t] = dot(vr[js, pair(t)], padded(dt[head(t), qs], t))
                h = t - ahead
                if 0 <= h < heads:
                    p = jnp.exp2(scores.pop(h) * SCALE - lse[h : h + 1, qs])
                    grads[h] = (p * (backs.pop(h) - delta[h : h + 1, qs])).astype(BF16)
                    probs[h] = p.astype(BF16)
                h = t - 2 * ahead
                if 0 <= h < heads:
                    ds, p = grads.pop(h), probs.pop(h)
                    dqs[head(h), qs] += dot(kt[head(h), js], ds)
                    dks[head(h), :] += dot(qt[head(h), qs], ds, 1, 1)
                    dvs[head(h), :] += dot(dt[head(h), qs], p, 1, 1)
            return 0

        end = (first * SUB + count * BLOCK + BLOCK - 1) // BLOCK
        need = jnp.where(count > 0, jnp.maximum(end, (j + 1) * unit), 0)
        lax.fori_loop(ready, need, arrive, 0)
        lax.fori_loop(0, count, step, 0)
        dk[:, js] = (dks[...] * factor).astype(BF16)
        dv[:, js] = dvs[...].astype(BF16)
        send(1, j, keys).start()
        send(2, j, keys).start()

        def whole_row(b):
            return (b < blocks) & (meta[1, jnp.minimum(b, blocks - 1)] <= (j + 1) * (keys // SUB))

        def flush(b):
            dq[:, at_block(b)] = (dqs[:, at_block(b)] * factor).astype(BF16)
            send(0, b, BLOCK).start()
            return b + 1

        return jnp.maximum(ready, need), lax.while_loop(whole_row, flush, flushed)

    ready, _ = lax.fori_loop(0, blocks // unit, column, (jnp.int32(0), jnp.int32(0)))
    lax.fori_loop(ready, blocks, arrive, 0)

    def finish_sends():
        def sent(b, _):
            send(0, b, BLOCK).wait()
            return 0

        def sent_column(j, _):
            send(1, j, keys).wait()
            send(2, j, keys).wait()
            return 0

        lax.fori_loop(0, blocks, sent, 0)
        lax.fori_loop(0, blocks // unit, sent_column, 0)

    return finish_sends


def reverse_kernel(heads, keys, ahead, meta, lse, delta, *refs):
    sources, outs, held, staged, sums = refs[:7], refs[7:10], refs[10:17], refs[17:20], refs[20:23]
    reverse_pass(heads, keys, ahead, meta, lse, delta, sources, held, outs, staged, sums, *refs[23:])()


def reverse_own_kernel(heads, keys, ahead, meta, lse, delta, early, gain, shift, *refs):
    sources, others, outs, (late, norms) = refs[:7], refs[7:9], refs[9:12], refs[12:14]
    held, staged, sums = refs[14:21], refs[21:24], refs[24:27]
    in_sems, out_sems, xh, w, sems = refs[27:]
    copies = [pltpu.make_async_copy(src, dst, sems.at[n]) for n, (src, dst) in enumerate(zip(others, (xh, w)))]
    finish_sends = reverse_pass(
        heads, keys, ahead, meta, lse, delta, sources, held, outs, staged, sums, in_sems, out_sems, copies
    )
    hc = staged[0].shape[0]
    slots = xh.shape[0]
    late[3 * hc :, :] = jnp.zeros((late.shape[0] - 3 * hc, late.shape[1]), BF16)
    late[3 * hc : 3 * hc + 8, :] = early[...].astype(BF16)
    for copy in copies:
        copy.wait()
    norm_gain, norm_shift = 0.0, 0.0
    for n, d in enumerate(staged):
        rows_of = slice(n * hc, (n + 1) * hc)
        product = dot(d[...], xh[...])
        total = dot(d[...], jnp.ones((slots, 128), BF16))[:, :1]
        late[rows_of, :] = (product * gain[...] + total * shift[...]).astype(BF16)
        if n != 1:
            row = dot(jnp.ones((8, slots), BF16), d[...], 1, 1)[:1]
            late[3 * hc + 8 : 3 * hc + 9, n // 2 * hc : (n // 2 + 1) * hc] = row.astype(BF16)
        part = w[rows_of, :].astype(F32)
        norm_gain += jnp.sum(part * product, axis=0, keepdims=True)
        norm_shift += jnp.sum(part * total, axis=0, keepdims=True)
    norms[0:1, :] = norm_gain
    norms[1:2, :] = norm_shift
    finish_sends()


def reverse(keys, ahead, meta, kr, vr, kt, qt, dt, codek, codet, lse, delta, own=None, late=0):
    hidden, slots = qt.shape
    heads = hidden // HEAD_DIM
    blocks = slots // BLOCK
    vm = pl.BlockSpec(memory_space=pltpu.VMEM)
    sources = (kr, vr, codek, kt, qt, dt, codet)
    shapes = [pltpu.HBM((hidden, slots), BF16)] * 3
    scratch = [pltpu.VMEM(v.shape, BF16) for v in sources] + [pltpu.VMEM((hidden, slots), BF16)] * 3
    scratch += [pltpu.VMEM((hidden, slots), F32)] + [pltpu.VMEM((hidden, keys), F32)] * 2
    scratch += [pltpu.SemaphoreType.DMA((7, blocks)), pltpu.SemaphoreType.DMA((3, blocks))]
    small, late_shapes = (lse, delta), []
    if own is not None:
        *others, early, gain, shift = own
        sources += tuple(others)
        small += (early, gain, shift)
        width = early.shape[1]
        late_shapes = [pltpu.HBM((late, width), BF16), pltpu.HBM((2, width), F32)]
        scratch += [pltpu.VMEM(v.shape, BF16) for v in others]
        scratch += [pltpu.SemaphoreType.DMA((2,))]
    return pl.pallas_call(
        functools.partial(reverse_kernel if own is None else reverse_own_kernel, heads, keys, ahead),
        in_specs=[SMEM] + [vm] * len(small) + [ANY] * len(sources),
        out_specs=[ANY] * 3 + [vm] * len(late_shapes),
        out_shape=shapes + late_shapes,
        scratch_shapes=scratch,
        compiler_params=pltpu.CompilerParams(vmem_limit_bytes=VMEM),
        cost_estimate=COST,
        name="reverse",
    )(meta, *small, *sources)


def finish_kernel(share, x, gm, q0, k0, v0, q1, k1, v1, w0, w1, gain, grads, out, *shards):
    *shards, joined = shards
    i = pl.program_id(0)
    @pl.when(i == 0)
    def _():
        chunk = joined.shape[0] // grads.shape[0]
        for c in range(grads.shape[0]):
            joined[c * chunk : (c + 1) * chunk, :] = grads[c, :chunk, :]

    first = 0
    for shard in shards:
        n = shard.shape[0]
        at = pl.ds(pl.multiple_of(first + i * n, 16), n)
        shard[...] = joined[at, :].astype(F32) * share
        first += n * pl.num_programs(0)
    hc, width = w0.shape[0] // 3, w0.shape[1]
    others = w1.shape[0]
    gn = dot(jnp.concatenate([q0[...], k0[...], v0[...]], axis=0), w0[...], 0, 0)
    for n, d in enumerate((q1, k1, v1)):
        gn += dot(d[...], w1[:, n * hc : (n + 1) * hc, :].reshape(others * hc, width), 0, 0)
    xhat, r = normalise(x[...].astype(F32))
    e = gn * gain[...]
    inner = r * (e - jnp.mean(e, axis=-1, keepdims=True) - xhat * jnp.mean(e * xhat, axis=-1, keepdims=True))
    out[...] = (gm[...].astype(F32) + inner).astype(BF16)


def finish(share, tokens, gm, own, rest, w0, w1, gain, grads, sizes):
    slots, width = tokens.shape
    steps = slots // LAST
    hc = own[0].shape[0]
    hr = rest[0].shape[0]
    return pl.pallas_call(
        functools.partial(finish_kernel, share),
        grid=(slots // LAST,),
        in_specs=[rows(LAST, width), rows(LAST, width)]
        + [cols(hc, LAST)] * 3
        + [cols(hr, LAST)] * 3
        + [whole(*w0.shape), whole(*w1.shape), whole(1, width), whole(*grads.shape)],
        out_specs=[rows(LAST, width)] + [rows(n // steps, width) for n in sizes],
        out_shape=[pltpu.HBM((slots, width), BF16)]
        + [pltpu.HBM((n, width), F32) for n in sizes],
        scratch_shapes=[pltpu.VMEM((sum(sizes), width), BF16)],
        compiler_params=pltpu.CompilerParams(vmem_limit_bytes=VMEM),
        cost_estimate=COST,
        name="finish",
    )(tokens, gm, *own, *rest, w0, w1, gain, grads)


def last_kernel(share, late, *refs):
    *norms, gw, bias = refs[:-8]
    *sums, joined = refs[-8:]
    hc = bias.shape[1]
    packs, n = late.shape[0], late.shape[1]
    for c in range(packs):
        joined[c * n : (c + 1) * n, :] = late[c]
    for p in range(3):
        gw[p] = joined[p * hc : (p + 1) * hc, :].astype(F32).T * share
    tail = joined[3 * hc : 3 * hc + 16, :].astype(F32) * share
    bias[0:1, :] = tail[8:9, :hc]
    bias[1:2, :] = tail[8:9, hc : 2 * hc]
    for k in range(5):
        sums[k][...] = tail[k : k + 1]
    total = sum(norm[...] for norm in norms[1:]) + norms[0][...]
    for k in range(2):
        sums[5 + k][...] = total[k : k + 1] * share


def last(share, late, norms, hc):
    packs, n, width = late.shape
    vm = pl.BlockSpec(memory_space=pltpu.VMEM)
    return pl.pallas_call(
        functools.partial(last_kernel, share),
        in_specs=[vm] * (1 + len(norms)),
        out_specs=[vm] * 9,
        out_shape=[
            jax.ShapeDtypeStruct((3, width, hc), F32),
            jax.ShapeDtypeStruct((2, hc), F32),
        ]
        + [jax.ShapeDtypeStruct((1, width), F32)] * 7,
        scratch_shapes=[pltpu.VMEM((packs * n, width), BF16)],
        compiler_params=pltpu.CompilerParams(vmem_limit_bytes=8 << 20),
        name="last",
    )(late, *norms)


def around(v, axis, k):
    n = lax.axis_size(axis)
    return lax.ppermute(v, axis, [(t, (t - k) % n) for t in range(n)])


def swapped(v, bit):
    return lax.ppermute(v, "dp", [(d, d ^ bit) for d in range(lax.axis_size("dp"))])


def summed_chunk(v):
    packs = lax.axis_size("dp")
    parts = lax.all_to_all(v, "dp", 0, 0, tiled=True)
    return jnp.sum(parts.reshape(packs, -1, v.shape[1]).astype(F32), axis=0).astype(v.dtype)


def spread(v):
    return jnp.broadcast_to(v[None], (lax.axis_size("dp"), *v.shape))


def three_parts(v):
    high = lax.reduce_precision(v, 8, 7)
    mid = lax.reduce_precision(v - high, 8, 7)
    return jnp.stack([high, mid, v - high - mid]).astype(BF16)


def body(
    tokens, lengths, cotangent, qkv_weight, qv_bias, out_weight, out_bias, up_weight, up_bias,
    down_weight, down_bias, first_gain, first_shift, second_gain, second_shift,
):
    groups, packs = lax.axis_size("tensor"), lax.axis_size("dp")
    width, _, hc = qkv_weight.shape
    ffn = up_weight.shape[1]
    share = 1.0 / packs
    core, side = place_of()
    row = lambda v: v.reshape(1, -1)
    turns = range(1, groups)
    local_qkv = jnp.transpose(qkv_weight, (1, 0, 2))
    biases = jnp.concatenate([up_bias.reshape(-1, hc), qv_bias])
    count = biases.shape[0]
    extra = jnp.pad(three_parts(biases).reshape(3 * count, hc), ((0, count + 8), (0, 0)))
    quarter = lax.dynamic_slice_in_dim(local_qkv, (2 * core + side) * (width // 4), width // 4, 1)
    quarter = jnp.concatenate([quarter.reshape(-1, hc), extra])
    qkv_mine = [around(quarter, "tensor", k) for k in turns]
    qt0, kt0, vt0, kr0, vr0, qn0, kn0, nl, xh, codek, codet, meta, wqkv0, near, far = prep_own(
        tokens, lengths, local_qkv, extra, row(first_gain), row(first_shift), out_weight, up_weight, down_weight
    )
    nl, near, *qkv_mine = lax.optimization_barrier((nl, near, *qkv_mine))
    qkv_mine = jnp.stack(qkv_mine)
    qkv_beside = swapped(qkv_mine, 2)
    near = [around(near, "tensor", k) for k in turns]
    ot0, low0, lse0 = attend(2 * BLOCK, OWNQ, 1, meta, qt0, codet, kr0, codek, vt0, qn0, kn0)
    ot0, qkv_beside, qkv_mine, far, near[0], near[-1] = lax.optimization_barrier(
        (ot0, qkv_beside, qkv_mine, far, near[0], near[-1])
    )
    qkv_parts = [v for part in (qkv_mine, qkv_beside) for v in (part, swapped(part, 1))]
    far = [around(far, "tensor", k) for k in turns]
    qt1, kt1, vt1, kr1, vr1, qn1, kn1, wqkv1, ub = prep_others(nl, qkv_parts)
    kr1, *near = lax.optimization_barrier((kr1, *near))
    near = jnp.stack(near)
    beside = swapped(near, 2)
    ot1, low1, lse1 = attend(BLOCK, 2 * BLOCK, 3, meta, qt1, codet, kr1, codek, vt1, qn1, kn1)
    ot1, near, beside, *far = lax.optimization_barrier((ot1, near, beside, *far))
    pieces = [near, beside, jnp.stack(far)]
    pieces = [v for piece in pieces for v in (piece, swapped(piece, 1))]
    out, gm, dt0, dt1, delta0, delta1, grads, sums = feed(
        meta, tokens, cotangent, ot0, ot1, low0, low1, out_weight, up_weight, down_weight, pieces,
        row(out_bias), row(up_bias), ub, row(down_bias), row(second_gain), row(second_shift),
    )
    grads = summed_chunk(grads)
    late_rows = -(-(3 * hc + 16) // (16 * packs)) * 16 * packs
    *own, late, norm_sums = reverse(
        2 * BLOCK, 1, meta, kr0, vr0, kt0, qt0, dt0, codek, codet, lse0, delta0,
        own=(xh, wqkv0, sums, row(first_gain), row(first_shift)), late=late_rows,
    )
    norms = jnp.pad(norm_sums.astype(BF16), ((0, 14), (0, 0)))
    chunk = grads.shape[0]
    mixed = jnp.concatenate([spread(jnp.concatenate([grads, norms])), late.reshape(packs, -1, width)], axis=1)
    mixed, kr1 = lax.optimization_barrier((mixed, kr1))
    mixed = lax.all_to_all(mixed, "dp", 0, 0)
    rest = reverse(BLOCK, 2, meta, kr1, vr1, kt1, qt1, dt1, codek, codet, lse1, delta1)
    mixed, rest0 = lax.optimization_barrier((mixed, rest[0]))
    late = jnp.sum(mixed[:, chunk + 16 :].astype(F32), axis=0).astype(BF16)
    late = lax.all_to_all(spread(late), "dp", 0, 0)
    norms = jnp.sum(mixed[:, chunk : chunk + 8].astype(F32), axis=0)
    norms = [norms] + [around(norms, "tensor", k) for k in turns]
    grad_tokens, grad_out, grad_up, grad_down = finish(
        share, tokens, gm, own, [rest0, *rest[1:]], wqkv0, wqkv1, row(first_gain),
        mixed, (hc, width, ffn),
    )
    gw, gb, *vectors = last(share, late, norms, hc)
    sums = [v.reshape(-1) for v in vectors]
    norm_sums = sums[5:]
    return (
        out,
        grad_tokens,
        jnp.transpose(gw, (1, 0, 2)),
        gb,
        grad_out,
        sums[3],
        grad_up,
        sums[4],
        grad_down,
        sums[0],
        norm_sums[0],
        norm_sums[1],
        sums[1],
        sums[2],
    )


def solution(mesh):
    in_specs = (
        P("dp", None),
        P("dp", None),
        P("dp", None),
        P(None, None, "tensor"),
        P(None, "tensor"),
        P("tensor", None),
        P(),
        P(None, "tensor"),
        P("tensor"),
        P("tensor", None),
        P(),
        P(),
        P(),
        P(),
        P(),
    )
    out_specs = (
        P("dp", None),
        P("dp", None),
        P(None, None, "tensor"),
        P(None, "tensor"),
        P("tensor", None),
        P(),
        P(None, "tensor"),
        P("tensor"),
        P("tensor", None),
        P(),
        P(),
        P(),
        P(),
        P(),
    )
    return jax.shard_map(body, mesh=mesh, in_specs=in_specs, out_specs=out_specs, check_vma=False)
```
